32 devices in a mesh: section: 2 (over y), dp: 16 (over z, x, core).
Axes of the slice: x: 2, y: 2, z: 4, core: 2. Of those that a mesh axis runs over, the one named last changes fastest.
Arguments:
- tokens: bfloat16 [2, 16, 512, 768], P(None, 'dp'), may hold values from -6 to 6
- out_cotangent: bfloat16 [2, 16, 512, 768], P(None, 'dp'), may hold values from -0.011962891 to 0.011962891
- lengths: int32 [2, 16, 4], P(None, 'dp'), may hold values from 1 to 256, 512 in all within a row
- partner: int32 [2, 64], P(None, 'dp'), may hold values from 0 to 63, as said below
- group_ids: int32 [2, 64], replicated, may hold values from 0 to 1, as said below
- attn_in: float32 [2, 768, 2304], P('section', 'dp'), may hold values from -0.21875 to 0.21875
- attn_out: float32 [2, 768, 768], P('section', 'dp'), may hold values from -1.75 to 1.75
- ff_in: float32 [2, 768, 3072], P('section', 'dp'), may hold values from -0.21875 to 0.21875
- ff_out: float32 [2, 3072, 768], P('section', 'dp'), may hold values from -0.109375 to 0.109375
- norm_gains: float32 [2, 2, 768], P('section', None, 'dp'), may hold values from 0.5 to 1.5
- biases: float32 [2, 6, 768], P('section', None, 'dp'), may hold values from -1 to 1
- ff_bias: float32 [2, 3072], P('section', 'dp'), may hold values from -1 to 1
Outputs:
- contrast_loss: float32 [], replicated
- hidden_states: bfloat16 [2, 2, 16, 512, 768], P('section', None, 'dp')
- hidden_grads: float32 [2, 2, 16, 512, 768], P('section', None, 'dp')
- attn_in_grad: float32 [2, 768, 2304], P('section', 'dp')
- attn_out_grad: float32 [2, 768, 768], P('section', 'dp')
- ff_in_grad: float32 [2, 768, 3072], P('section', 'dp')
- ff_out_grad: float32 [2, 3072, 768], P('section', 'dp')
- gains_grad: float32 [2, 2, 768], P('section', None, 'dp')
- biases_grad: float32 [2, 6, 768], P('section', None, 'dp')
- ff_bias_grad: float32 [2, 3072], P('section', 'dp')
The draws below stay inside these ranges and needn't reach their ends.
Inputs may be any that keep to these rules, and one draw needn't show every extreme that they name: Each row's 4 lengths sum to 512; in every row the longest is 256. In each micro-batch the sentences form twin pairs: partner[m, partner[m, i]] = i and partner[m, i] != i; twins share a group; sentences 0 and 32 are twins. `group_ids`: in each micro-batch every group holds exactly 32 sentences.
All inputs are finite; a program needn't handle non-finite values.
Results may differ from the reference program's by a relative error of at most 0.015.
Values may be sent and summed in bfloat16 or wider, within the bound.
No kernel may reach another device: no remote copies, remote signals or barrier semaphores. Data moves between devices by JAX's collectives and lax.ppermute only.
A program may use at most 320 MiB of HBM per device.

```python
import math
import jax
import jax.numpy as jnp
import numpy as np
from jax import lax

D = 768
HEADS = 12
FF = 3072
HEAD = 64
SEQ = 512
SEGS = 4
MICRO = 2
GROUP = 32
ROWS_ALL = 16
ALLSEG = 64
N_SECTION = 2


def pairing(key):
    partner_list = []
    group_list = []
    for micro in range(MICRO):
        micro_key = jax.random.fold_in(key, micro)
        order = jax.random.permutation(micro_key, ALLSEG).astype(jnp.int32)
        ranks = jnp.argsort(order, stable=True).astype(jnp.int32)
        ranks = ranks.at[0].set(-2).at[ALLSEG // 2].set(-1)
        order = jnp.argsort(ranks, stable=True).astype(jnp.int32)
        places = jnp.argsort(order, stable=True).astype(jnp.int32)
        partner_list.append(order[jnp.bitwise_xor(places, 1)])
        group_list.append(places // GROUP)
    return (jnp.stack(partner_list).astype(jnp.int32), jnp.stack(group_list).astype(jnp.int32))


def draw_partner(key, part):
    return pairing(key)[0]


def draw_group_ids(key, part):
    return pairing(key)[1]


def shard_levels(stream_key, dims, split, low, high):
    def one(axis_at, shards_of):
        draws = jax.random.uniform(jax.random.fold_in(jax.random.fold_in(stream_key, 6), axis_at), (shards_of,), jnp.float32, low / len(split), high / len(split))
        return jnp.repeat(jnp.exp(draws), dims[axis_at] // shards_of).reshape((-1,) + (1,) * (len(dims) - axis_at - 1))

    loudness = one(*split[0])
    for cut in split[1:]:
        loudness = loudness * one(*cut)
    return loudness


def split_up(number_of, total, bound, skew):
    weights = [(1 << 20) // math.isqrt(grade ** skew) + 1 for grade in range(2, number_of + 1)]
    surplus, holding = total - bound - (number_of - 1), [1] * (number_of - 1)
    while surplus > 0:
        free = [i for i in range(number_of - 1) if holding[i] < bound]
        pool, budget = sum([weights[i] for i in free]), surplus
        for i in free:
            addition = min(bound - holding[i], max(1, budget * weights[i] // pool), surplus)
            holding[i] = holding[i] + addition
            surplus = surplus - addition
    return np.array([bound] + holding)


def ragged_sizes(rng, amount, total, reach, lean):
    if amount == 2:
        one = jax.random.randint(rng, (), max(1, total - reach), min(reach, total - 1) + 1)
        return jnp.stack([one, total - one])
    sizes = jnp.asarray(split_up(amount, total, reach, lean), jnp.int32)
    twos = (amount - 1) // 2
    giver, taker = sizes[1:1 + 2 * twos:2], sizes[2:2 + 2 * twos:2]
    margin = jnp.minimum(giver - 1, reach - taker)
    shifted = jax.random.randint(jax.random.fold_in(rng, 1), (twos,), 0, 1 << 20) % (margin + 1)
    sizes = sizes.at[1:1 + 2 * twos:2].set(giver - shifted).at[2:2 + 2 * twos:2].set(taker + shifted)
    return sizes[jax.random.permutation(jax.random.fold_in(rng, 2), amount)]


def scatter_about(key, extent, scale, bound, cuts=(), kind=jnp.bfloat16):
    array = jax.random.normal(key, extent, jnp.float32) * scale
    if len(cuts) > 0:
        array = shard_levels(key, extent, cuts, -0.22, 0.18) * array
    return jnp.clip(array, min=-bound, max=bound).astype(kind)


def setup_inputs(seed: int = 0) -> dict:
    arg_keys = jax.random.split(jax.random.key(seed), 13)
    return {
        "tokens": scatter_about(arg_keys[0], (MICRO, ROWS_ALL, SEQ, D), 1.0, 6.0, ((1, 16),)),
        "out_cotangent": scatter_about(arg_keys[1], (MICRO, ROWS_ALL, SEQ, D), 0.002, 0.011962891, ((1, 16),)),
        "lengths": jax.vmap(lambda own: ragged_sizes(own, SEGS, SEQ, SEQ // 2, 1))(jax.random.split(arg_keys[2], MICRO * ROWS_ALL)).reshape((MICRO, ROWS_ALL, SEGS)).astype(jnp.int32),
        "partner": draw_partner(jax.random.fold_in(arg_keys[12], 71), 0),
        "group_ids": draw_group_ids(jax.random.fold_in(arg_keys[12], 71), 0),
        "attn_in": scatter_about(arg_keys[5], (N_SECTION, D, 3 * D), D ** -0.5, 0.21875, ((0, 2), (1, 16)), jnp.float32),
        "attn_out": scatter_about(arg_keys[6], (N_SECTION, D, D), (D // 64) ** -0.5, 1.75, ((0, 2), (1, 16)), jnp.float32),
        "ff_in": scatter_about(arg_keys[7], (N_SECTION, D, FF), D ** -0.5, 0.21875, ((0, 2), (1, 16)), jnp.float32),
        "ff_out": scatter_about(arg_keys[8], (N_SECTION, FF, D), FF ** -0.5, 0.109375, ((0, 2), (1, 16)), jnp.float32),
        "norm_gains": jnp.clip(1.0 + 0.1 * jax.random.normal(arg_keys[9], (N_SECTION, 2, D), jnp.float32), 0.5, 1.5),
        "biases": scatter_about(arg_keys[10], (N_SECTION, 6, D), 0.2, 1.0, ((0, 2), (2, 16)), jnp.float32),
        "ff_bias": scatter_about(arg_keys[11], (N_SECTION, FF), 0.2, 1.0, ((0, 2), (1, 16)), jnp.float32),
    }


@jax.custom_vjp
def low(v):
    return lax.optimization_barrier(v.astype(jnp.bfloat16)).astype(jnp.float32)

@jax.custom_vjp
def low_back(v):
    return v

def low_keep(v):
    return (low(v), None)

def low_pass(kept, grad):
    return (grad,)

def back_keep(v):
    return (v, None)

def back_low(kept, grad):
    return (low(grad),)
low.defvjp(low_keep, low_pass)
low_back.defvjp(back_keep, back_low)
highest = lax.Precision.HIGHEST
norm_eps = 1e-05
unit_eps = 1e-06
masked_value = -1000000000.0
contrast_scale = 10.0

def norm_rows(value, gain_row, shift_row):
    row_mean = lax.optimization_barrier(jnp.mean(value, axis=-1, keepdims=True))
    centered = value - row_mean
    variance = lax.optimization_barrier(jnp.mean(centered * centered, axis=-1, keepdims=True))
    return centered * lax.rsqrt(variance + norm_eps) * gain_row + shift_row

def segment_row(lengths):
    row_ends = jnp.cumsum(lengths, dtype=jnp.int32).astype(jnp.int32)
    places = jnp.arange(SEQ, dtype=jnp.int32)
    return lax.optimization_barrier(jnp.sum((places[:, None] >= row_ends[None, :]).astype(jnp.int32), axis=1))

def pool_unit(final, lengths):
    row_ends = jnp.cumsum(lengths, dtype=jnp.int32).astype(jnp.int32)
    row_starts = row_ends - lengths
    places = jnp.arange(SEQ, dtype=jnp.int32)
    member = ((places[None, :] >= row_starts[:, None]) & (places[None, :] < row_ends[:, None])).astype(jnp.float32)
    pooled = jnp.dot(member, final, precision=highest) / lengths[:, None].astype(jnp.float32)
    return pooled * lax.rsqrt(lax.optimization_barrier(jnp.sum(pooled * pooled, axis=-1, keepdims=True)) + unit_eps)

def block(inputs, segment, weights):
    attn_in, attn_out, ff_in, ff_out, norm_gains, biases, ff_bias = weights
    zero_part = jnp.zeros((D,), jnp.float32)
    qkv_bias = jnp.concatenate([biases[0], zero_part, biases[1]])
    qkv_rows = low_back(low(jnp.dot(low(inputs), attn_in, precision=highest) + qkv_bias))
    split_rows = qkv_rows.reshape(SEQ, 3, HEADS, HEAD)
    scores = jnp.einsum('qhd,khd->hqk', split_rows[:, 0], split_rows[:, 1], precision=highest)
    scores = low_back(scores * HEAD ** (-0.5))
    same = segment[:, None] == segment[None, :]
    scores = jnp.where(same[None], scores, masked_value)
    row_top = lax.optimization_barrier(jnp.max(scores, axis=-1, keepdims=True))
    raw = jnp.exp(scores - row_top)
    probs = raw / lax.optimization_barrier(jnp.sum(raw, axis=-1, keepdims=True))
    mixture = jnp.einsum('hqk,khd->qhd', low(probs), split_rows[:, 2], precision=highest)
    mixture = low_back(low(mixture.reshape(SEQ, D)))
    attended = low_back(jnp.dot(mixture, attn_out, precision=highest) + biases[2])
    hidden = inputs + attended
    normed = norm_rows(hidden, norm_gains[0], biases[3])
    pre_act = low_back(jnp.dot(low(normed), ff_in, precision=highest) + ff_bias)
    gelu_out = low(jax.nn.gelu(pre_act, approximate=False))
    branch = low_back(jnp.dot(gelu_out, ff_out, precision=highest) + biases[4])
    return norm_rows(normed + branch, norm_gains[1], biases[5])

def contrast(unit, partner_row, group_row):
    logits = contrast_scale * jnp.dot(unit, unit.T, precision=highest)
    column_ids = jnp.arange(ALLSEG, dtype=jnp.int32)
    allowed = (group_row[:, None] == group_row[None, :]) & (column_ids[:, None] != column_ids[None, :])
    masked = jnp.where(allowed, logits, masked_value)
    row_top = lax.optimization_barrier(jnp.max(masked, axis=1, keepdims=True))
    log_total = row_top[:, 0] + jnp.log(lax.optimization_barrier(jnp.sum(jnp.exp(masked - row_top), axis=1)))
    chosen = (column_ids[None, :] == partner_row[:, None]).astype(jnp.float32)
    return jnp.sum(log_total - lax.optimization_barrier(jnp.sum(chosen * logits, axis=1)))

def forward(tokens32, offsets, masters, lengths, partner, group_ids):
    lowered = [low(master) for master in masters]
    first_layer = tuple((master[0] for master in lowered))
    second_layer = tuple((master[1] for master in lowered))
    rows_in = tokens32.reshape(MICRO * ROWS_ALL, SEQ, D)
    rows_len = lengths.reshape(MICRO * ROWS_ALL, SEGS)
    rows_offset = offsets.reshape(MICRO * ROWS_ALL, SEQ, D)

    def one_row(packed):
        inputs, row_len, offset = packed
        segment = segment_row(row_len)
        middle = low(block(inputs, segment, first_layer))
        final = block(low_back(middle) + offset, segment, second_layer)
        return (middle, final, pool_unit(final, row_len))
    middle, final, unit = lax.map(jax.checkpoint(one_row), (rows_in, rows_len, rows_offset))
    unit = unit.reshape(MICRO, ALLSEG, D)
    total = jnp.zeros((), jnp.float32)
    for micro in range(MICRO):
        total = total + contrast(unit[micro], partner[micro], group_ids[micro])
    loss_value = total / (MICRO * ALLSEG)
    return (loss_value, middle.reshape(tokens32.shape), final.reshape(tokens32.shape))

def reference(tokens, out_cotangent, lengths, partner, group_ids, attn_in, attn_out, ff_in, ff_out, norm_gains, biases, ff_bias):
    tokens32 = tokens.astype(jnp.float32)
    cotangent = out_cotangent.astype(jnp.float32)
    masters = (attn_in, attn_out, ff_in, ff_out, norm_gains, biases, ff_bias)
    offsets = jnp.zeros_like(tokens32)

    def objective(inputs, offset_in, weights):
        return forward(inputs, offset_in, weights, lengths, partner, group_ids)
    (loss_value, middle, final), pull = jax.vjp(objective, tokens32, offsets, masters)
    loss_weight = jnp.full_like(loss_value, float(MICRO * ALLSEG))
    grad_tokens, grad_middle, grad_masters = pull((loss_weight, jnp.zeros_like(middle), cotangent))
    hidden_states = jnp.stack([middle, final]).astype(jnp.bfloat16)
    hidden_grads = jnp.stack([grad_tokens, grad_middle])
    return (loss_value, hidden_states, hidden_grads, grad_masters[0], grad_masters[1], grad_masters[2], grad_masters[3], grad_masters[4], grad_masters[5], grad_masters[6])
```

```python
from functools import partial

import jax
import jax.numpy as jnp
from jax import lax
from jax.experimental import pallas as pl
from jax.experimental.pallas import tpu as pltpu
from jax.sharding import PartitionSpec as P

D = 768
HEADS = 12
HEAD = 64
SEQ = 512
MICRO = 2
FF = 3072

bf16 = jnp.bfloat16
f32 = jnp.float32
highest = lax.Precision.HIGHEST
norm_eps = 1e-05
unit_eps = 1e-06
masked_value = -1000000000.0
contrast_scale = 10.0
vmem_limit = 56 * 2**20


def swapped(value, axis, mask):
    count = lax.axis_size(axis)
    return lax.ppermute(value, axis, [(i, i ^ mask) for i in range(count)])


def ring_order(chips):
    return list(range(0, chips, 2)) + list(range(chips - 1, 0, -2))


def ring_hop(value, backward=False):
    chips = lax.axis_size("dp") // 2
    order = ring_order(chips)
    pairs = []
    for place in range(chips):
        for core in range(2):
            step = 1 if core == 0 else -1
            pairs.append((order[place] * 2 + core, order[(place + step) % chips] * 2 + core))
    return lax.ppermute(value, "dp", pairs)


def ring_place():
    me = lax.axis_index("dp").astype(jnp.int32)
    chips = lax.axis_size("dp") // 2
    order = ring_order(chips)
    places = [order.index(chip) for chip in range(chips)]
    place = jnp.asarray(places, jnp.int32)[me // 2]
    core = me % 2
    return place, 1 - 2 * core, core


def owners(steps, cores):
    chips = lax.axis_size("dp") // 2
    place, way, core = ring_place()
    order = jnp.asarray(ring_order(chips), jnp.int32)
    found = order[(place + way * jnp.asarray(steps, jnp.int32)) % chips] * 2
    return found + (core + jnp.asarray(cores, jnp.int32)) % 2


def fast_ring():
    return lax.axis_size("dp") == 16


def gather_pieces(shard):
    mate = swapped(shard, "dp", 1)
    first = jnp.stack([shard, mate])
    one = ring_hop(first)
    one_mate = swapped(one, "dp", 1)
    two = ring_hop(one)
    two_mate = swapped(two, "dp", 1)
    three = ring_hop(two)
    three_mate = swapped(three, "dp", 1)
    four = ring_hop(three[:1])
    four_mate = swapped(four, "dp", 1)
    return [first, one, two, three, four, one_mate, two_mate, three_mate, four_mate]


def gather_owners():
    steps = [0, 0, -1, -1, -2, -2, -3, -3, -4, 1, 1, 2, 2, 3, 3, 4]
    cores = [0, 1, 0, 1, 0, 1, 0, 1, 0, 1, 0, 1, 0, 1, 0, 1]
    return owners(steps, cores)


def assemble_kernel(blocks, counts, owner_ref, *refs):
    pieces, outs, sems = refs[: len(counts)], refs[len(counts) : -1], refs[-1]
    copies = []
    at = 0
    for piece, count in zip(pieces, counts):
        for k in range(count):
            owner = owner_ref[at]
            row = 0
            for which, (out, (rows, columns)) in enumerate(zip(outs, blocks)):
                for block in range(columns):
                    start = pl.multiple_of(owner * rows, 16)
                    copies.append(
                        pltpu.make_async_copy(
                            piece.at[k, pl.ds(row, rows)],
                            out.at[pl.ds(start, rows), pl.ds(block * D, D)],
                            sems.at[len(copies)],
                        )
                    )
                    row += rows
            at += 1
    for copy in copies:
        copy.start()
    for copy in copies:
        copy.wait()


def assemble(pieces, blocks, owner):
    counts = [piece.shape[0] for piece in pieces]
    total = sum(counts)
    return pl.pallas_call(
        partial(assemble_kernel, blocks, counts),
        out_shape=[jax.ShapeDtypeStruct((total * rows, columns * D), bf16) for rows, columns in blocks],
        in_specs=[pl.BlockSpec(memory_space=pltpu.SMEM)]
        + [pl.BlockSpec(memory_space=pl.ANY)] * len(pieces),
        out_specs=[pl.BlockSpec(memory_space=pltpu.VMEM)] * len(blocks),
        scratch_shapes=[pltpu.SemaphoreType.DMA((total * sum(c for _, c in blocks),))],
        compiler_params=pltpu.CompilerParams(vmem_limit_bytes=vmem_limit),
        name="assemble",
    )(owner, *pieces)


def deal_kernel(blocks, keep_ref, send_ref, *refs):
    ins, (keep_out, send_out, sems) = refs[: len(blocks)], refs[len(blocks) :]
    copies = []
    for table, out in ((keep_ref, keep_out), (send_ref, send_out)):
        for unit in range(8):
            owner = table[unit]
            row = 0
            for ref, (rows, columns) in zip(ins, blocks):
                for block in range(columns):
                    start = pl.multiple_of(owner * rows, 16)
                    copies.append(
                        pltpu.make_async_copy(
                            ref.at[pl.ds(start, rows), pl.ds(block * D, D)],
                            out.at[unit, pl.ds(row, rows)],
                            sems.at[len(copies)],
                        )
                    )
                    row += rows
    for copy in copies:
        copy.start()
    for copy in copies:
        copy.wait()


def deal(grads, blocks, keep, send):
    height = sum(rows * columns for rows, columns in blocks)
    return pl.pallas_call(
        partial(deal_kernel, blocks),
        out_shape=[jax.ShapeDtypeStruct((8, height, D), bf16)] * 2,
        in_specs=[pl.BlockSpec(memory_space=pltpu.SMEM)] * 2
        + [pl.BlockSpec(memory_space=pltpu.VMEM)] * len(grads),
        out_specs=[pl.BlockSpec(memory_space=pl.ANY)] * 2,
        scratch_shapes=[pltpu.SemaphoreType.DMA((16 * sum(c for _, c in blocks),))],
        compiler_params=pltpu.CompilerParams(vmem_limit_bytes=vmem_limit),
        name="deal",
    )(keep, send, *grads)


unit_steps = [1, 1, 2, 2, 3, 3, 4, 0]


def deal_tables():
    core = ring_place()[2]
    cores_keep = [0, 1, 0, 1, 0, 1]
    keep = owners(unit_steps, [0] * 8)
    send = owners([-step for step in unit_steps], [1] * 8)
    absolute = jnp.asarray(cores_keep, jnp.int32)
    keep = jnp.concatenate([keep[:6] // 2 * 2 + absolute, keep[6:]])
    send = jnp.concatenate([send[:6] // 2 * 2 + absolute, send[6:]])
    return keep, send, core


def reduce_units(keep, send, core):
    mine = keep.astype(f32) + swapped(send, "dp", 1).astype(f32)
    total = ring_hop(mine[6:7].astype(bf16))
    third = mine[4:6] + jnp.where(
        jnp.arange(2)[:, None, None] == core, total.astype(f32), jnp.zeros((), f32)
    )
    total = ring_hop(third.astype(bf16))
    total = ring_hop((mine[2:4] + total.astype(f32)).astype(bf16))
    total = ring_hop((mine[0:2] + total.astype(f32)).astype(bf16))
    own = lax.dynamic_index_in_dim(total, core, 0, keepdims=False)
    other = swapped(lax.dynamic_index_in_dim(total, 1 - core, 0, keepdims=False), "dp", 1)
    return mine[7] + own.astype(f32) + other.astype(f32)


def gather_small(value):
    me = lax.axis_index("dp")
    value = value[None]
    mask = 1
    while mask < lax.axis_size("dp"):
        other = swapped(value, "dp", mask)
        upper = (me & mask) != 0
        value = jnp.concatenate([jnp.where(upper, other, value), jnp.where(upper, value, other)])
        mask *= 2
    return value


def reduce_small(value):
    me = lax.axis_index("dp")
    mask = lax.axis_size("dp") // 2
    while mask >= 1:
        half = value.shape[0] // 2
        upper = (me & mask) != 0
        keep = jnp.where(upper, value[half:], value[:half])
        send = jnp.where(upper, value[:half], value[half:])
        value = keep + swapped(send, "dp", mask)
        mask //= 2
    return value[0]


def norm_rows(value, gain_row, shift_row):
    row_mean = jnp.mean(value, axis=-1, keepdims=True)
    centered = value - row_mean
    variance = jnp.mean(centered * centered, axis=-1, keepdims=True)
    return centered * lax.rsqrt(variance + norm_eps) * gain_row + shift_row


def pool_unit(final_rows, lengths):
    row_ends = jnp.cumsum(lengths, axis=-1, dtype=jnp.int32)
    row_starts = row_ends - lengths
    places = jnp.arange(SEQ, dtype=jnp.int32)
    member = ((places[None, :] >= row_starts[:, None]) & (places[None, :] < row_ends[:, None])).astype(f32)
    pooled = jnp.dot(member, final_rows, precision=highest) / lengths[:, None].astype(f32)
    return pooled * lax.rsqrt(jnp.sum(pooled * pooled, axis=-1, keepdims=True) + unit_eps)


def attend(query_rows, key_rows, value_rows, segment):
    scores = jnp.einsum(
        "qhd,khd->hqk", query_rows, key_rows, preferred_element_type=f32
    ) * HEAD ** (-0.5)
    same = segment[:, None] == segment[None, :]
    scores = jnp.where(same[None], scores, masked_value)
    row_top = jnp.max(scores, axis=-1, keepdims=True)
    raw = jnp.exp(scores - row_top)
    row_total = jnp.sum(raw, axis=-1, keepdims=True)
    probs = raw / row_total
    mixture = jnp.einsum(
        "hqk,khd->qhd", probs.astype(bf16), value_rows, preferred_element_type=f32
    )
    return (mixture, row_top + jnp.log(row_total))


def attend_back(query_rows, key_rows, value_rows, segment, log_total, grad_mixture):
    scores = jnp.einsum(
        "qhd,khd->hqk", query_rows, key_rows, preferred_element_type=f32
    ) * HEAD ** (-0.5)
    same = segment[:, None] == segment[None, :]
    scores = jnp.where(same[None], scores, masked_value)
    probs = jnp.exp(scores - log_total)
    grad_value = jnp.einsum(
        "hqk,qhd->khd", probs.astype(bf16), grad_mixture, preferred_element_type=f32
    )
    grad_probs = jnp.einsum("qhd,khd->hqk", grad_mixture, value_rows, preferred_element_type=f32)
    row_dot = jnp.sum(grad_probs * probs, axis=-1, keepdims=True)
    grad_scores = (probs * (grad_probs - row_dot)).astype(bf16)
    grad_query = jnp.einsum(
        "hqk,khd->qhd", grad_scores, key_rows, preferred_element_type=f32
    ) * HEAD ** (-0.5)
    grad_key = jnp.einsum(
        "hqk,qhd->khd", grad_scores, query_rows, preferred_element_type=f32
    ) * HEAD ** (-0.5)
    return (grad_query, grad_key, grad_value)


def layer_forward(rows, segment, weights, vectors):
    attn_in, attn_out, ff_in, ff_out = weights
    gains, biases, ff_bias = vectors
    zero_part = jnp.zeros((D,), f32)
    qkv_bias = jnp.concatenate([biases[0], zero_part, biases[1]])
    qkv = (jnp.dot(rows, attn_in, preferred_element_type=f32) + qkv_bias).astype(bf16)
    parts = qkv.reshape(SEQ, 3, HEADS, HEAD)
    mixture, log_total = attend(parts[:, 0], parts[:, 1], parts[:, 2], segment)
    mixture = mixture.reshape(SEQ, D).astype(bf16)
    attended = jnp.dot(mixture, attn_out, preferred_element_type=f32) + biases[2]
    hidden = rows.astype(f32) + attended
    normed = norm_rows(hidden, gains[0], biases[3])
    pre_act = jnp.dot(normed.astype(bf16), ff_in, preferred_element_type=f32) + ff_bias
    gelu_out = jax.nn.gelu(pre_act, approximate=False).astype(bf16)
    branch = jnp.dot(gelu_out, ff_out, preferred_element_type=f32) + biases[4]
    output = norm_rows(normed + branch, gains[1], biases[5])
    return (output, (parts, log_total, mixture, hidden, normed, pre_act, branch))


def layer_backward(rows, segment, weights, vectors, stored, grad_out):
    attn_in, attn_out, ff_in, ff_out = weights
    gains, biases, ff_bias = vectors
    parts, log_total, mixture, hidden, normed, pre_act, branch = stored
    _, out_pull = jax.vjp(norm_rows, normed + branch, gains[1], biases[5])
    grad_sum, grad_gain_out, grad_shift_out = out_pull(grad_out)
    grad_branch = grad_sum.astype(bf16)
    gelu_value, gelu_pull = jax.vjp(partial(jax.nn.gelu, approximate=False), pre_act)
    grad_ff_out = jnp.einsum(
        "tf,td->fd", gelu_value.astype(bf16), grad_branch, preferred_element_type=f32
    ).astype(bf16)
    grad_bias_out = jnp.sum(grad_branch, axis=0, dtype=f32)
    grad_gelu = jnp.einsum("td,fd->tf", grad_branch, ff_out, preferred_element_type=f32)
    grad_pre = gelu_pull(grad_gelu)[0].astype(bf16)
    grad_ff_in = jnp.einsum(
        "td,tf->df", normed.astype(bf16), grad_pre, preferred_element_type=f32
    ).astype(bf16)
    grad_ff_bias = jnp.sum(grad_pre, axis=0, dtype=f32)
    grad_normed = grad_sum + jnp.einsum("tf,df->td", grad_pre, ff_in, preferred_element_type=f32)
    _, in_pull = jax.vjp(norm_rows, hidden, gains[0], biases[3])
    grad_hidden, grad_gain_in, grad_shift_in = in_pull(grad_normed)
    grad_attended = grad_hidden.astype(bf16)
    grad_attn_out = jnp.einsum(
        "ti,to->io", mixture, grad_attended, preferred_element_type=f32
    ).astype(bf16)
    grad_bias_attn = jnp.sum(grad_attended, axis=0, dtype=f32)
    grad_mixture = jnp.einsum("to,io->ti", grad_attended, attn_out, preferred_element_type=f32)
    grad_mixture = grad_mixture.astype(bf16).reshape(SEQ, HEADS, HEAD)
    grad_query, grad_key, grad_value = attend_back(
        parts[:, 0], parts[:, 1], parts[:, 2], segment, log_total, grad_mixture
    )
    grad_qkv = (
        jnp.stack([grad_query, grad_key, grad_value], axis=1).reshape(SEQ, 3 * D).astype(bf16)
    )
    grad_attn_in = jnp.einsum("ti,tj->ij", rows, grad_qkv, preferred_element_type=f32).astype(bf16)
    grad_bias_qkv = jnp.sum(grad_qkv, axis=0, dtype=f32)
    grad_inputs = grad_hidden + jnp.einsum("tj,ij->ti", grad_qkv, attn_in, preferred_element_type=f32)
    small = jnp.stack(
        [
            grad_gain_in,
            grad_gain_out,
            grad_bias_qkv[:D],
            grad_bias_qkv[2 * D :],
            grad_bias_attn,
            grad_shift_in,
            grad_bias_out,
            grad_shift_out,
        ]
    )
    return grad_inputs, (grad_attn_in, grad_attn_out, grad_ff_in, grad_ff_out), (small, grad_ff_bias)


def contrast(final_rows, lengths, partner_all, group_row):
    unit_own, unit_pull = jax.vjp(lambda value: pool_unit(value, lengths), final_rows)
    table = gather_small(unit_own).reshape(-1, D)
    count = table.shape[0]
    offset = lax.axis_index("dp") * unit_own.shape[0]
    ids = jnp.arange(count, dtype=jnp.int32)
    chosen = (ids[None, :] == partner_all[:, None]).astype(f32)
    logits = contrast_scale * jnp.dot(table, table.T, precision=highest)
    allowed = (group_row[:, None] == group_row[None, :]) & (ids[:, None] != ids[None, :])
    masked = jnp.where(allowed, logits, masked_value)
    row_top = jnp.max(masked, axis=1, keepdims=True)
    raw = jnp.exp(masked - row_top)
    row_total = jnp.sum(raw, axis=1, keepdims=True)
    loss = jnp.sum(row_top[:, 0] + jnp.log(row_total[:, 0]) - jnp.sum(chosen * logits, axis=1))
    grad_logits = raw / row_total - chosen
    both = lax.dynamic_slice_in_dim(grad_logits + grad_logits.T, offset, unit_own.shape[0])
    grad_unit = contrast_scale * jnp.dot(both, table, precision=highest)
    return loss / (MICRO * count), unit_pull(grad_unit)[0]


def blocked(shard):
    rows, columns = shard.shape
    return shard.reshape(rows, columns // D, D).transpose(1, 0, 2).reshape(-1, D)


def unblocked(shard, columns):
    return shard.reshape(columns, -1, D).transpose(1, 0, 2).reshape(-1, columns * D)


def local(
    tokens,
    out_cotangent,
    lengths,
    partner,
    group_ids,
    attn_in,
    attn_out,
    ff_in,
    ff_out,
    norm_gains,
    biases,
    ff_bias,
):
    section = lax.axis_index("section")
    leading = section == 0
    n_dp = lax.axis_size("dp")
    rows_in = D // n_dp
    rows_out = FF // n_dp

    def pick(stack):
        return lax.dynamic_index_in_dim(stack, section, 0, keepdims=False)

    small = jnp.concatenate(
        [norm_gains[0].reshape(-1), biases[0].reshape(-1), ff_bias[0].reshape(-1)]
    )
    small = small.astype(bf16).astype(f32)
    small_other = swapped(small, "section", 1)
    small = jnp.concatenate([small, small_other, partner.astype(f32).reshape(-1)])
    small = gather_small(small)
    width = 8 * rows_in + rows_out
    vectors = []
    for layer in range(2):
        mine = jnp.where(
            section == layer, small[:, :width], small[:, width : 2 * width]
        )
        both = mine[:, : 8 * rows_in].reshape(n_dp, 8, rows_in).transpose(1, 0, 2).reshape(8, D)
        vectors.append((both[:2], both[2:8], mine[:, 8 * rows_in :].reshape(FF)))
    partner_all = small[:, 2 * width :].reshape(n_dp, MICRO, -1)
    partner_mine = lax.dynamic_index_in_dim(partner_all, section, 1, keepdims=False)
    partner_mine = partner_mine.reshape(-1).astype(jnp.int32)

    chunk_blocks = [
        [(rows_in, 3)],
        [(rows_in, 1), (rows_in, 4)],
        [(rows_out, 1)],
    ]
    weights = [[], []]
    if fast_ring():
        packed = [
            blocked(attn_in[0].astype(bf16)),
            jnp.concatenate([attn_out[0].astype(bf16), blocked(ff_in[0].astype(bf16))]),
            ff_out[0].astype(bf16),
        ]
        crossed = [swapped(piece, "section", 1) for piece in packed]
        owner = gather_owners()
        for layer in range(2):
            for mine, other, blocks in zip(packed, crossed, chunk_blocks):
                shard = jnp.where(section == layer, mine, other)
                weights[layer] += assemble(gather_pieces(shard), blocks, owner)
    else:
        for shard in (attn_in, attn_out, ff_in, ff_out):
            whole = lax.all_gather(shard[0].astype(bf16), ("section", "dp"), axis=0, tiled=True)
            half = whole.shape[0] // 2
            weights[0].append(whole[:half])
            weights[1].append(whole[half:])

    my_tokens = pick(tokens)[0]
    my_cotangent = pick(out_cotangent)[0]
    my_lengths = pick(lengths)[0]
    my_groups = pick(group_ids)
    row_ends = jnp.cumsum(my_lengths, dtype=jnp.int32)
    places = jnp.arange(SEQ, dtype=jnp.int32)
    segment = jnp.sum((places[:, None] >= row_ends[None, :]).astype(jnp.int32), axis=-1)

    first_out, first_stored = layer_forward(my_tokens, segment, weights[0], vectors[0])
    middle = first_out.astype(bf16)
    final, second_stored = layer_forward(middle, segment, weights[1], vectors[1])
    final_low = final.astype(bf16)
    loss, grad_final = contrast(final, my_lengths, partner_mine, my_groups)
    contrast_loss = loss + swapped(loss, "section", 1)
    grad_final = grad_final + my_cotangent.astype(f32)

    grad_middle, second_grads, second_small = layer_backward(
        middle, segment, weights[1], vectors[1], second_stored, grad_final
    )
    grad_middle_low = grad_middle.astype(bf16)
    grad_tokens, first_grads, first_small = layer_backward(
        my_tokens, segment, weights[0], vectors[0], first_stored, grad_middle_low.astype(f32)
    )

    if fast_ring():
        keep_table, send_table, core = deal_tables()
        totals = []
        for grads in (second_grads, first_grads):
            grad_in, grad_out, grad_ff_in, grad_ff_out = grads
            chunks = []
            for group, blocks in (
                ([grad_ff_out], chunk_blocks[2]),
                ([grad_out, grad_ff_in], chunk_blocks[1]),
                ([grad_in], chunk_blocks[0]),
            ):
                keep, send = deal(group, blocks, keep_table, send_table)
                chunks.append(reduce_units(keep, send, core))
            totals.append(chunks)
        own = []
        for second, first in zip(*totals):
            send = jnp.where(leading, second, first).astype(bf16)
            keep = jnp.where(leading, first, second)
            own.append(keep + swapped(send, "section", 1).astype(f32))
        own_ff_out = own[0]
        own_attn_out, own_ff_in = own[1][:rows_in], unblocked(own[1][rows_in:], 4)
        own_attn_in = unblocked(own[2], 3)
    else:
        shares = []
        for first, second in zip(first_grads, second_grads):
            both = jnp.concatenate([first, second]).astype(f32)
            shares.append(lax.psum_scatter(both, ("section", "dp"), scatter_dimension=0, tiled=True))
        own_attn_in, own_attn_out, own_ff_in, own_ff_out = shares

    def flat(pair):
        rows, bias = pair
        rows = rows.reshape(8, n_dp, rows_in).transpose(1, 0, 2).reshape(n_dp, -1)
        return jnp.concatenate([rows, bias.reshape(n_dp, -1)], axis=1)

    first_flat, second_flat = flat(first_small), flat(second_small)
    keep = jnp.where(leading, first_flat, second_flat)
    send = jnp.where(leading, second_flat, first_flat)
    own_small = reduce_small(keep + swapped(send, "section", 1))
    own_rows = own_small[: 8 * rows_in].reshape(8, rows_in)
    own_bias = own_small[8 * rows_in :]

    state_other = swapped(jnp.where(leading, final_low, middle), "section", 1)
    state_mine = jnp.where(leading, middle, final_low)
    hidden_states = jnp.stack(
        [jnp.where(leading, state_mine, state_other), jnp.where(leading, state_other, state_mine)]
    )
    grad_other = swapped(
        jnp.where(leading, grad_middle_low, grad_tokens.astype(bf16)), "section", 1
    ).astype(f32)
    grad_mine = jnp.where(leading, grad_tokens, grad_middle)
    hidden_grads = jnp.stack(
        [jnp.where(leading, grad_mine, grad_other), jnp.where(leading, grad_other, grad_mine)]
    )
    return (
        contrast_loss,
        hidden_states[None, :, None],
        hidden_grads[None, :, None],
        own_attn_in[None],
        own_attn_out[None],
        own_ff_in[None],
        own_ff_out[None],
        own_rows[None, :2],
        own_rows[None, 2:],
        own_bias[None],
    )


def solution(mesh):
    return jax.shard_map(
        local,
        mesh=mesh,
        in_specs=(
            P(None, "dp", None, None),
            P(None, "dp", None, None),
            P(None, "dp", None),
            P(None, "dp"),
            P(),
            P("section", "dp", None),
            P("section", "dp", None),
            P("section", "dp", None),
            P("section", "dp", None),
            P("section", None, "dp"),
            P("section", None, "dp"),
            P("section", "dp"),
        ),
        out_specs=(
            P(),
            P("section", None, "dp", None, None),
            P("section", None, "dp", None, None),
            P("section", "dp", None),
            P("section", "dp", None),
            P("section", "dp", None),
            P("section", "dp", None),
            P("section", None, "dp"),
            P("section", None, "dp"),
            P("section", "dp"),
        ),
        check_vma=False,
    )
```

```python
from functools import partial

import jax
import jax.numpy as jnp
from jax import lax
from jax.experimental import pallas as pl
from jax.experimental.pallas import tpu as pltpu
from jax.sharding import PartitionSpec as P

D = 768
HEADS = 12
HEAD = 64
SEQ = 512
MICRO = 2
FF = 3072

bf16 = jnp.bfloat16
f32 = jnp.float32
highest = lax.Precision.HIGHEST
norm_eps = 1e-05
unit_eps = 1e-06
masked_value = -1000000000.0
contrast_scale = 10.0
vmem_limit = 20 * 2**20


def params():
    return pltpu.CompilerParams(vmem_limit_bytes=vmem_limit)


def cost(flops, size):
    return pl.CostEstimate(flops=int(10 * flops), bytes_accessed=int(10 * size), transcendentals=0)


def swapped(value, axis, mask):
    count = lax.axis_size(axis)
    return lax.ppermute(value, axis, [(i, i ^ mask) for i in range(count)])


def ring_order(chips):
    return list(range(0, chips, 2)) + list(range(chips - 1, 0, -2))


def ring_hop(value, backward=False):
    chips = lax.axis_size("dp") // 2
    order = ring_order(chips)
    pairs = []
    for place in range(chips):
        for core in range(2):
            step = 1 if core == 0 else -1
            pairs.append((order[place] * 2 + core, order[(place + step) % chips] * 2 + core))
    return lax.ppermute(value, "dp", pairs)


def ring_place():
    me = lax.axis_index("dp").astype(jnp.int32)
    chips = lax.axis_size("dp") // 2
    order = ring_order(chips)
    places = [order.index(chip) for chip in range(chips)]
    place = jnp.asarray(places, jnp.int32)[me // 2]
    core = me % 2
    return place, 1 - 2 * core, core


def owners(steps, cores):
    chips = lax.axis_size("dp") // 2
    place, way, core = ring_place()
    order = jnp.asarray(ring_order(chips), jnp.int32)
    found = order[(place + way * jnp.asarray(steps, jnp.int32)) % chips] * 2
    return found + (core + jnp.asarray(cores, jnp.int32)) % 2


def fast_ring():
    return lax.axis_size("dp") == 16


def gather_owners():
    steps = [0, 0, -1, -1, -2, -2, -3, -3, -4, 1, 1, 2, 2, 3, 3, 4]
    cores = [0, 1, 0, 1, 0, 1, 0, 1, 0, 1, 0, 1, 0, 1, 0, 1]
    return owners(steps, cores)


def assemble_kernel(counts, owner_ref, *refs):
    pieces, out_ref, sems = refs[: len(counts)], refs[-2], refs[-1]
    rows = pieces[0].shape[2]
    copies = []
    for piece, count in zip(pieces, counts):
        for k in range(count):
            start = pl.multiple_of(owner_ref[len(copies)] * rows, 16)
            copies.append(
                pltpu.make_async_copy(
                    piece.at[k], out_ref.at[:, pl.ds(start, rows), :], sems.at[len(copies)]
                )
            )
    for copy in copies:
        copy.start()
    for copy in copies:
        copy.wait()


def assemble(pieces, owner):
    counts = [piece.shape[0] for piece in pieces]
    total = sum(counts)
    blocks, rows = pieces[0].shape[1:3]
    return pl.pallas_call(
        partial(assemble_kernel, counts),
        out_shape=jax.ShapeDtypeStruct((blocks, total * rows, D), bf16),
        in_specs=[pl.BlockSpec(memory_space=pltpu.SMEM)]
        + [pl.BlockSpec(memory_space=pl.ANY)] * len(pieces),
        out_specs=pl.BlockSpec(memory_space=pltpu.VMEM),
        scratch_shapes=[pltpu.SemaphoreType.DMA((total,))],
        compiler_params=params(),
        cost_estimate=cost(0, 1e7),
        name="assemble",
    )(owner, *pieces)


unit_steps = [1, 1, 2, 2, 3, 3, 4, 0]


def slots():
    if not fast_ring():
        return jnp.arange(16, dtype=jnp.int32)
    core = ring_place()[2]
    both = jnp.arange(6, dtype=jnp.int32) % 2
    keep = owners(unit_steps, [0] * 8)
    send = owners([-step for step in unit_steps], [1] * 8)
    table = [keep[:6] // 2 * 2 + both, keep[6:], send[:6] // 2 * 2 + both, send[6:]]
    table = jnp.concatenate(table)
    index = jnp.arange(16, dtype=jnp.int32)
    return jnp.sum(jnp.where(table[None, :] == index[:, None], index[None, :], 0), axis=1)


def fold_kernel(one, core_ref, keep_ref, mate_ref, *refs):
    total = keep_ref[...].astype(f32) + mate_ref[...].astype(f32)
    if len(refs) > 1:
        there = refs[0][...].astype(f32)
        if one:
            there = jnp.where(pl.program_id(0) == core_ref[0], there, 0.0)
        total = total + there
    refs[-1][...] = total.astype(bf16)


def fold(core, keep, mate, first, there=None):
    rows, width = keep.shape[1:]
    count = 1 if there is None else 2
    one = there is not None and there.shape[0] == 1
    unit = pl.BlockSpec((1, rows, width), lambda i, _: (first + i, 0, 0))
    out = pl.BlockSpec((1, rows, width), lambda i, _: (i, 0, 0))
    arrived = pl.BlockSpec((1, rows, width), lambda i, _: (0, 0, 0)) if one else out
    return pl.pallas_call(
        partial(fold_kernel, one),
        grid_spec=pltpu.PrefetchScalarGridSpec(
            num_scalar_prefetch=1,
            grid=(count,),
            in_specs=[unit, unit] + ([] if there is None else [arrived]),
            out_specs=out,
        ),
        out_shape=jax.ShapeDtypeStruct((count, rows, width), bf16),
        compiler_params=params(),
        cost_estimate=cost(0, 0),
        name="fold",
    )(core, keep, mate, *([] if there is None else [there]))


def settle_kernel(place_ref, *refs):
    totals = []
    for layer in range(2):
        parts = refs[4 * layer : 4 * layer + 4]
        totals.append(sum(part[0].astype(f32) for part in parts))
    leading = place_ref[1] == 0
    keep_ref, send_ref = refs[8:]
    keep_ref[...] = jnp.where(leading, totals[0], totals[1])
    send_ref[...] = jnp.where(leading, totals[1], totals[0]).astype(bf16)


def settle(place, first, second):
    rows, width = first.keep.shape[1:]
    tile = rows // 3
    own = pl.BlockSpec((1, tile, width), lambda i, _: (7, i, 0))
    end = pl.BlockSpec((1, tile, width), lambda i, place: (place[0], i, 0))
    out = pl.BlockSpec((tile, width), lambda i, _: (i, 0))
    return pl.pallas_call(
        settle_kernel,
        grid_spec=pltpu.PrefetchScalarGridSpec(
            num_scalar_prefetch=1,
            grid=(3,),
            in_specs=[own, own, end, end] * 2,
            out_specs=[out, out],
        ),
        out_shape=[
            jax.ShapeDtypeStruct((rows, width), f32),
            jax.ShapeDtypeStruct((rows, width), bf16),
        ],
        compiler_params=params(),
        cost_estimate=cost(0, 0),
        name="settle",
    )(place, *first.parts(), *second.parts())


class Reduction:
    def __init__(self, core, keep, send):
        self.core, self.keep, self.send = core, keep, send
        self.moving = [swapped(send, "dp", 1)] if fast_ring() else []
        self.stage = 0

    def step(self):
        arrived = self.moving[0]
        if self.stage == 0:
            self.mate = arrived
            self.moving = [ring_hop(fold(self.core, self.keep, self.mate, 6))]
        elif self.stage < 4:
            first = 6 - 2 * self.stage
            self.moving = [ring_hop(fold(self.core, self.keep, self.mate, first, arrived))]
        elif self.stage == 4:
            self.near = arrived
            self.moving = [swapped(self.near, "dp", 1)]
        else:
            self.last = arrived
            self.moving = []
        self.stage += 1

    def parts(self):
        return self.keep, self.mate, self.near, self.last


class Settled:
    def __init__(self, place, first, second):
        self.keep, send = settle(place, first, second)
        self.moving = [swapped(send, "section", 1)]

    def step(self):
        self.value = self.keep + self.moving[0].astype(f32)
        self.moving = []


class Sent:
    def __init__(self, value, pairs):
        half = value.shape[0] // 2
        self.halves, self.pairs, self.arrived = [value[:half], value[half:]], pairs, []
        self.send()

    def send(self):
        half = self.halves[len(self.arrived)]
        self.moving = [lax.ppermute(half, "section", self.pairs)]

    def step(self):
        self.arrived += self.moving
        self.moving = []
        if len(self.arrived) < 2:
            self.send()

    def value(self):
        return jnp.concatenate(self.arrived)


class Sum:
    def __init__(self, value):
        self.value = value
        self.left = [("section", 1)]
        mask = 1
        while mask < lax.axis_size("dp"):
            self.left.append(("dp", mask))
            mask *= 2
        self.send()

    def send(self):
        self.moving = [swapped(self.value, *self.left[0])] if self.left else []

    def step(self):
        self.value = self.value + self.moving[0]
        self.left = self.left[1:]
        self.send()


class Gather:
    def __init__(self, shard):
        self.pieces, self.mates = [shard], []
        self.moving = [swapped(shard, "dp", 1)]
        self.stage = 0

    def step(self):
        if self.stage == 0:
            self.pieces = [jnp.stack([self.pieces[0], self.moving[0]])]
            self.moving = [ring_hop(self.pieces[0])]
        elif self.stage < 5:
            self.pieces.append(self.moving[0])
            self.mates += self.moving[1:]
            self.moving = [swapped(self.pieces[-1], "dp", 1)]
            if self.stage < 4:
                last = self.pieces[-1] if self.stage < 3 else self.pieces[-1][:1]
                self.moving = [ring_hop(last)] + self.moving
        else:
            self.mates += self.moving
            self.moving = []
        self.stage += 1

    def all(self):
        return self.pieces + self.mates


def onward(items, values=()):
    items = [item for item in items if item.moving]
    if items:
        values, moved = lax.optimization_barrier((values, [item.moving for item in items]))
        for item, moving in zip(items, moved):
            item.moving = moving
            item.step()
    return values


def tie(values, *others):
    return lax.optimization_barrier((values, others))[0]


def add_up(value, axis):
    mask = 1
    while mask < lax.axis_size(axis):
        value = value + swapped(value, axis, mask)
        mask *= 2
    return value


def gather_near(value):
    mask = lax.axis_size("dp") // 2
    while mask >= 1:
        value = jnp.concatenate([value, swapped(value, "dp", mask)])
        mask //= 2
    return value


def mm(a, b):
    return lax.dot_general(a, b, (((1,), (0,)), ((), ())), preferred_element_type=f32)


def mm_nt(a, b):
    return lax.dot_general(a, b, (((1,), (1,)), ((), ())), preferred_element_type=f32)


def mm_tn(a, b):
    return lax.dot_general(a, b, (((0,), (0,)), ((), ())), preferred_element_type=f32)


def full(shape):
    return pl.BlockSpec(shape, lambda i, *_: (0,) * len(shape))


def sds(shape, dtype):
    return jax.ShapeDtypeStruct(shape, dtype)


group = 256
groups = D // group
product = 2 * SEQ * D * D
token_block = (SEQ, D)
table_rows = 12
vec_spec = full((2 * table_rows, D))


def column_sum(value):
    return jnp.sum(value, axis=0, keepdims=True)


def attend_kernel(base, x_ref, wq_ref, wk_ref, wv_ref, vec_ref, seg_col_ref, seg_row_ref, *refs):
    q_ref, k_ref, v_ref, mixed_ref, lse_ref, mask_ref = refs
    i = pl.program_id(0)

    @pl.when(i == 0)
    def _():
        mask_ref[...] = jnp.where(seg_col_ref[...] == seg_row_ref[...], 0.0, masked_value)

    lanes = pl.ds(pl.multiple_of(i * group, group), group)
    x = x_ref[...]
    q = (mm(x, wq_ref[...]) + vec_ref[base + 2 : base + 3, lanes]).astype(bf16)
    k = mm(x, wk_ref[...]).astype(bf16)
    v = (mm(x, wv_ref[...]) + vec_ref[base + 3 : base + 4, lanes]).astype(bf16)
    q_ref[...] = q
    k_ref[...] = k
    v_ref[...] = v
    scaled = q * jnp.asarray(HEAD**-0.5, bf16)
    outs, lses = [], []
    for h in range(group // HEAD):
        c = slice(h * HEAD, (h + 1) * HEAD)
        scores = mm_nt(scaled[:, c], k[:, c]) + mask_ref[...]
        top = jnp.max(scores, axis=1, keepdims=True)
        raw = jnp.exp(scores - top)
        total = jnp.sum(raw, axis=1, keepdims=True)
        outs.append(mm(raw.astype(bf16), v[:, c]) / total)
        lses.append(top + jnp.log(total))
    mixed_ref[...] = jnp.concatenate(outs, axis=1).astype(bf16)
    lse_ref[...] = jnp.concatenate(lses + [jnp.zeros((SEQ, 128 - len(lses)), f32)], axis=1)


def attend(x, w_in, vec, base, seg_col, seg_row):
    def weight(b):
        return pl.BlockSpec((None, D, group), lambda i: (b, 0, i))

    out = pl.BlockSpec((SEQ, group), lambda i: (0, i))
    return pl.pallas_call(
        partial(attend_kernel, base),
        grid=(groups,),
        in_specs=[full(token_block)]
        + [weight(b) for b in range(3)]
        + [vec_spec, full((SEQ, 1)), full((1, SEQ))],
        out_specs=[out] * 4 + [pl.BlockSpec((None, SEQ, 128), lambda i: (i, 0, 0))],
        out_shape=[sds(token_block, bf16)] * 4 + [sds((groups, SEQ, 128), f32)],
        scratch_shapes=[pltpu.VMEM((SEQ, SEQ), f32)],
        compiler_params=params(),
        cost_estimate=cost(5 * product, 3e7),
        name="attend",
    )(x, w_in, w_in, w_in, vec, seg_col, seg_row)


def normalize(hidden):
    centered = hidden - jnp.mean(hidden, axis=1, keepdims=True)
    variance = jnp.mean(centered * centered, axis=1, keepdims=True)
    rstd = lax.rsqrt(variance + norm_eps)
    return centered * rstd, rstd


def gelu_both(x):
    base = 1.0 + 0.3275911 * 0.7071067811865476 * jnp.abs(x)
    t = pl.reciprocal(base, approx=True)
    t = t * (2.0 - base * t)
    bell = jnp.exp(x * x * -0.5)
    series = 1.421413741 + t * (-1.453152027 + t * 1.061405429)
    series = t * (0.254829592 + t * (-0.284496736 + t * series))
    tail = 0.5 * series * bell
    cdf = jnp.where(x >= 0, 1.0 - tail, tail)
    return x * cdf, cdf + x * bell * 0.3989422804014327


def widen_kernel(base, mixed_ref, x_ref, wo_ref, wi_ref, vec_ref, *refs):
    xhat_ref, rstd_ref, gelu_ref, dgelu_ref, normed_ref = refs
    i = pl.program_id(0)

    @pl.when(i == 0)
    def _():
        attended = mm(mixed_ref[...], wo_ref[...]) + vec_ref[base + 4 : base + 5, :]
        xhat, rstd = normalize(x_ref[...].astype(f32) + attended)
        xhat_ref[...] = xhat
        rstd_ref[...] = rstd
        normed = xhat * vec_ref[base : base + 1, :] + vec_ref[base + 5 : base + 6, :]
        normed_ref[...] = normed.astype(bf16)

    pre_act = mm(normed_ref[...], wi_ref[...]) + vec_ref[pl.ds(base + 8 + i, 1), :]
    value, slope = gelu_both(pre_act)
    gelu_ref[...] = value.astype(bf16)
    dgelu_ref[...] = slope.astype(bf16)


def widen(mixed, x, w_wide, vec, base):
    out = pl.BlockSpec(token_block, lambda i: (0, i))
    return pl.pallas_call(
        partial(widen_kernel, base),
        grid=(FF // D,),
        in_specs=[
            full(token_block),
            full(token_block),
            pl.BlockSpec((None, D, D), lambda i: (0, 0, 0)),
            pl.BlockSpec((None, D, D), lambda i: (1 + i, 0, 0)),
            vec_spec,
        ],
        out_specs=[full(token_block), full((SEQ, 1)), out, out],
        out_shape=[sds(token_block, f32), sds((SEQ, 1), f32)] + [sds((SEQ, FF), bf16)] * 2,
        scratch_shapes=[pltpu.VMEM(token_block, bf16)],
        compiler_params=params(),
        cost_estimate=cost(5 * product, 3e7),
        name="widen",
    )(mixed, x, w_wide, w_wide, vec)


def narrow_kernel(base, last, gelu_ref, wf_ref, xhat1_ref, vec_ref, *refs):
    if last:
        seg_row_ref, out_ref, xhat_ref, rstd_ref, pooled_ref, unit_ref, acc_ref = refs
    else:
        out_ref, xhat_ref, rstd_ref, acc_ref = refs
    i = pl.program_id(0)

    @pl.when(i == 0)
    def _():
        acc_ref[...] = mm(gelu_ref[...], wf_ref[...])

    @pl.when(i > 0)
    def _():
        acc_ref[...] += mm(gelu_ref[...], wf_ref[...])

    @pl.when(i == pl.num_programs(0) - 1)
    def _():
        normed = xhat1_ref[...] * vec_ref[base : base + 1, :] + vec_ref[base + 5 : base + 6, :]
        xhat, rstd = normalize(normed + (acc_ref[...] + vec_ref[base + 6 : base + 7, :]))
        xhat_ref[...] = xhat
        rstd_ref[...] = rstd
        out = xhat * vec_ref[base + 1 : base + 2, :] + vec_ref[base + 7 : base + 8, :]
        out_ref[...] = out.astype(bf16)
        if last:
            member = seg_row_ref[...] == lax.broadcasted_iota(jnp.int32, (8, SEQ), 0)
            count = jnp.sum(member.astype(f32), axis=1, keepdims=True)
            member = member.astype(bf16)
            high = out.astype(bf16)
            rest = out - high.astype(f32)
            middle = rest.astype(bf16)
            low = (rest - middle.astype(f32)).astype(bf16)
            pooled = mm(member, high) + mm(member, middle) + mm(member, low)
            pooled = pooled / jnp.maximum(count, 1.0)
            pooled_ref[...] = pooled
            norm = jnp.sum(pooled * pooled, axis=1, keepdims=True) + unit_eps
            unit_ref[...] = pooled * lax.rsqrt(norm)


def narrow(gelu, w_narrow, xhat1, vec, base, seg_row=None):
    last = seg_row is not None
    outs = [sds(token_block, bf16), sds(token_block, f32), sds((SEQ, 1), f32)]
    if last:
        outs += [sds((8, D), f32)] * 2
    return pl.pallas_call(
        partial(narrow_kernel, base, last),
        grid=(FF // D,),
        in_specs=[
            pl.BlockSpec(token_block, lambda i: (0, i)),
            pl.BlockSpec((None, D, D), lambda i: (0, i, 0)),
            full(token_block),
            vec_spec,
        ]
        + ([full((1, SEQ))] if last else []),
        out_specs=[full(out.shape) for out in outs],
        out_shape=outs,
        scratch_shapes=[pltpu.VMEM(token_block, f32)],
        compiler_params=params(),
        cost_estimate=cost(4 * product, 2e7),
        name="narrow",
    )(gelu, w_narrow, xhat1, vec, *([seg_row] if last else []))


def contrast_kernel(where_ref, table_ref, pooled_ref, groups_ref, partner_ref, seg_row_ref, *refs, total):
    loss_ref, gseg_ref = refs
    me, micro = where_ref[0], where_ref[1]
    dot = partial(lax.dot_general, precision=highest, preferred_element_type=f32)
    rows_nt = (((1,), (1,)), ((), ()))
    table = table_ref[...]
    count = table.shape[0]
    devices = count // 8
    segs = groups_ref.shape[1] // devices

    def sentence(shape, axis):
        index = lax.broadcasted_iota(jnp.int32, shape, axis)
        block, place = index >> 3, index & 7
        owner = jnp.zeros_like(block)
        far = devices // 2
        bit = 0
        while far >= 1:
            owner = owner | ((block >> bit) & 1) * far
            bit += 1
            far //= 2
        return jnp.where(place < segs, (owner ^ me) * segs + place, -1)

    ids_row, ids_col = sentence((1, count), 1), sentence((count, 1), 0)
    every = groups_ref.shape[1]
    groups = jnp.where(micro == 0, groups_ref[0:1, :], groups_ref[1:2, :]).astype(f32)
    groups = jnp.broadcast_to(groups, (8, every))
    hot_row = (lax.broadcasted_iota(jnp.int32, (every, 1), 0) == ids_row).astype(f32)
    hot_col = (lax.broadcasted_iota(jnp.int32, (1, every), 1) == ids_col).astype(f32)
    groups_row = dot(groups, hot_row, (((1,), (0,)), ((), ())))[0:1]
    groups_col = dot(hot_col, groups, rows_nt)[:, 0:1]
    logits = contrast_scale * dot(table, table, rows_nt)
    real = (ids_row >= 0) & (ids_col >= 0)
    allowed = real & (groups_col == groups_row) & (ids_col != ids_row)
    masked = jnp.where(allowed, logits, masked_value)
    top = jnp.max(masked, axis=0, keepdims=True)
    lse_row = top + jnp.log(column_sum(jnp.exp(masked - top)))
    mine = masked[:8]
    top = jnp.max(mine, axis=1, keepdims=True)
    raw = jnp.exp(mine - top)
    raw_total = jnp.sum(raw, axis=1, keepdims=True)
    across = jnp.exp(mine - lse_row)
    place = lax.broadcasted_iota(jnp.int32, (8, 1), 0)
    partner = jnp.zeros((8, 1), jnp.int32)
    for s in range(segs):
        partner = jnp.where(place == s, jnp.where(micro == 0, partner_ref[0, s], partner_ref[1, s]), partner)
    chosen = ((partner == ids_row) & (place < segs)).astype(f32)
    terms = top + jnp.log(raw_total) - jnp.sum(chosen * logits[:8], axis=1, keepdims=True)
    loss_ref[...] = column_sum(jnp.where(place < segs, terms, 0.0)) / total
    grad = raw / raw_total + across - 2.0 * chosen
    grad = contrast_scale * dot(grad, table, (((1,), (0,)), ((), ())))
    pooled = pooled_ref[...]
    scale = lax.rsqrt(jnp.sum(pooled * pooled, axis=1, keepdims=True) + unit_eps)
    dots = jnp.sum(grad * pooled, axis=1, keepdims=True)
    grad = scale * grad - pooled * (scale * scale * scale * dots)
    member = (seg_row_ref[...] == lax.broadcasted_iota(jnp.int32, (8, SEQ), 0)).astype(f32)
    gseg_ref[...] = grad / jnp.maximum(jnp.sum(member, axis=1, keepdims=True), 1.0)


def contrast(where, table, pooled, group_ids, partner, seg_row, total):
    vmem = pl.BlockSpec(memory_space=pltpu.VMEM)
    smem = pl.BlockSpec(memory_space=pltpu.SMEM)
    return pl.pallas_call(
        partial(contrast_kernel, total=total),
        out_shape=[sds((1, 1), f32), sds((8, D), f32)],
        in_specs=[smem, vmem, vmem, vmem, smem, vmem],
        out_specs=[vmem] * 2,
        compiler_params=params(),
        name="contrast",
    )(where, table, pooled, group_ids, partner, seg_row)


def norm_back(grad, xhat, rstd, gain):
    scaled = grad * gain
    mean = jnp.mean(scaled, axis=1, keepdims=True)
    along = jnp.mean(scaled * xhat, axis=1, keepdims=True)
    return rstd * (scaled - mean - xhat * along)


def put(slot, keep_ref, send_ref, index, value):
    @pl.when(slot < 8)
    def _():
        keep_ref[(slot,) + index] = value

    @pl.when(slot >= 8)
    def _():
        send_ref[(slot - 8,) + index] = value


def back_out_kernel(base, last, slot_ref, *refs):
    if last:
        cot_ref, seg_col_ref, gseg_ref, *refs = refs
    else:
        cot_ref, *refs = refs
    xhat_ref, rstd_ref, vec_ref, gelu_ref, gsum_ref, gbranch_ref, small_ref, keep_ref, send_ref = refs
    i = pl.program_id(0)

    @pl.when(i == 0)
    def _():
        grad = cot_ref[...].astype(f32)
        if last:
            for s in range(4):
                grad = grad + jnp.where(seg_col_ref[...] == s, gseg_ref[s : s + 1, :], 0.0)
        xhat = xhat_ref[...]
        grad_sum = norm_back(grad, xhat, rstd_ref[...], vec_ref[base + 1 : base + 2, :])
        gsum_ref[...] = grad_sum
        low = grad_sum.astype(bf16)
        gbranch_ref[...] = low
        small_ref[...] = jnp.zeros((16, D), f32)
        small_ref[1:2, :] = column_sum(grad * xhat)
        small_ref[6:7, :] = column_sum(low.astype(f32))
        small_ref[7:8, :] = column_sum(grad)

    rows = FF // 16
    grad_weight = mm_tn(gelu_ref[...], gbranch_ref[...]).astype(bf16)
    for j in range(4):
        put(slot_ref[4 * i + j], keep_ref, send_ref, (), grad_weight[j * rows : (j + 1) * rows])


def back_out(slot, cot, xhat2, rstd2, vec, base, gelu, seg_col=None, gseg=None):
    last = gseg is not None
    ins = [cot] + ([seg_col, gseg] if last else []) + [xhat2, rstd2, vec, gelu]
    outs = [sds(token_block, f32), sds(token_block, bf16), sds((16, D), f32)]
    outs += [sds((8, FF // 16, D), bf16)] * 2
    return pl.pallas_call(
        partial(back_out_kernel, base, last),
        grid_spec=pltpu.PrefetchScalarGridSpec(
            num_scalar_prefetch=1,
            grid=(FF // D,),
            in_specs=[full(a.shape) for a in ins[:-1]]
            + [pl.BlockSpec(token_block, lambda i, *_: (0, i))],
            out_specs=[full(out.shape) for out in outs],
        ),
        out_shape=outs,
        compiler_params=params(),
        cost_estimate=cost(4 * product, 2e7),
        name="back_out",
    )(slot, *ins)


def back_pre_kernel(base, slot_ref, *refs):
    gbranch_ref, wf_ref, dgelu_ref, xhat_ref, vec_ref, small_in_ref, *refs = refs
    gpre_ref, small_ref, keep_ref, send_ref, normed_ref = refs
    i = pl.program_id(0)
    rows = D // 16

    @pl.when(i == 0)
    def _():
        normed = xhat_ref[...] * vec_ref[base : base + 1, :] + vec_ref[base + 5 : base + 6, :]
        normed_ref[...] = normed.astype(bf16)
        small_ref[...] = small_in_ref[...]

    grad_gelu = mm_nt(gbranch_ref[...], wf_ref[...])
    grad_pre = (grad_gelu * dgelu_ref[...].astype(f32)).astype(bf16)
    gpre_ref[...] = grad_pre
    small_ref[pl.ds(8 + i, 1), :] = column_sum(grad_pre.astype(f32))
    grad_weight = mm_tn(normed_ref[...], grad_pre).astype(bf16)
    row = pl.multiple_of(rows * i, 16)
    for d in range(16):
        value = grad_weight[d * rows : (d + 1) * rows]
        put(slot_ref[d], keep_ref, send_ref, (pl.ds(row, rows),), value)


def back_pre(slot, gbranch, w_narrow, dgelu, xhat1, vec, base, small):
    outs = [sds((SEQ, FF), bf16), sds((16, D), f32)] + [sds((8, 4 * D // 16, D), bf16)] * 2
    return pl.pallas_call(
        partial(back_pre_kernel, base),
        grid_spec=pltpu.PrefetchScalarGridSpec(
            num_scalar_prefetch=1,
            grid=(FF // D,),
            in_specs=[
                full(token_block),
                pl.BlockSpec((None, D, D), lambda i, *_: (0, i, 0)),
                pl.BlockSpec(token_block, lambda i, *_: (0, i)),
                full(token_block),
                vec_spec,
                full((16, D)),
            ],
            out_specs=[pl.BlockSpec(token_block, lambda i, *_: (0, i))]
            + [full(out.shape) for out in outs[1:]],
            scratch_shapes=[pltpu.VMEM(token_block, bf16)],
        ),
        out_shape=outs,
        compiler_params=params(),
        cost_estimate=cost(8 * product, 3e7),
        name="back_pre",
    )(slot, gbranch, w_narrow, dgelu, xhat1, vec, small)


def back_mid_kernel(base, slot_ref, *refs):
    gsum_ref, gpre_ref, wi_ref, xhat_ref, rstd_ref, mixed_ref, wo_ref, vec_ref, *refs = refs
    small_in_ref, ghid_ref, gmixed_ref, small_ref, keep_ref, send_ref, acc_ref = refs
    i = pl.program_id(0)
    rows = D // 16

    @pl.when(i == 0)
    def _():
        acc_ref[...] = gsum_ref[...]
        small_ref[...] = small_in_ref[...]

    acc_ref[...] += mm_nt(gpre_ref[...], wi_ref[...])

    @pl.when(i == pl.num_programs(0) - 1)
    def _():
        grad = acc_ref[...]
        xhat = xhat_ref[...]
        grad_hidden = norm_back(grad, xhat, rstd_ref[...], vec_ref[base : base + 1, :])
        ghid_ref[...] = grad_hidden
        low = grad_hidden.astype(bf16)
        gmixed_ref[...] = mm_nt(low, wo_ref[...]).astype(bf16)
        small_ref[0:1, :] = column_sum(grad * xhat)
        small_ref[4:5, :] = column_sum(low.astype(f32))
        small_ref[5:6, :] = column_sum(grad)
        grad_out = mm_tn(mixed_ref[...], low).astype(bf16)
        for d in range(16):
            put(slot_ref[d], keep_ref, send_ref, (), grad_out[d * rows : (d + 1) * rows])


def back_mid(slot, gsum, gpre, w_wide, xhat1, rstd1, mixed, vec, base, small):
    outs = [sds(token_block, f32), sds(token_block, bf16), sds((16, D), f32)]
    outs += [sds((8, 4 * D // 16, D), bf16)] * 2
    return pl.pallas_call(
        partial(back_mid_kernel, base),
        grid_spec=pltpu.PrefetchScalarGridSpec(
            num_scalar_prefetch=1,
            grid=(FF // D,),
            in_specs=[
                full(token_block),
                pl.BlockSpec(token_block, lambda i, *_: (0, i)),
                pl.BlockSpec((None, D, D), lambda i, *_: (1 + i, 0, 0)),
                full(token_block),
                full((SEQ, 1)),
                full(token_block),
                pl.BlockSpec((None, D, D), lambda i, *_: (0, 0, 0)),
                vec_spec,
                full((16, D)),
            ],
            out_specs=[full(out.shape) for out in outs[:3]]
            + [pl.BlockSpec((8, D // 16, D), lambda i, *_: (0, 3, 0))] * 2,
            scratch_shapes=[pltpu.VMEM(token_block, f32)],
        ),
        out_shape=outs,
        compiler_params=params(),
        cost_estimate=cost(6 * product, 3e7),
        name="back_mid",
    )(slot, gsum, gpre, w_wide, xhat1, rstd1, mixed, w_wide, vec, small)


def attend_back_kernel(first, n_chunk, slot_ref, *refs):
    x_ref, q_ref, k_ref, v_ref, gm_ref, lse_ref, wq_ref, wk_ref, wv_ref, *refs = refs
    ghid_ref, seg_col_ref, seg_row_ref, small_in_ref, *refs = refs
    gx_ref, low_ref, small_ref, keep_ref, send_ref, mask_ref = refs[n_chunk:]
    i = pl.program_id(0)
    rows = D // 16

    @pl.when(i == 0)
    def _():
        mask_ref[...] = jnp.where(seg_col_ref[...] == seg_row_ref[...], 0.0, masked_value)
        gx_ref[...] = ghid_ref[...]
        small_ref[...] = small_in_ref[...]

    q, k, v, gm = q_ref[...], k_ref[...], v_ref[...], gm_ref[...]
    scaled = q * jnp.asarray(HEAD**-0.5, bf16)
    lse = jnp.transpose(lse_ref[...])
    parts = [[], [], []]
    for h in range(group // HEAD):
        c = slice(h * HEAD, (h + 1) * HEAD)
        probs = jnp.exp(mm_nt(k[:, c], scaled[:, c]) + mask_ref[...] - lse[h : h + 1, :])
        grad_probs = mm_nt(v[:, c], gm[:, c])
        parts[2].append(mm(probs.astype(bf16), gm[:, c]))
        dots = column_sum(grad_probs * probs)
        grad_scores = (probs * (grad_probs - dots)).astype(bf16)
        parts[1].append(mm(grad_scores, scaled[:, c]))
        parts[0].append(mm_tn(grad_scores, k[:, c]) * HEAD**-0.5)
    grads = [jnp.concatenate(part, axis=1).astype(bf16) for part in parts]
    x = x_ref[...]
    for b, grad in enumerate(grads):
        grad_weight = mm_tn(x, grad).astype(bf16)
        for d in range(16):
            index = (slice(b * rows, (b + 1) * rows),)
            put(slot_ref[d], keep_ref, send_ref, index, grad_weight[d * rows : (d + 1) * rows])
    lanes = pl.ds(pl.multiple_of((first + i) * group, group), group)
    small_ref[2:3, lanes] = column_sum(grads[0].astype(f32))
    small_ref[3:4, lanes] = column_sum(grads[2].astype(f32))
    gx_ref[...] += (
        mm_nt(grads[0], wq_ref[...]) + mm_nt(grads[1], wk_ref[...]) + mm_nt(grads[2], wv_ref[...])
    )

    @pl.when(i == pl.num_programs(0) - 1)
    def _():
        low_ref[...] = gx_ref[...].astype(bf16)


def attend_back(slot, x, q, k, v, gm, lse, w_in, ghid, seg_col, seg_row, small, first, count, chunk):
    def weight(b):
        return pl.BlockSpec((None, D, group), lambda i, *_: (b, 0, first + i))

    heads = pl.BlockSpec((SEQ, group), lambda i, *_: (0, first + i))
    units = pl.BlockSpec((8, 3 * D // 16, group), lambda i, *_: (0, 0, first + i))
    outs = [sds(token_block, f32), sds(token_block, bf16), sds((16, D), f32)]
    outs += [sds((8, 4 * D // 16, D), bf16)] * 2
    ins = [x, q, k, v, gm, lse, w_in, w_in, w_in, ghid, seg_col, seg_row, small]
    return pl.pallas_call(
        partial(attend_back_kernel, first, len(chunk)),
        grid_spec=pltpu.PrefetchScalarGridSpec(
            num_scalar_prefetch=1,
            grid=(count,),
            in_specs=[full(token_block)]
            + [heads] * 4
            + [pl.BlockSpec((None, SEQ, 128), lambda i, *_: (first + i, 0, 0))]
            + [weight(b) for b in range(3)]
            + [full(token_block), full((SEQ, 1)), full((1, SEQ)), full((16, D))]
            + [pl.BlockSpec(memory_space=pl.ANY)] * len(chunk),
            out_specs=[full(out.shape) for out in outs[:3]] + [units] * 2,
            scratch_shapes=[pltpu.VMEM((SEQ, SEQ), f32)],
        ),
        out_shape=outs,
        input_output_aliases={len(ins) + 1 + n: 3 + n for n in range(len(chunk))},
        compiler_params=params(),
        cost_estimate=cost(6 * count * product, 3e7),
        name="attend_back",
    )(slot, *ins, *chunk)


def blocked(shard):
    rows, columns = shard.shape
    return shard.reshape(rows, columns // D, D).transpose(1, 0, 2)


def unblocked(shard):
    blocks, rows, columns = shard.shape
    return shard.transpose(1, 0, 2).reshape(rows, blocks * columns)


class Cross:
    def __init__(self, shard):
        self.shard = shard
        self.moving = [swapped(shard, "section", 1)]

    def step(self):
        self.other = self.moving[0]
        self.moving = []

    def layer(self, layer):
        return jnp.where(lax.axis_index("section") == layer, self.shard, self.other)


def gather_plain(attn_in, attn_out, ff_in, ff_out):
    weights = [[], []]
    for shard in (attn_in, attn_out, ff_in, ff_out):
        both = lax.all_gather(shard.astype(bf16), ("section", "dp"), axis=0, tiled=True)
        half = both.shape[0] // 2
        for layer in range(2):
            weights[layer].append(blocked(both[layer * half : (layer + 1) * half]))
    return [[w[0], jnp.concatenate([w[1], w[2]]), w[3]] for w in weights]


def local(
    tokens,
    out_cotangent,
    lengths,
    partner,
    group_ids,
    attn_in,
    attn_out,
    ff_in,
    ff_out,
    norm_gains,
    biases,
    ff_bias,
):
    section = lax.axis_index("section").astype(jnp.int32)
    me = lax.axis_index("dp").astype(jnp.int32)
    leading = section == 0
    n_dp = lax.axis_size("dp")
    rows_in = D // n_dp
    rows_out = FF // n_dp
    segs = lengths.shape[-1]

    def pick(stack):
        return lax.dynamic_index_in_dim(stack, section, 0, keepdims=False)

    vectors = jnp.concatenate(
        [norm_gains[0].reshape(-1), biases[0].reshape(-1), ff_bias[0].reshape(-1)]
    ).astype(bf16)

    def vector_table(every):
        rows = every[:, :, : 8 * rows_in].reshape(n_dp, 2, 8, rows_in)
        rows = rows.transpose(1, 2, 0, 3).reshape(2, 8, D)
        bias = every[:, :, 8 * rows_in :].transpose(1, 0, 2).reshape(2, 4, D)
        return jnp.concatenate([rows, bias], axis=1).reshape(2 * table_rows, D).astype(f32)

    my_tokens = pick(tokens)[0]
    my_cotangent = pick(out_cotangent)[0]
    row_ends = jnp.cumsum(pick(lengths)[0], dtype=jnp.int32)
    places = jnp.arange(SEQ, dtype=jnp.int32)
    segment = jnp.sum((places[:, None] >= row_ends[None, :]).astype(jnp.int32), axis=-1)
    seg_col, seg_row = segment[:, None], segment[None, :]
    slot = slots()

    running = []
    if fast_ring():
        owner = gather_owners()
        cross_in = Cross(blocked(attn_in[0].astype(bf16)))
        cross_vec = Cross(vectors)
        onward([cross_in, cross_vec])
        table = jnp.stack([cross_vec.layer(0), cross_vec.layer(1)])
        table = jnp.pad(table, ((0, 14), (0, D - table.shape[1])))
        gather_vec = Gather(table[None])
        in0 = Gather(cross_in.layer(0))
        late = tie((attn_out, ff_in, ff_out), cross_in.other)
        wide_shard = [late[0][0].astype(bf16)[None], blocked(late[1][0].astype(bf16))]
        cross_wide = Cross(jnp.concatenate(wide_shard))
        onward([in0, gather_vec])
        onward([in0, gather_vec, cross_wide])
        wide_gather0 = Gather(cross_wide.layer(0))
        cross_narrow = Cross(tie(late[2], cross_wide.other)[0].astype(bf16)[None])
        onward([in0, gather_vec, wide_gather0])
        onward([in0, gather_vec, wide_gather0, cross_narrow])
        narrow_gather0 = Gather(cross_narrow.layer(0))
        onward([in0, gather_vec, wide_gather0, narrow_gather0])
        in1 = Gather(tie(cross_in.layer(1), narrow_gather0.pieces[0]))
        onward([in0, gather_vec, wide_gather0, narrow_gather0, in1])
        vec = assemble(gather_vec.all(), owner).reshape(n_dp, 16, D)
        vec = vector_table(vec[:, :2, : vectors.shape[0]])
        w_in0 = assemble(in0.all(), owner)
        q0, k0, v0, mixed0, lse0 = attend(my_tokens, w_in0, vec, 0, seg_col, seg_row)
        mixed0 = onward([wide_gather0, narrow_gather0, in1], mixed0)
        wide_gather1 = Gather(tie(cross_wide.layer(1), mixed0))
        onward([wide_gather0, narrow_gather0, in1, wide_gather1])
        w_wide0 = assemble(wide_gather0.all(), owner)
        wide0 = widen(mixed0, my_tokens, w_wide0, vec, 0)
        gelu0 = onward([narrow_gather0, in1, wide_gather1], wide0[2])
        narrow_gather1 = Gather(tie(cross_narrow.layer(1), gelu0))
        onward([narrow_gather0, in1, wide_gather1, narrow_gather1])
        w_narrow0 = assemble(narrow_gather0.all(), owner)
        middle, *tail0 = narrow(gelu0, w_narrow0, wide0[0], vec, 0)
        middle = onward([in1, wide_gather1, narrow_gather1], middle)
        w_in1 = assemble(in1.all(), owner)
        middle_sent = Sent(middle, [(1, 0)])
        q1, k1, v1, mixed1, lse1 = attend(middle, w_in1, vec, table_rows, seg_col, seg_row)
        mixed1 = onward([wide_gather1, narrow_gather1, middle_sent], mixed1)
        onward([wide_gather1, narrow_gather1, middle_sent])
        w_wide1 = assemble(wide_gather1.all(), owner)
        wide1 = widen(mixed1, middle, w_wide1, vec, table_rows)
        gelu1 = onward([narrow_gather1], wide1[2])
        onward([narrow_gather1])
        w_narrow1 = assemble(narrow_gather1.all(), owner)
        weights = [(w_in0, w_wide0, w_narrow0), (w_in1, w_wide1, w_narrow1)]
    else:
        weights = gather_plain(attn_in[0], attn_out[0], ff_in[0], ff_out[0])
        both = lax.all_gather(vectors, ("section", "dp")).reshape(2, n_dp, -1)
        vec = vector_table(both.transpose(1, 0, 2))
        q0, k0, v0, mixed0, lse0 = attend(my_tokens, weights[0][0], vec, 0, seg_col, seg_row)
        wide0 = widen(mixed0, my_tokens, weights[0][1], vec, 0)
        middle, *tail0 = narrow(wide0[2], weights[0][2], wide0[0], vec, 0)
        middle_sent = Sent(middle, [(1, 0)])
        q1, k1, v1, mixed1, lse1 = attend(middle, weights[1][0], vec, table_rows, seg_col, seg_row)
        wide1 = widen(mixed1, middle, weights[1][1], vec, table_rows)
        gelu1 = wide1[2]
        w_narrow1 = weights[1][2]
    final_low, *tail1, pooled, unit = narrow(
        gelu1, w_narrow1, wide1[0], vec, table_rows, seg_row
    )
    final_sent = Sent(final_low, [(0, 1)])
    running += [middle_sent, final_sent]

    table = gather_near(unit)
    total = MICRO * n_dp * segs
    where = jnp.stack([me, section])
    loss, grad_segs = contrast(where, table, pooled, group_ids, partner, seg_row, total)

    chunks = {}
    core = (me % 2)[None]

    def backward(layer, rows, heads, wide, tail, cot, segs_grad):
        base = layer * table_rows
        w_in, w_wide, w_narrow = weights[layer]
        q, k, v, mixed, lse = heads
        xhat1, rstd1, gelu, dgelu = wide
        grad_sum, grad_branch, small, keep, send = back_out(
            slot, cot, *tail, vec, base, gelu, *segs_grad
        )
        grad_branch = onward(running, grad_branch)
        chunks[layer, 2] = Reduction(core, keep, send)
        running.append(chunks[layer, 2])
        grad_pre, small, keep, send = back_pre(
            slot, grad_branch, w_narrow, dgelu, xhat1, vec, base, small
        )
        grad_pre = onward(running, grad_pre)
        chunks[layer, 1] = Reduction(core, keep, send)
        running.append(chunks[layer, 1])
        grad_x, grad_mixed, small, *chunk = back_mid(
            slot, grad_sum, grad_pre, w_wide, xhat1, rstd1, mixed, vec, base, small
        )
        grad_mixed = onward(running, grad_mixed)
        ins = (slot, rows, q, k, v, grad_mixed, lse, w_in)
        for first in range(groups):
            grad_x, grad_low, small, *chunk = attend_back(
                *ins, grad_x, seg_col, seg_row, small, first, 1, chunk
            )
            grad_x, grad_low = onward(running, (grad_x, grad_low))
        chunks[layer, 0] = Reduction(core, *chunk)
        running.append(chunks[layer, 0])
        return grad_x, grad_low, small

    heads = (q1, k1, v1, mixed1, lse1)
    grad_middle, grad_middle_low, small1 = backward(
        1, middle, heads, wide1, tail1, my_cotangent, (seg_col, grad_segs)
    )
    small1 = Sum(lax.dynamic_update_slice(small1, loss, (12, 0)))
    middle_grad_sent = Sent(grad_middle_low, [(0, 1)])
    running += [small1, middle_grad_sent]
    heads = (q0, k0, v0, mixed0, lse0)
    grad_tokens, grad_tokens_low, small0 = backward(
        0, my_tokens, heads, wide0, tail0, grad_middle_low, ()
    )
    small0 = Sum(small0)
    tokens_grad_sent = Sent(grad_tokens_low, [(1, 0)])
    running += [small0, tokens_grad_sent]

    settled = {}
    while True:
        for chunk in (2, 1, 0):
            ends = [chunks[layer, chunk] for layer in range(2)]
            if chunk not in settled and all(end.stage == 6 for end in ends):
                settled[chunk] = Settled(jnp.stack([me % 2, section]), *ends)
                running.append(settled[chunk])
        if not any(item.moving for item in running):
            break
        onward(running)

    if fast_ring():
        own_ff_out = settled[2].value
        own_ff_in = unblocked(settled[1].value.reshape(4, rows_in, D))
        own_attn_in = unblocked(settled[0].value[: 3 * rows_in].reshape(3, rows_in, D))
        own_attn_out = settled[0].value[3 * rows_in :]
    else:

        def natural(layer, name, blocks):
            item = chunks[layer, name]
            both = jnp.concatenate([item.keep, item.send])
            both = both.reshape(16, blocks, -1, D)
            return both.transpose(1, 0, 2, 3).reshape(blocks, -1, D)

        whole = [[], [], [], []]
        for layer in range(2):
            parts = natural(layer, 0, 4)
            whole[0].append(unblocked(parts[:3]))
            whole[1].append(parts[3])
            whole[2].append(unblocked(natural(layer, 1, 4)))
            whole[3].append(natural(layer, 2, 1)[0])
        own_attn_in, own_attn_out, own_ff_in, own_ff_out = (
            lax.psum_scatter(
                jnp.concatenate(pair).astype(f32), ("section", "dp"), scatter_dimension=0, tiled=True
            )
            for pair in whole
        )

    contrast_loss = small1.value[12, 0]
    small = jnp.where(leading, small0.value, small1.value)
    own_rows = lax.dynamic_slice(small, (0, me * rows_in), (8, rows_in))
    spot = me * rows_out
    own_bias = lax.dynamic_slice(small, (8 + spot // D, spot % D), (1, rows_out))

    hidden_states = jnp.where(
        leading,
        jnp.stack([middle, middle_sent.value()]),
        jnp.stack([final_sent.value(), final_low]),
    )
    hidden_grads = jnp.where(
        leading,
        jnp.stack([grad_tokens, tokens_grad_sent.value().astype(f32)]),
        jnp.stack([middle_grad_sent.value().astype(f32), grad_middle]),
    )
    return (
        contrast_loss,
        hidden_states[None, :, None],
        hidden_grads[None, :, None],
        own_attn_in[None],
        own_attn_out[None],
        own_ff_in[None],
        own_ff_out[None],
        own_rows[None, :2],
        own_rows[None, 2:],
        own_bias,
    )


def solution(mesh):
    return jax.shard_map(
        local,
        mesh=mesh,
        in_specs=(
            P(None, "dp", None, None),
            P(None, "dp", None, None),
            P(None, "dp", None),
            P(None, "dp"),
            P(),
            P("section", "dp", None),
            P("section", "dp", None),
            P("section", "dp", None),
            P("section", "dp", None),
            P("section", None, "dp"),
            P("section", None, "dp"),
            P("section", "dp"),
        ),
        out_specs=(
            P(),
            P("section", None, "dp", None, None),
            P("section", None, "dp", None, None),
            P("section", "dp", None),
            P("section", "dp", None),
            P("section", "dp", None),
            P("section", "dp", None),
            P("section", None, "dp"),
            P("section", None, "dp"),
            P("section", "dp"),
        ),
        check_vma=False,
    )
```

```python
from functools import partial

import jax
import jax.numpy as jnp
from jax import lax
from jax.experimental import pallas as pl
from jax.experimental.pallas import tpu as pltpu
from jax.sharding import PartitionSpec as P

D = 768
HEADS = 12
HEAD = 64
SEQ = 512
MICRO = 2
FF = 3072

bf16 = jnp.bfloat16
f32 = jnp.float32
highest = lax.Precision.HIGHEST
norm_eps = 1e-05
unit_eps = 1e-06
masked_value = -1000000000.0
contrast_scale = 10.0
vmem_limit = 16 * 2**20
slot_vmem = 36 * 2**20


def params(size=vmem_limit):
    return pltpu.CompilerParams(vmem_limit_bytes=size)


def cost(flops, size):
    return pl.CostEstimate(flops=int(10 * flops), bytes_accessed=int(10 * size), transcendentals=0)


def swapped(value, axis, mask):
    count = lax.axis_size(axis)
    return lax.ppermute(value, axis, [(i, i ^ mask) for i in range(count)])


def ring_order(chips):
    return list(range(0, chips, 2)) + list(range(chips - 1, 0, -2))


def ring_hop(value, backward=False):
    chips = lax.axis_size("dp") // 2
    order = ring_order(chips)
    pairs = []
    for place in range(chips):
        for core in range(2):
            step = 1 if core == 0 else -1
            pairs.append((order[place] * 2 + core, order[(place + step) % chips] * 2 + core))
    return lax.ppermute(value, "dp", pairs)


def ring_place(me):
    chips = lax.axis_size("dp") // 2
    order = ring_order(chips)
    places = [order.index(chip) for chip in range(chips)]
    place = jnp.asarray(places, jnp.int32)[me // 2]
    core = me % 2
    return place, 1 - 2 * core, core


def owners(me, steps, cores):
    chips = lax.axis_size("dp") // 2
    place, way, core = ring_place(me)
    order = jnp.asarray(ring_order(chips), jnp.int32)
    found = order[(place + way * jnp.asarray(steps, jnp.int32)) % chips] * 2
    return found + (core + jnp.asarray(cores, jnp.int32)) % 2


def fast_ring():
    return lax.axis_size("dp") == 16


def gather_owners(me):
    steps = [0, 0, -1, -1, -2, -2, -3, -3, -4, 1, 1, 2, 2, 3, 3, 4]
    cores = [0, 1, 0, 1, 0, 1, 0, 1, 0, 1, 0, 1, 0, 1, 0, 1]
    return owners(me, steps, cores)


def assemble_kernel(counts, owner_ref, *refs):
    pieces, out_ref, sems = refs[: len(counts)], refs[-2], refs[-1]
    rows = pieces[0].shape[2]
    copies = []
    for piece, count in zip(pieces, counts):
        for k in range(count):
            start = pl.multiple_of(owner_ref[len(copies)] * rows, 16)
            copies.append(
                pltpu.make_async_copy(
                    piece.at[k], out_ref.at[:, pl.ds(start, rows), :], sems.at[len(copies)]
                )
            )
    for copy in copies:
        copy.start()
    for copy in copies:
        copy.wait()


def assemble(pieces, owner):
    counts = [piece.shape[0] for piece in pieces]
    total = sum(counts)
    blocks, rows = pieces[0].shape[1:3]
    return pl.pallas_call(
        partial(assemble_kernel, counts),
        out_shape=jax.ShapeDtypeStruct((blocks, total * rows, D), bf16),
        in_specs=[pl.BlockSpec(memory_space=pltpu.SMEM)]
        + [pl.BlockSpec(memory_space=pl.ANY)] * len(pieces),
        out_specs=pl.BlockSpec(memory_space=pltpu.VMEM),
        scratch_shapes=[pltpu.SemaphoreType.DMA((total,))],
        compiler_params=params(),
        cost_estimate=cost(0, 1e7),
        name="assemble",
    )(owner, *[pltpu.with_memory_space_constraint(piece, pltpu.HBM) for piece in pieces])


unit_steps = [1, 1, 2, 2, 3, 3, 4, 0]


def slots(me):
    if not fast_ring():
        return jnp.arange(16, dtype=jnp.int32)
    both = jnp.arange(6, dtype=jnp.int32) % 2
    keep = owners(me, unit_steps, [0] * 8)
    send = owners(me, [-step for step in unit_steps], [1] * 8)
    table = [keep[:6] // 2 * 2 + both, keep[6:], send[:6] // 2 * 2 + both, send[6:]]
    table = jnp.concatenate(table)
    index = jnp.arange(16, dtype=jnp.int32)
    return jnp.sum(jnp.where(table[None, :] == index[:, None], index[None, :], 0), axis=1)


def fold_first_kernel(keep_ref, mate_ref, out_ref, own_ref):
    total = keep_ref[...].astype(f32) + mate_ref[...].astype(f32)
    out_ref[...] = total[:1].astype(bf16)
    own_ref[...] = total[1]


def fold_first(keep, mate):
    rows, width = keep.shape[1:]
    tile = rows // 2
    units = pl.BlockSpec((2, tile, width), lambda i: (3, i, 0))
    return pl.pallas_call(
        fold_first_kernel,
        grid=(2,),
        in_specs=[units, units],
        out_specs=[
            pl.BlockSpec((1, tile, width), lambda i: (0, i, 0)),
            pl.BlockSpec((tile, width), lambda i: (i, 0)),
        ],
        out_shape=[
            jax.ShapeDtypeStruct((1, rows, width), bf16),
            jax.ShapeDtypeStruct((rows, width), f32),
        ],
        compiler_params=params(),
        cost_estimate=cost(0, 0),
        name="fold_first",
    )(keep, mate)


def fold_kernel(one, core_ref, keep_ref, mate_ref, there_ref, out_ref):
    there = there_ref[...].astype(f32)
    if one:
        there = jnp.where(pl.program_id(0) == core_ref[0], there, 0.0)
    total = keep_ref[...].astype(f32) + mate_ref[...].astype(f32) + there
    out_ref[...] = total.astype(bf16)


def fold(core, keep, mate, first, there):
    rows, width = keep.shape[1:]
    one = there.shape[0] == 1
    unit = pl.BlockSpec((1, rows, width), lambda i, _: (first + i, 0, 0))
    out = pl.BlockSpec((1, rows, width), lambda i, _: (i, 0, 0))
    arrived = pl.BlockSpec((1, rows, width), lambda i, _: (0, 0, 0)) if one else out
    return pl.pallas_call(
        partial(fold_kernel, one),
        grid_spec=pltpu.PrefetchScalarGridSpec(
            num_scalar_prefetch=1, grid=(2,), in_specs=[unit, unit, arrived], out_specs=out
        ),
        out_shape=jax.ShapeDtypeStruct((2, rows, width), bf16),
        compiler_params=params(),
        cost_estimate=cost(0, 0),
        name="fold",
    )(core, keep, mate, there)


class Reduction:
    def __init__(self, core, keep, send):
        self.core, self.keep, self.send = core, keep, send
        self.moving = [swapped(send, "dp", 1)] if fast_ring() else []
        self.stage = 0

    def step(self):
        arrived = self.moving[0]
        if self.stage == 0:
            self.mate = arrived
            first, self.own = fold_first(self.keep, self.mate)
            self.moving = [ring_hop(first)]
        elif self.stage < 4:
            first = 6 - 2 * self.stage
            self.moving = [ring_hop(fold(self.core, self.keep, self.mate, first, arrived))]
        elif self.stage == 4:
            self.near = arrived
            self.moving = [swapped(self.near, "dp", 1)]
        else:
            self.last = arrived
            self.moving = []
        self.stage += 1

    def value(self):
        def mine(pair):
            return lax.dynamic_index_in_dim(pair, self.core[0], 0, keepdims=False).astype(f32)

        return self.own + mine(self.near) + mine(self.last)


class Sent:
    def __init__(self, value, pairs):
        self.moving = [lax.ppermute(value, "section", pairs)]

    def step(self):
        self.arrived = self.moving[0]
        self.moving = []

    def value(self):
        return self.arrived


class Near:
    def __init__(self, value):
        self.value, self.mask = value, lax.axis_size("dp") // 2
        self.send()

    def send(self):
        self.moving = [swapped(self.value, "dp", self.mask)] if self.mask else []

    def step(self):
        self.value = jnp.concatenate([self.value, self.moving[0]])
        self.mask //= 2
        self.send()


class Sum:
    def __init__(self, value):
        self.value, self.mask = value, lax.axis_size("dp") // 2
        self.send()

    def send(self):
        self.moving = [swapped(self.value, "dp", self.mask)] if self.mask else []

    def step(self):
        self.value = self.value + self.moving[0]
        self.mask //= 2
        self.send()


class Swapped:
    def __init__(self, value):
        self.own, self.moving = value, [swapped(value, "section", 1)]

    def step(self):
        self.both = self.own + self.moving[0]
        self.moving = []


class Gather:
    def __init__(self, shard):
        self.pieces, self.mates = [shard], []
        self.moving = [swapped(shard, "dp", 1)]
        self.stage = 0

    def step(self):
        if self.stage == 0:
            self.pieces = [jnp.stack([self.pieces[0], self.moving[0]])]
            self.moving = [ring_hop(self.pieces[0])]
        elif self.stage < 5:
            self.pieces.append(self.moving[0])
            self.mates += self.moving[1:]
            self.moving = [swapped(self.pieces[-1], "dp", 1)]
            if self.stage < 4:
                last = self.pieces[-1] if self.stage < 3 else self.pieces[-1][:1]
                self.moving = [ring_hop(last)] + self.moving
        else:
            self.mates += self.moving
            self.moving = []
        self.stage += 1

    def all(self):
        return self.pieces + self.mates


class Order:
    def __init__(self, start):
        self.token = start

    def onward(self, items, values=()):
        for item in items:
            if item.moving:
                item.moving, self.token = lax.optimization_barrier((item.moving, self.token))
                item.step()
        values, self.token = lax.optimization_barrier((values, self.token))
        return values


def tie(values, *others):
    return lax.optimization_barrier((values, others))[0]


def add_up(value, axis):
    mask = 1
    while mask < lax.axis_size(axis):
        value = value + swapped(value, axis, mask)
        mask *= 2
    return value


def mm(a, b):
    return lax.dot_general(a, b, (((1,), (0,)), ((), ())), preferred_element_type=f32)


def mm_nt(a, b):
    return lax.dot_general(a, b, (((1,), (1,)), ((), ())), preferred_element_type=f32)


def mm_tn(a, b):
    return lax.dot_general(a, b, (((0,), (0,)), ((), ())), preferred_element_type=f32)


def full(shape):
    return pl.BlockSpec(shape, lambda i, *_: (0,) * len(shape))


def sds(shape, dtype):
    return jax.ShapeDtypeStruct(shape, dtype)


def far(shape, dtype):
    return pltpu.HBM(shape, dtype)


group = 256
groups = D // group
product = 2 * SEQ * D * D
token_block = (SEQ, D)
table_rows = 12
loss_row = 12
entries = MICRO + 1
everything = pl.BlockSpec(memory_space=pl.ANY)


def far(shape, dtype):
    return pltpu.HBM(shape, dtype)


def tokens_buffer(width, dtype):
    return far((entries, SEQ, width), dtype)


def busy(i, m):
    return jnp.where(m[0] < MICRO, i, 0)


def at_entry(block, *where):
    place = where[0] if where else (lambda i: (0,) * len(block))
    return pl.BlockSpec((None, *block), lambda i, m: (m[0], *place(busy(i, m))))


def at_micro(block):
    return pl.BlockSpec((None, *block), lambda i, m: (jnp.minimum(m[0], MICRO - 1),) + (0,) * len(block))


def column_sum(value):
    return jnp.sum(value, axis=0, keepdims=True)


class Slot:
    def __init__(self, entry, ahead=False):
        self.entry, self.ahead = entry, ahead


def in_place(value):
    if value.ndim > 2 and value.shape[0] in (MICRO, entries):
        return pltpu.with_memory_space_constraint(value, pltpu.HBM)
    return value


def slot_call(kernel, m, grid, ins, in_specs, outs, out_specs, before, scratch, size, name, kept=None):
    first = len(outs) - len(before)
    aliases = {1 + len(ins) + n: first + n for n in range(len(before))}
    if kept is not None:
        aliases[1 + kept[0]] = kept[1]
    return pl.pallas_call(
        kernel,
        grid_spec=pltpu.PrefetchScalarGridSpec(
            num_scalar_prefetch=1,
            grid=(grid,),
            in_specs=in_specs + [everything] * len(before),
            out_specs=out_specs,
            scratch_shapes=scratch,
        ),
        out_shape=outs,
        input_output_aliases=aliases,
        compiler_params=params(slot_vmem),
        cost_estimate=cost(0, 0) if m.ahead else cost(size * product, 3e7),
        name=name,
    )(m.entry, *[in_place(value) for value in ins], *[in_place(value) for value in before])


def attend_kernel(n_before, m_ref, *refs):
    x_ref, wq_ref, wk_ref, wv_ref, vec_ref, seg_col_ref, seg_row_ref, *refs = refs
    q_ref, k_ref, v_ref, mixed_ref, lse_ref, mask_ref = refs[n_before:]
    i = pl.program_id(0)

    @pl.when(m_ref[0] < MICRO)
    def _():
        @pl.when(i == 0)
        def _():
            mask_ref[...] = jnp.where(seg_col_ref[...] == seg_row_ref[...], 0.0, masked_value)

        lanes = pl.ds(pl.multiple_of(i * group, group), group)
        x = x_ref[...]
        q = (mm(x, wq_ref[...]) + vec_ref[2:3, lanes]).astype(bf16)
        k = mm(x, wk_ref[...]).astype(bf16)
        v = (mm(x, wv_ref[...]) + vec_ref[3:4, lanes]).astype(bf16)
        q_ref[...] = q
        k_ref[...] = k
        v_ref[...] = v
        scaled = q * jnp.asarray(HEAD**-0.5, bf16)
        outs, lses = [], []
        for h in range(group // HEAD):
            c = slice(h * HEAD, (h + 1) * HEAD)
            scores = mm_nt(scaled[:, c], k[:, c]) + mask_ref[...]
            top = jnp.max(scores, axis=1, keepdims=True)
            raw = jnp.exp(scores - top)
            total = jnp.sum(raw, axis=1, keepdims=True)
            outs.append(mm(raw.astype(bf16), v[:, c]) / total)
            lses.append(top + jnp.log(total))
        mixed_ref[...] = jnp.concatenate(outs, axis=1).astype(bf16)
        lse_ref[...] = jnp.concatenate(lses + [jnp.zeros((SEQ, 128 - len(lses)), f32)], axis=1)


vec_spec = full((table_rows, D))


def attend(m, x, w_in, vec, seg_col, seg_row, before):
    def weight(b):
        return pl.BlockSpec((None, D, group), lambda i, m: (b, 0, busy(i, m)))

    heads = at_entry((SEQ, group), lambda i: (0, i))
    return slot_call(
        partial(attend_kernel, len(before)),
        m,
        groups,
        [x, w_in, w_in, w_in, vec, seg_col, seg_row],
        [full(token_block)]
        + [weight(b) for b in range(3)]
        + [vec_spec, at_entry((SEQ, 1)), at_entry((1, SEQ))],
        [tokens_buffer(D, bf16)] * 4 + [far((entries, groups, SEQ, 128), f32)],
        [heads] * 4 + [at_entry((None, SEQ, 128), lambda i: (i, 0, 0))],
        before,
        [pltpu.VMEM((SEQ, SEQ), f32)],
        5,
        "attend",
    )


def normalize(hidden):
    centered = hidden - jnp.mean(hidden, axis=1, keepdims=True)
    variance = jnp.mean(centered * centered, axis=1, keepdims=True)
    rstd = lax.rsqrt(variance + norm_eps)
    return centered * rstd, rstd


def gelu_both(x):
    cdf = 0.5 + 0.5 * lax.erf(x * 0.7071067811865476)
    return x * cdf, cdf + x * (jnp.exp(x * x * -0.5) * 0.3989422804014327)


def forward_kernel(last, n_before, m_ref, mixed_ref, x_ref, wo_ref, wi_ref, wf_ref, vec_ref, *refs):
    seg_row_ref, *refs = refs
    refs = refs[n_before:]
    if last:
        pooled_ref, unit_ref, *refs = refs
    else:
        out_ref, *refs = refs
    xhat1_ref, rstd1_ref, gelu_ref, dgelu_ref, state_ref, xhat2_ref, rstd2_ref, *refs = refs
    normed_ref, acc_ref = refs
    i = pl.program_id(0)

    @pl.when(m_ref[0] < MICRO)
    def _():
        @pl.when(i == 0)
        def _():
            attended = mm(mixed_ref[...], wo_ref[...]) + vec_ref[4:5, :]
            xhat, rstd = normalize(x_ref[...].astype(f32) + attended)
            xhat1_ref[...] = xhat.astype(bf16)
            rstd1_ref[...] = rstd
            normed = xhat * vec_ref[0:1, :] + vec_ref[5:6, :]
            normed_ref[...] = normed.astype(bf16)
            acc_ref[...] = normed + vec_ref[6:7, :]

        pre_act = mm(normed_ref[...], wi_ref[...]) + vec_ref[pl.ds(8 + i, 1), :]
        value, slope = gelu_both(pre_act)
        value = value.astype(bf16)
        gelu_ref[...] = value
        dgelu_ref[...] = slope.astype(bf16)
        acc_ref[...] += mm(value, wf_ref[...])

        @pl.when(i == pl.num_programs(0) - 1)
        def _():
            xhat, rstd = normalize(acc_ref[...])
            xhat2_ref[...] = xhat.astype(bf16)
            rstd2_ref[...] = rstd
            out = xhat * vec_ref[1:2, :] + vec_ref[7:8, :]
            state_ref[...] = out.astype(bf16)
            if not last:
                out_ref[...] = out.astype(bf16)
            else:
                member = seg_row_ref[...] == lax.broadcasted_iota(jnp.int32, (8, SEQ), 0)
                count = jnp.sum(member.astype(f32), axis=1, keepdims=True)
                member = member.astype(bf16)
                high = out.astype(bf16)
                rest = out - high.astype(f32)
                middle = rest.astype(bf16)
                low = (rest - middle.astype(f32)).astype(bf16)
                pooled = mm(member, high) + mm(member, middle) + mm(member, low)
                pooled = pooled / jnp.maximum(count, 1.0)
                pooled_ref[...] = pooled
                norm = jnp.sum(pooled * pooled, axis=1, keepdims=True) + unit_eps
                unit_ref[...] = pooled * lax.rsqrt(norm)

    if last:

        @pl.when(m_ref[0] >= MICRO)
        def _():
            pooled_ref[...] = jnp.zeros((8, D), f32)
            unit_ref[...] = jnp.zeros((8, D), f32)


def forward(m, mixed, x, w_wide, w_narrow, vec, seg_row, last, before):
    part = at_entry(token_block, lambda i: (0, i))
    now = [sds((8, D), f32)] * 2 if last else [sds(token_block, bf16)]
    row = sds((entries, SEQ, 1), f32)
    outs = now + [tokens_buffer(D, bf16), row] + [tokens_buffer(FF, bf16)] * 2
    outs += [tokens_buffer(D, bf16), tokens_buffer(D, bf16), row]
    return slot_call(
        partial(forward_kernel, last, len(before)),
        m,
        FF // D,
        [mixed, x, w_wide, w_wide, w_narrow, vec, seg_row],
        [
            at_entry(token_block),
            full(token_block),
            pl.BlockSpec((None, D, D), lambda i, m: (0, 0, 0)),
            pl.BlockSpec((None, D, D), lambda i, m: (1 + busy(i, m), 0, 0)),
            pl.BlockSpec((None, D, D), lambda i, m: (0, busy(i, m), 0)),
            vec_spec,
            at_entry((1, SEQ)),
        ],
        outs,
        [full(out.shape) for out in now]
        + [at_entry(token_block), at_entry((SEQ, 1)), part, part]
        + [at_entry(token_block), at_entry(token_block), at_entry((SEQ, 1))],
        before,
        [pltpu.VMEM(token_block, bf16), pltpu.VMEM(token_block, f32)],
        9,
        "forward",
    )


def contrast_kernel(me_ref, table_ref, pooled_ref, groups_ref, partner_ref, seg_row_ref, *refs, micro, total):
    loss_ref, gseg_ref = refs
    me = me_ref[0]
    dot = partial(lax.dot_general, precision=highest, preferred_element_type=f32)
    rows_nt = (((1,), (1,)), ((), ()))
    table = table_ref[...].reshape(-1, D)
    count = table.shape[0]
    devices = count // 8
    every = groups_ref.shape[1]
    segs = every // devices

    def sentence(shape, axis):
        index = lax.broadcasted_iota(jnp.int32, shape, axis)
        block, place = index >> 3, index & 7
        owner = jnp.zeros_like(block)
        far_one = devices // 2
        bit = 0
        while far_one >= 1:
            owner = owner | ((block >> bit) & 1) * far_one
            bit += 1
            far_one //= 2
        return jnp.where(place < segs, (owner ^ me) * segs + place, -1)

    ids_row, ids_col = sentence((1, count), 1), sentence((count, 1), 0)
    ids = groups_ref[micro : micro + 1, :].astype(f32)
    ids = jnp.broadcast_to(ids, (8, every))
    hot_row = (lax.broadcasted_iota(jnp.int32, (every, 1), 0) == ids_row).astype(f32)
    hot_col = (lax.broadcasted_iota(jnp.int32, (1, every), 1) == ids_col).astype(f32)
    groups_row = dot(ids, hot_row, (((1,), (0,)), ((), ())))[0:1]
    groups_col = dot(hot_col, ids, rows_nt)[:, 0:1]
    logits = contrast_scale * dot(table, table, rows_nt)
    real = (ids_row >= 0) & (ids_col >= 0)
    allowed = real & (groups_col == groups_row) & (ids_col != ids_row)
    masked = jnp.where(allowed, logits, masked_value)
    top = jnp.max(masked, axis=0, keepdims=True)
    lse_row = top + jnp.log(column_sum(jnp.exp(masked - top)))
    mine = masked[:8]
    top = jnp.max(mine, axis=1, keepdims=True)
    raw = jnp.exp(mine - top)
    raw_total = jnp.sum(raw, axis=1, keepdims=True)
    across = jnp.exp(mine - lse_row)
    place = lax.broadcasted_iota(jnp.int32, (8, 1), 0)
    partner = jnp.zeros((8, 1), jnp.int32)
    for s in range(segs):
        partner = jnp.where(place == s, partner_ref[micro, s], partner)
    chosen = ((partner == ids_row) & (place < segs)).astype(f32)
    terms = top + jnp.log(raw_total) - jnp.sum(chosen * logits[:8], axis=1, keepdims=True)
    loss = column_sum(jnp.where(place < segs, terms, 0.0)) / total
    loss_ref[...] = jnp.broadcast_to(loss, (1, D))
    grad = raw / raw_total + across - 2.0 * chosen
    grad = contrast_scale * dot(grad, table, (((1,), (0,)), ((), ())))
    pooled = pooled_ref[...]
    scale = lax.rsqrt(jnp.sum(pooled * pooled, axis=1, keepdims=True) + unit_eps)
    dots = jnp.sum(grad * pooled, axis=1, keepdims=True)
    grad = scale * grad - pooled * (scale * scale * scale * dots)
    member = (seg_row_ref[...] == lax.broadcasted_iota(jnp.int32, (8, SEQ), 0)).astype(f32)
    gseg_ref[...] = grad / jnp.maximum(jnp.sum(member, axis=1, keepdims=True), 1.0)


def contrast(me, table, pooled, group_ids, partner, seg_row, micro, total):
    smem = pl.BlockSpec(memory_space=pltpu.SMEM)
    return pl.pallas_call(
        partial(contrast_kernel, micro=micro, total=total),
        grid=(1,),
        out_shape=[sds((1, D), f32), sds((8, D), f32)],
        in_specs=[
            smem,
            full(table.shape),
            full((8, D)),
            full(group_ids.shape),
            smem,
            pl.BlockSpec((None, 1, SEQ), lambda i: (micro, 0, 0)),
        ],
        out_specs=[full((1, D)), full((8, D))],
        compiler_params=params(slot_vmem),
        name="contrast",
    )(me, table, pooled, group_ids, partner, seg_row)


def norm_back(grad, xhat, rstd, gain):
    scaled = grad * gain
    mean = jnp.mean(scaled, axis=1, keepdims=True)
    along = jnp.mean(scaled * xhat, axis=1, keepdims=True)
    return rstd * (scaled - mean - xhat * along)


def ff_back_kernel(last, n_before, m_ref, cot_ref, *refs):
    if last:
        seg_col_ref, gseg_ref, loss_ref, *refs = refs
    xhat2_ref, rstd2_ref, vec_ref, wf_ref, dgelu_ref, wi_ref, xhat1_ref, rstd1_ref, *refs = refs
    wo_ref, small_in_ref, *refs = refs
    ghid_ref, gmixed_ref, small_ref, gbranch_ref, gpre_ref, gatt_ref, acc_ref = refs[n_before:]
    i = pl.program_id(0)

    @pl.when(i == 0)
    def _():
        small_ref[...] = small_in_ref[...]

    @pl.when(m_ref[0] < MICRO)
    def _():
        @pl.when(i == 0)
        def _():
            grad = cot_ref[...].astype(f32)
            if last:
                for s in range(4):
                    grad = grad + jnp.where(seg_col_ref[...] == s, gseg_ref[s : s + 1, :], 0.0)
            xhat = xhat2_ref[...].astype(f32)
            grad_sum = norm_back(grad, xhat, rstd2_ref[...], vec_ref[1:2, :])
            acc_ref[...] = grad_sum
            low = grad_sum.astype(bf16)
            gbranch_ref[...] = low
            if last:
                small_ref[loss_row : loss_row + 1, :] += loss_ref[...]
            small_ref[1:2, :] += column_sum(grad * xhat)
            small_ref[6:7, :] += column_sum(low.astype(f32))
            small_ref[7:8, :] += column_sum(grad)

        grad_gelu = mm_nt(gbranch_ref[...], wf_ref[...])
        grad_pre = (grad_gelu * dgelu_ref[...].astype(f32)).astype(bf16)
        gpre_ref[...] = grad_pre
        small_ref[pl.ds(8 + i, 1), :] += column_sum(grad_pre.astype(f32))
        acc_ref[...] += mm_nt(grad_pre, wi_ref[...])

        @pl.when(i == pl.num_programs(0) - 1)
        def _():
            grad = acc_ref[...]
            xhat = xhat1_ref[...].astype(f32)
            grad_hidden = norm_back(grad, xhat, rstd1_ref[...], vec_ref[0:1, :])
            ghid_ref[...] = grad_hidden
            low = grad_hidden.astype(bf16)
            gatt_ref[...] = low
            gmixed_ref[...] = mm_nt(low, wo_ref[...]).astype(bf16)
            small_ref[0:1, :] += column_sum(grad * xhat)
            small_ref[4:5, :] += column_sum(low.astype(f32))
            small_ref[5:6, :] += column_sum(grad)


def ff_back(m, cot, segs, xhat2, rstd2, vec, w_narrow, dgelu, w_wide, xhat1, rstd1, small, before):
    last = len(segs) > 0
    part = at_entry(token_block, lambda i: (0, i))
    return slot_call(
        partial(ff_back_kernel, last, len(before)),
        m,
        FF // D,
        [cot, *segs, xhat2, rstd2, vec, w_narrow, dgelu, w_wide, xhat1, rstd1, w_wide, small],
        (
            [at_micro(token_block), at_entry((SEQ, 1)), full((8, D)), full((1, D))]
            if last
            else [full(token_block)]
        )
        + [
            at_entry(token_block),
            at_entry((SEQ, 1)),
            vec_spec,
            pl.BlockSpec((None, D, D), lambda i, m: (0, busy(i, m), 0)),
            part,
            pl.BlockSpec((None, D, D), lambda i, m: (1 + busy(i, m), 0, 0)),
            at_entry(token_block),
            at_entry((SEQ, 1)),
            pl.BlockSpec((None, D, D), lambda i, m: (0, 0, 0)),
            full((16, D)),
        ],
        [sds(token_block, f32), sds(token_block, bf16), sds((16, D), f32)]
        + [tokens_buffer(D, bf16), tokens_buffer(FF, bf16), far((entries, 4, SEQ, D), bf16)],
        [full(token_block), full(token_block), full((16, D))]
        + [at_entry(token_block), part, at_entry((None, SEQ, D), lambda i: (3, 0, 0))],
        before,
        [pltpu.VMEM(token_block, f32)],
        12,
        "ff_back",
    )


def attend_back_kernel(first, n_total, n_before, m_ref, *refs):
    q_ref, k_ref, v_ref, gm_ref, lse_ref, wq_ref, wk_ref, wv_ref, *refs = refs
    totals, refs = refs[:n_total], refs[n_total:]
    seg_col_ref, seg_row_ref, small_in_ref, *refs = refs
    low_ref, small_ref, gx_ref, gqkv_ref, mask_ref = refs[n_before:]
    i = pl.program_id(0)
    active = m_ref[0] < MICRO

    @pl.when(i == 0)
    def _():
        small_ref[...] = small_in_ref[...]

    @pl.when((i == 0) & active)
    def _():
        mask_ref[...] = jnp.where(seg_col_ref[...] == seg_row_ref[...], 0.0, masked_value)
        gx_ref[...] = totals[0][...]

    @pl.when((i == 0) & jnp.logical_not(active))
    def _():
        gx_ref[...] = totals[-1][...]

    @pl.when(active)
    def _():
        q, k, v, gm = q_ref[...], k_ref[...], v_ref[...], gm_ref[...]
        scaled = q * jnp.asarray(HEAD**-0.5, bf16)
        lse = jnp.transpose(lse_ref[...])
        parts = [[], [], []]
        for h in range(group // HEAD):
            c = slice(h * HEAD, (h + 1) * HEAD)
            probs = jnp.exp(mm_nt(k[:, c], scaled[:, c]) + mask_ref[...] - lse[h : h + 1, :])
            grad_probs = mm_nt(v[:, c], gm[:, c])
            parts[2].append(mm(probs.astype(bf16), gm[:, c]))
            dots = column_sum(grad_probs * probs)
            grad_scores = (probs * (grad_probs - dots)).astype(bf16)
            parts[1].append(mm(grad_scores, scaled[:, c]))
            parts[0].append(mm_tn(grad_scores, k[:, c]) * HEAD**-0.5)
        grads = [jnp.concatenate(part, axis=1).astype(bf16) for part in parts]
        for b, grad in enumerate(grads):
            gqkv_ref[b] = grad
        lanes = pl.ds(pl.multiple_of((first + i) * group, group), group)
        small_ref[2:3, lanes] += column_sum(grads[0].astype(f32))
        small_ref[3:4, lanes] += column_sum(grads[2].astype(f32))
        gx_ref[...] += (
            mm_nt(grads[0], wq_ref[...]) + mm_nt(grads[1], wk_ref[...]) + mm_nt(grads[2], wv_ref[...])
        )

        @pl.when(i == pl.num_programs(0) - 1)
        def _():
            low_ref[...] = gx_ref[...].astype(bf16)


def attend_back(m, q, k, v, gm, lse, w_in, totals, seg_col, seg_row, small, first, count, before):
    def weight(b):
        return pl.BlockSpec((None, D, group), lambda i, m: (b, 0, first + busy(i, m)))

    heads = at_entry((SEQ, group), lambda i: (0, first + i))
    buffer = at_micro(token_block)
    total_specs = [buffer] if first else [full(token_block), buffer][: len(totals)]
    return slot_call(
        partial(attend_back_kernel, first, len(totals), len(before)),
        m,
        count,
        [q, k, v, gm, lse, w_in, w_in, w_in, *totals, seg_col, seg_row, small],
        [heads] * 3
        + [pl.BlockSpec((SEQ, group), lambda i, m: (0, first + busy(i, m)))]
        + [at_entry((None, SEQ, 128), lambda i: (first + i, 0, 0))]
        + [weight(b) for b in range(3)]
        + total_specs
        + [at_entry((SEQ, 1)), at_entry((1, SEQ)), full((16, D))],
        [sds(token_block, bf16), sds((16, D), f32)]
        + [far((MICRO, SEQ, D), f32), far((entries, 4, SEQ, D), bf16)],
        [full(token_block), full((16, D)), buffer]
        + [at_entry((3, SEQ, group), lambda i: (0, 0, first + i))],
        before,
        [pltpu.VMEM((SEQ, SEQ), f32)],
        6 * count,
        "attend_back",
        (7 + len(totals), 2) if first or len(totals) > 1 else None,
    )


def put(slot, keep_ref, send_ref, index, value):
    @pl.when(slot < 8)
    def _():
        keep_ref[(slot,) + index] = value

    @pl.when(slot >= 8)
    def _():
        send_ref[(slot - 8,) + index] = value


def weight_call(kernel, slot, ins, in_specs, scratch, name):
    outs = [sds((8, FF // 16, D), bf16)] * 2
    return pl.pallas_call(
        kernel,
        grid_spec=pltpu.PrefetchScalarGridSpec(
            num_scalar_prefetch=1,
            grid=(4,),
            in_specs=in_specs,
            out_specs=[full(out.shape) for out in outs],
            scratch_shapes=scratch,
        ),
        out_shape=outs,
        compiler_params=params(),
        cost_estimate=cost(8 * product, 3e7),
        name=name,
    )(slot, *[in_place(value) for value in ins])


def weight_out_kernel(slot_ref, gelu_ref, gbranch_ref, keep_ref, send_ref):
    i = pl.program_id(0)
    rows = FF // 16
    total = sum(mm_tn(gelu_ref[m], gbranch_ref[m]) for m in range(MICRO)).astype(bf16)
    for j in range(4):
        put(slot_ref[4 * i + j], keep_ref, send_ref, (), total[j * rows : (j + 1) * rows])


def weight_wide_kernel(slot_ref, xhat_ref, vec_ref, gpre_ref, keep_ref, send_ref, normed_ref):
    i = pl.program_id(0)
    rows = D // 16

    @pl.when(i == 0)
    def _():
        for m in range(MICRO):
            normed = (xhat_ref[m].astype(f32) * vec_ref[0:1, :] + vec_ref[5:6, :]).astype(bf16)
            normed_ref[:, m * SEQ : (m + 1) * SEQ] = jnp.transpose(normed)

    total = mm(normed_ref[...], gpre_ref[...].reshape(MICRO * SEQ, D)).astype(bf16)
    row = pl.multiple_of(rows * i, 16)
    for d in range(16):
        put(slot_ref[d], keep_ref, send_ref, (pl.ds(row, rows),), total[d * rows : (d + 1) * rows])


def weight_attn_kernel(slot_ref, x_ref, mixed_ref, grad_ref, keep_ref, send_ref, left_ref):
    i = pl.program_id(0)
    rows = D // 16

    def turn(ref):
        for m in range(MICRO):
            left_ref[:, m * SEQ : (m + 1) * SEQ] = jnp.transpose(ref[m])

    @pl.when(i == 0)
    def _():
        turn(x_ref)

    @pl.when(i == 3)
    def _():
        turn(mixed_ref)

    total = mm(left_ref[...], grad_ref[...].reshape(MICRO * SEQ, D)).astype(bf16)
    row = pl.multiple_of(rows * i, 16)
    for d in range(16):
        put(slot_ref[d], keep_ref, send_ref, (pl.ds(row, rows),), total[d * rows : (d + 1) * rows])


both_blocks = (MICRO, SEQ, D)
both_parts = pl.BlockSpec(both_blocks, lambda i, _: (0, 0, i))


def weight_out(slot, gelu, gbranch):
    specs = [both_parts, full(both_blocks)]
    return weight_call(weight_out_kernel, slot, [gelu, gbranch], specs, [], "weight_out")


def weight_wide(slot, xhat1, vec, gpre):
    specs = [full(both_blocks), vec_spec, both_parts]
    scratch = [pltpu.VMEM((D, MICRO * SEQ), bf16)]
    return weight_call(weight_wide_kernel, slot, [xhat1, vec, gpre], specs, scratch, "weight_wide")


def weight_attn(slot, x, mixed, grads):
    grad_spec = pl.BlockSpec((MICRO, None, SEQ, D), lambda i, _: (0, i, 0, 0))
    specs = [full(both_blocks), full(both_blocks), grad_spec]
    scratch = [pltpu.VMEM((D, MICRO * SEQ), bf16)]
    return weight_call(weight_attn_kernel, slot, [x, mixed, grads], specs, scratch, "weight_attn")


def blocked(shard):
    rows, columns = shard.shape
    return shard.reshape(rows, columns // D, D).transpose(1, 0, 2)


def unblocked(shard):
    blocks, rows, columns = shard.shape
    return shard.transpose(1, 0, 2).reshape(rows, blocks * columns)


def gather_plain(shard):
    return blocked(lax.all_gather(shard.astype(bf16), "dp", axis=0, tiled=True))


def local(
    tokens,
    out_cotangent,
    lengths,
    partner,
    group_ids,
    attn_in,
    attn_out,
    ff_in,
    ff_out,
    norm_gains,
    biases,
    ff_bias,
):
    section = lax.axis_index("section").astype(jnp.int32)
    me = lax.axis_index("dp").astype(jnp.int32)
    leading = section == 0
    n_dp = lax.axis_size("dp")
    rows_in = D // n_dp
    rows_out = FF // n_dp
    segs = lengths.shape[-1]

    vectors = jnp.concatenate(
        [norm_gains[0].reshape(-1), biases[0].reshape(-1), ff_bias[0].reshape(-1)]
    ).astype(bf16)

    def vector_table(every):
        rows = every[:, : 8 * rows_in].reshape(n_dp, 8, rows_in).transpose(1, 0, 2).reshape(8, D)
        return jnp.concatenate([rows, every[:, 8 * rows_in :].reshape(4, D)]).astype(f32)

    spare = jnp.int32(MICRO)

    def entry(micro, layer):
        return jnp.where(section == layer, jnp.int32(micro), spare)[None]

    def segment_forms(lengths):
        row_ends = jnp.cumsum(lengths[:, 0], axis=-1, dtype=jnp.int32)
        places = jnp.arange(SEQ, dtype=jnp.int32)
        segment = jnp.sum((places[None, :, None] >= row_ends[:, None, :]).astype(jnp.int32), axis=-1)
        segment = jnp.concatenate([segment, segment[:1]])
        return segment[:, :, None], segment[:, None, :]

    order = Order(lengths[0, 0, 0])
    onward = order.onward

    first = Slot(entry(0, 0))
    x = tokens[0, 0]
    if fast_ring():
        in_gather = Gather(blocked(attn_in[0].astype(bf16)))
        table = jnp.pad(vectors[None], ((0, 15), (0, D - vectors.shape[0])))
        vec_gather = Gather(table[None])
        onward([in_gather, vec_gather])
        onward([in_gather, vec_gather])
        late = tie((attn_out, ff_in, ff_out, lengths, me), in_gather.pieces[1])
        wide_shard = [late[0][0].astype(bf16)[None], blocked(late[1][0].astype(bf16))]
        wide_gather = Gather(jnp.concatenate(wide_shard))
        seg_col, seg_row = segment_forms(late[3])
        owner, slot = gather_owners(late[4]), slots(late[4])
        onward([in_gather, vec_gather])
        onward([wide_gather])
        onward([in_gather, vec_gather])
        narrow_gather = Gather(tie(late[2], in_gather.pieces[3])[0].astype(bf16)[None])
        onward([in_gather, vec_gather])
        onward([wide_gather])
        onward([narrow_gather])
        onward([in_gather, vec_gather])
        vec = assemble(vec_gather.all(), owner).reshape(n_dp, 16, D)
        vec = vector_table(vec[:, 0, : vectors.shape[0]])
        w_in = assemble(in_gather.all(), owner)
        heads = attend(first, x, w_in, vec, seg_col, seg_row, [])
        heads = onward([wide_gather, narrow_gather], heads)
        onward([wide_gather, narrow_gather])
        onward([wide_gather])
        onward([narrow_gather])
        onward([wide_gather])
        w_wide = assemble(wide_gather.all(), owner)
        onward([narrow_gather])
        onward([narrow_gather])
        w_narrow = assemble(narrow_gather.all(), owner)
    else:
        w_in = gather_plain(attn_in[0])
        w_wide = jnp.concatenate([gather_plain(attn_out[0]), gather_plain(ff_in[0])])
        w_narrow = gather_plain(ff_out[0])
        vec = vector_table(lax.all_gather(vectors, "dp"))
        seg_col, seg_row = segment_forms(lengths)
        slot = slots(me)
        heads = attend(first, x, w_in, vec, seg_col, seg_row, [])
    out, *stored = forward(first, heads[3], x, w_wide, w_narrow, vec, seg_row, False, [])
    pairs = [(0, 1)]
    sent0 = Sent(out, pairs)

    second = Slot(entry(1, 0), True)
    x = tokens[1, 0]
    heads = attend(second, x, w_in, vec, seg_col, seg_row, heads)
    out, *stored = forward(second, heads[3], x, w_wide, w_narrow, vec, seg_row, False, stored)
    heads, stored, out = onward([sent0], (heads, stored, out))
    sent1 = Sent(out, pairs)

    third = Slot(entry(0, 1), True)
    x = received0 = sent0.value()
    heads = attend(third, x, w_in, vec, seg_col, seg_row, heads)
    pooled0, unit0, *stored = forward(
        third, heads[3], x, w_wide, w_narrow, vec, seg_row, True, stored
    )
    near0 = Near(unit0)
    heads, stored = onward([sent1], (heads, stored))

    fourth = Slot(entry(1, 1))
    x = received1 = sent1.value()
    heads = attend(fourth, x, w_in, vec, seg_col, seg_row, heads)
    heads = onward([near0], heads)
    pooled1, unit1, *stored = forward(
        fourth, heads[3], x, w_wide, w_narrow, vec, seg_row, True, stored
    )
    q, k, v, mixed, lse = heads
    xhat1, rstd1, gelu, dgelu, states, xhat2, rstd2 = stored

    total = MICRO * n_dp * segs

    def contrasted(near, pooled, micro):
        while near.moving:
            onward([near])
        table = near.value.reshape(-1, D)
        loss, grad_segs = contrast(
            me[None], table, pooled, group_ids, partner, seg_row, micro, total
        )
        return seg_col, grad_segs, loss

    near1 = Near(unit1)
    segs0 = contrasted(near0, pooled0, 0)

    cots = out_cotangent[:, 0]
    grads = []
    hidden_grads = []
    small = jnp.zeros((16, D), f32)

    def ff_slot(m, cot, segs_in, small):
        grad_hidden, grad_mixed, small, *buffers = ff_back(
            m, cot, segs_in, xhat2, rstd2, vec, w_narrow, dgelu, w_wide, xhat1, rstd1, small, grads
        )
        return grad_hidden, grad_mixed, small, buffers

    def heads_slot(m, grad_hidden, grad_mixed, small, buffers, items, calls):
        total, all_grads = grad_hidden, buffers[2]
        for first, count in calls:
            low, small, total, all_grads = attend_back(
                m,
                *(q, k, v, grad_mixed, lse, w_in),
                [total] if first else [total] + hidden_grads,
                *(seg_col, seg_row, small, first, count, [all_grads]),
            )
            total, all_grads, low, small = onward(items(), (total, all_grads, low, small))
        return low, small, [total], [buffers[0], buffers[1], all_grads]

    all_heads = ((0, groups),)
    pairs = [(1, 0)]
    m = Slot(entry(0, 1))
    state = ff_slot(m, cots, segs0, small)
    state = onward([near1], state)
    two_calls = ((0, 2), (2, 1))
    low, small, hidden_grads, grads = heads_slot(m, *state, lambda: [near1], two_calls)
    sent0 = Sent(low, pairs)

    m = Slot(entry(1, 1), True)
    state = ff_slot(m, cots, contrasted(near1, pooled1, 1), small)
    low, small, hidden_grads, grads = heads_slot(m, *state, lambda: [sent0], all_heads)
    sent1 = Sent(low, pairs)

    m = Slot(entry(0, 0), True)
    state = ff_slot(m, sent0.value(), (), small)
    states_out, state = onward([], (states[None, :MICRO, None], state))
    low, small, hidden_grads, grads = heads_slot(m, *state, lambda: [sent1], all_heads)

    m = Slot(entry(1, 0))
    core = (me % 2)[None]
    running = []

    def reduction(chunk):
        running.append(Reduction(core, *chunk))
        return running[-1]

    *state, buffers = ff_slot(m, sent1.value(), (), small)
    chunk_out = weight_out(slot, gelu, buffers[0])
    reduced_out = reduction(chunk_out)
    chunk_wide = weight_wide(slot, xhat1, vec, buffers[1])
    state, buffers = onward(running, (state, buffers))
    reduced_wide = reduction(chunk_wide)
    one_by_one = [(first, 1) for first in range(groups)]
    low, small, hidden_grads, grads = heads_slot(m, *state, buffers, lambda: running, one_by_one)
    inputs = jnp.where(leading, tokens[:, 0], jnp.stack([received0, received1]))
    chunk_attn = weight_attn(slot, inputs, mixed, grads[2])
    reduced_attn = reduction(chunk_attn)
    small = Sum(small)
    running += [small]
    loss = None
    while True:
        if loss is None and not small.moving:
            loss = Swapped(small.value[loss_row : loss_row + 1, :128])
            running.append(loss)
        if not any(item.moving for item in running):
            break
        onward([reduced_attn])
        onward([item for item in running if item is not reduced_attn])

    if fast_ring():
        own_ff_out = reduced_out.value()
        own_ff_in = unblocked(reduced_wide.value().reshape(4, rows_in, D))
        own_attn = reduced_attn.value()
        own_attn_in = unblocked(own_attn[: 3 * rows_in].reshape(3, rows_in, D))
        own_attn_out = own_attn[3 * rows_in :]
    else:

        def natural(chunk, blocks):
            both = jnp.concatenate(chunk).reshape(16, blocks, -1, D)
            return both.transpose(1, 0, 2, 3).reshape(blocks, -1, D)

        attn = natural(chunk_attn, 4)
        whole = [unblocked(attn[:3]), attn[3], unblocked(natural(chunk_wide, 4))]
        whole.append(natural(chunk_out, 1)[0])
        own_attn_in, own_attn_out, own_ff_in, own_ff_out = (
            lax.psum_scatter(grad.astype(f32), "dp", scatter_dimension=0, tiled=True)
            for grad in whole
        )

    contrast_loss = jnp.where(order.token < 0, 0.0, loss.both[0, 0])
    small = small.value
    own_rows = lax.dynamic_slice(small, (0, me * rows_in), (8, rows_in))
    spot = me * rows_out
    own_bias = lax.dynamic_slice(small, (8 + spot // D, spot % D), (1, rows_out))
    return (
        contrast_loss,
        states_out,
        hidden_grads[0][None, :, None],
        own_attn_in[None],
        own_attn_out[None],
        own_ff_in[None],
        own_ff_out[None],
        own_rows[None, :2],
        own_rows[None, 2:],
        own_bias,
    )


def solution(mesh):
    return jax.shard_map(
        local,
        mesh=mesh,
        in_specs=(
            P(None, "dp", None, None),
            P(None, "dp", None, None),
            P(None, "dp", None),
            P(None, "dp"),
            P(),
            P("section", "dp", None),
            P("section", "dp", None),
            P("section", "dp", None),
            P("section", "dp", None),
            P("section", None, "dp"),
            P("section", None, "dp"),
            P("section", "dp"),
        ),
        out_specs=(
            P(),
            P("section", None, "dp", None, None),
            P("section", None, "dp", None, None),
            P("section", "dp", None),
            P("section", "dp", None),
            P("section", "dp", None),
            P("section", "dp", None),
            P("section", None, "dp"),
            P("section", None, "dp"),
            P("section", "dp"),
        ),
        check_vma=False,
    )
```

```python
from functools import partial

import jax
import jax.numpy as jnp
from jax import lax
from jax.experimental import pallas as pl
from jax.experimental.pallas import tpu as pltpu
from jax.sharding import PartitionSpec as P

D = 768
HEADS = 12
HEAD = 64
SEQ = 512
MICRO = 2
FF = 3072

bf16 = jnp.bfloat16
f32 = jnp.float32
highest = lax.Precision.HIGHEST
norm_eps = 1e-05
unit_eps = 1e-06
masked_value = -1000000000.0
contrast_scale = 10.0
vmem_limit = 16 * 2**20
slot_vmem = 36 * 2**20


def params(size=vmem_limit):
    return pltpu.CompilerParams(vmem_limit_bytes=size)


def cost(flops, size, factor=2):
    return pl.CostEstimate(
        flops=int(factor * flops), bytes_accessed=int(factor * size), transcendentals=0
    )


def swapped(value, axis, mask):
    count = lax.axis_size(axis)
    return lax.ppermute(value, axis, [(i, i ^ mask) for i in range(count)])


def ring_order(chips):
    return list(range(0, chips, 2)) + list(range(chips - 1, 0, -2))


def ring_hop(value, backward=False):
    chips = lax.axis_size("dp") // 2
    order = ring_order(chips)
    pairs = []
    for place in range(chips):
        for core in range(2):
            step = 1 if core == 0 else -1
            pairs.append((order[place] * 2 + core, order[(place + step) % chips] * 2 + core))
    return lax.ppermute(value, "dp", pairs)


def ring_place(me):
    chips = lax.axis_size("dp") // 2
    order = ring_order(chips)
    places = [order.index(chip) for chip in range(chips)]
    place = jnp.asarray(places, jnp.int32)[me // 2]
    core = me % 2
    return place, 1 - 2 * core, core


def owners(me, steps, cores):
    chips = lax.axis_size("dp") // 2
    place, way, core = ring_place(me)
    order = jnp.asarray(ring_order(chips), jnp.int32)
    found = order[(place + way * jnp.asarray(steps, jnp.int32)) % chips] * 2
    return found + (core + jnp.asarray(cores, jnp.int32)) % 2


def fast_ring():
    return lax.axis_size("dp") == 16


def gather_owners(me):
    steps = [0, 0, -1, -1, -2, -2, -3, -3, -4, 1, 1, 2, 2, 3, 3, 4]
    cores = [0, 1, 0, 1, 0, 1, 0, 1, 0, 1, 0, 1, 0, 1, 0, 1]
    return owners(me, steps, cores)


def assemble_kernel(counts, owner_ref, *refs):
    pieces, out_ref, sems = refs[: len(counts)], refs[-2], refs[-1]
    rows = pieces[0].shape[2]
    copies = []
    for piece, count in zip(pieces, counts):
        for k in range(count):
            start = pl.multiple_of(owner_ref[len(copies)] * rows, 16)
            copies.append(
                pltpu.make_async_copy(
                    piece.at[k], out_ref.at[:, pl.ds(start, rows), :], sems.at[len(copies)]
                )
            )
    for copy in copies:
        copy.start()
    for copy in copies:
        copy.wait()


def assemble(pieces, owner):
    counts = [piece.shape[0] for piece in pieces]
    total = sum(counts)
    blocks, rows = pieces[0].shape[1:3]
    return pl.pallas_call(
        partial(assemble_kernel, counts),
        out_shape=jax.ShapeDtypeStruct((blocks, total * rows, D), bf16),
        in_specs=[pl.BlockSpec(memory_space=pltpu.SMEM)]
        + [pl.BlockSpec(memory_space=pl.ANY)] * len(pieces),
        out_specs=pl.BlockSpec(memory_space=pltpu.VMEM),
        scratch_shapes=[pltpu.SemaphoreType.DMA((total,))],
        compiler_params=params(),
        cost_estimate=cost(0, 1e7),
        name="assemble",
    )(owner, *[pltpu.with_memory_space_constraint(piece, pltpu.HBM) for piece in pieces])


unit_steps = [1, 1, 2, 2, 3, 3, 4, 0]


def slots(me):
    if not fast_ring():
        return jnp.arange(16, dtype=jnp.int32)
    both = jnp.arange(6, dtype=jnp.int32) % 2
    keep = owners(me, unit_steps, [0] * 8)
    send = owners(me, [-step for step in unit_steps], [1] * 8)
    table = [keep[:6] // 2 * 2 + both, keep[6:], send[:6] // 2 * 2 + both, send[6:]]
    table = jnp.concatenate(table)
    index = jnp.arange(16, dtype=jnp.int32)
    return jnp.sum(jnp.where(table[None, :] == index[:, None], index[None, :], 0), axis=1)


def fold_first_kernel(keep_ref, mate_ref, out_ref, own_ref):
    total = keep_ref[...].astype(f32) + mate_ref[...].astype(f32)
    out_ref[...] = total[:1].astype(bf16)
    own_ref[...] = total[1]


def fold_first(keep, mate):
    rows, width = keep.shape[1:]
    tile = rows // 2
    units = pl.BlockSpec((2, tile, width), lambda i: (3, i, 0))
    return pl.pallas_call(
        fold_first_kernel,
        grid=(2,),
        in_specs=[units, units],
        out_specs=[
            pl.BlockSpec((1, tile, width), lambda i: (0, i, 0)),
            pl.BlockSpec((tile, width), lambda i: (i, 0)),
        ],
        out_shape=[
            jax.ShapeDtypeStruct((1, rows, width), bf16),
            jax.ShapeDtypeStruct((rows, width), f32),
        ],
        compiler_params=params(),
        cost_estimate=cost(0, 0),
        name="fold_first",
    )(keep, mate)


def fold_kernel(one, core_ref, keep_ref, mate_ref, there_ref, out_ref):
    there = there_ref[...].astype(f32)
    if one:
        there = jnp.where(pl.program_id(0) == core_ref[0], there, 0.0)
    total = keep_ref[...].astype(f32) + mate_ref[...].astype(f32) + there
    out_ref[...] = total.astype(bf16)


def fold(core, keep, mate, first, there):
    rows, width = keep.shape[1:]
    one = there.shape[0] == 1
    unit = pl.BlockSpec((1, rows, width), lambda i, _: (first + i, 0, 0))
    out = pl.BlockSpec((1, rows, width), lambda i, _: (i, 0, 0))
    arrived = pl.BlockSpec((1, rows, width), lambda i, _: (0, 0, 0)) if one else out
    return pl.pallas_call(
        partial(fold_kernel, one),
        grid_spec=pltpu.PrefetchScalarGridSpec(
            num_scalar_prefetch=1, grid=(2,), in_specs=[unit, unit, arrived], out_specs=out
        ),
        out_shape=jax.ShapeDtypeStruct((2, rows, width), bf16),
        compiler_params=params(),
        cost_estimate=cost(0, 0),
        name="fold",
    )(core, keep, mate, there)


class Reduction:
    def __init__(self, core, keep, send):
        self.core, self.keep, self.send = core, keep, send
        self.moving = [swapped(send, "dp", 1)] if fast_ring() else []
        self.stage = 0

    def step(self):
        arrived = self.moving[0]
        if self.stage == 0:
            self.mate = arrived
            first, self.own = fold_first(self.keep, self.mate)
            self.moving = [ring_hop(first)]
        elif self.stage < 4:
            first = 6 - 2 * self.stage
            self.moving = [ring_hop(fold(self.core, self.keep, self.mate, first, arrived))]
        elif self.stage == 4:
            self.near = arrived
            self.moving = [swapped(self.near, "dp", 1)]
        else:
            self.last = arrived
            self.moving = []
        self.stage += 1

    def value(self):
        def mine(pair):
            return lax.dynamic_index_in_dim(pair, self.core[0], 0, keepdims=False).astype(f32)

        return self.own + mine(self.near) + mine(self.last)


class Sent:
    def __init__(self, value, pairs):
        self.moving = [lax.ppermute(value, "section", pairs)]

    def step(self):
        self.arrived = self.moving[0]
        self.moving = []

    def value(self):
        return self.arrived


class Near:
    def __init__(self, value):
        self.value, self.mask = value, lax.axis_size("dp") // 2
        self.send()

    def send(self):
        self.moving = [swapped(self.value, "dp", self.mask)] if self.mask else []

    def step(self):
        self.value = jnp.concatenate([self.value, self.moving[0]])
        self.mask //= 2
        self.send()


class Sum:
    def __init__(self, value):
        self.value, self.mask = value, lax.axis_size("dp") // 2
        self.send()

    def send(self):
        self.moving = [swapped(self.value, "dp", self.mask)] if self.mask else []

    def step(self):
        self.value = self.value + self.moving[0]
        self.mask //= 2
        self.send()


class Swapped:
    def __init__(self, value):
        self.own, self.moving = value, [swapped(value, "section", 1)]

    def step(self):
        self.both = self.own + self.moving[0]
        self.moving = []


class Gather:
    def __init__(self, shard):
        self.pieces, self.mates = [shard], []
        self.moving = [swapped(shard, "dp", 1)]
        self.stage = 0

    def step(self):
        if self.stage == 0:
            self.pieces = [jnp.stack([self.pieces[0], self.moving[0]])]
            self.moving = [ring_hop(self.pieces[0])]
        elif self.stage < 5:
            self.pieces.append(self.moving[0])
            self.mates += self.moving[1:]
            self.moving = [swapped(self.pieces[-1], "dp", 1)]
            if self.stage < 4:
                last = self.pieces[-1] if self.stage < 3 else self.pieces[-1][:1]
                self.moving = [ring_hop(last)] + self.moving
        else:
            self.mates += self.moving
            self.moving = []
        self.stage += 1

    def all(self):
        return self.pieces + self.mates


class Order:
    def __init__(self, start):
        self.token = start

    def onward(self, items, values=()):
        for item in items:
            if item.moving:
                item.moving, self.token = lax.optimization_barrier((item.moving, self.token))
                item.step()
        values, self.token = lax.optimization_barrier((values, self.token))
        return values


def tie(values, *others):
    return lax.optimization_barrier((values, others))[0]


def add_up(value, axis):
    mask = 1
    while mask < lax.axis_size(axis):
        value = value + swapped(value, axis, mask)
        mask *= 2
    return value


def mm(a, b):
    return lax.dot_general(a, b, (((1,), (0,)), ((), ())), preferred_element_type=f32)


def mm_nt(a, b):
    return lax.dot_general(a, b, (((1,), (1,)), ((), ())), preferred_element_type=f32)


def mm_tn(a, b):
    return lax.dot_general(a, b, (((0,), (0,)), ((), ())), preferred_element_type=f32)


def full(shape):
    return pl.BlockSpec(shape, lambda i, *_: (0,) * len(shape))


def sds(shape, dtype):
    return jax.ShapeDtypeStruct(shape, dtype)


def far(shape, dtype):
    return pltpu.HBM(shape, dtype)


group = 256
groups = D // group
product = 2 * SEQ * D * D
token_block = (SEQ, D)
table_rows = 12
loss_row = 12
entries = MICRO + 1
everything = pl.BlockSpec(memory_space=pl.ANY)


def far(shape, dtype):
    return pltpu.HBM(shape, dtype)


def tokens_buffer(width, dtype):
    return far((entries, SEQ, width), dtype)


def busy(i, m):
    return jnp.where(m[0] < MICRO, i, 0)


def at_entry(block, *where):
    place = where[0] if where else (lambda i: (0,) * len(block))
    return pl.BlockSpec((None, *block), lambda i, m: (m[0], *place(busy(i, m))))


def at_micro(block):
    return pl.BlockSpec((None, *block), lambda i, m: (jnp.minimum(m[0], MICRO - 1),) + (0,) * len(block))


def column_sum(value):
    return jnp.sum(value, axis=0, keepdims=True)


class Slot:
    def __init__(self, entry, ahead=False):
        self.entry, self.ahead = entry, ahead


def in_place(value):
    if value.ndim > 2 and value.shape[0] in (MICRO, entries):
        return pltpu.with_memory_space_constraint(value, pltpu.HBM)
    return value


def slot_call(kernel, m, grid, ins, in_specs, outs, out_specs, before, scratch, size, name, kept=None):
    first = len(outs) - len(before)
    aliases = {1 + len(ins) + n: first + n for n in range(len(before))}
    if kept is not None:
        aliases[1 + kept[0]] = kept[1]
    return pl.pallas_call(
        kernel,
        grid_spec=pltpu.PrefetchScalarGridSpec(
            num_scalar_prefetch=1,
            grid=(grid,),
            in_specs=in_specs + [everything] * len(before),
            out_specs=out_specs,
            scratch_shapes=scratch,
        ),
        out_shape=outs,
        input_output_aliases=aliases,
        compiler_params=params(slot_vmem),
        cost_estimate=cost(0, 0) if m.ahead else cost(size * product, 3e7, 10 if "back" in name else 2),
        name=name,
    )(m.entry, *[in_place(value) for value in ins], *[in_place(value) for value in before])


def attend_kernel(first, n_before, m_ref, *refs):
    x_ref, wq_ref, wk_ref, wv_ref, vec_ref, seg_col_ref, seg_row_ref, *refs = refs
    q_ref, k_ref, v_ref, mixed_ref, lse_ref, mask_ref = refs[n_before:]
    i = pl.program_id(0)

    @pl.when(m_ref[0] < MICRO)
    def _():
        @pl.when(i == 0)
        def _():
            mask_ref[...] = jnp.where(seg_col_ref[...] == seg_row_ref[...], 0.0, masked_value)

        lanes = pl.ds(pl.multiple_of((first + i) * group, group), group)
        x = x_ref[...]
        q = (mm(x, wq_ref[...]) + vec_ref[2:3, lanes]).astype(bf16)
        k = mm(x, wk_ref[...]).astype(bf16)
        v = (mm(x, wv_ref[...]) + vec_ref[3:4, lanes]).astype(bf16)
        q_ref[...] = q
        k_ref[...] = k
        v_ref[...] = v
        scaled = q * jnp.asarray(HEAD**-0.5, bf16)
        outs, lses = [], []
        for h in range(group // HEAD):
            c = slice(h * HEAD, (h + 1) * HEAD)
            scores = mm_nt(scaled[:, c], k[:, c]) + mask_ref[...]
            top = jnp.max(scores, axis=1, keepdims=True)
            raw = jnp.exp(scores - top)
            total = jnp.sum(raw, axis=1, keepdims=True)
            outs.append(mm(raw.astype(bf16), v[:, c]) / total)
            lses.append(top + jnp.log(total))
        mixed_ref[...] = jnp.concatenate(outs, axis=1).astype(bf16)
        lses = jnp.concatenate(lses + [jnp.zeros((SEQ, 128 - len(lses)), f32)], axis=1)
        lse_ref[...] = jnp.transpose(lses)[:8]


vec_spec = full((table_rows, D))


def attend(m, x, w_in, vec, seg_col, seg_row, before, first=0, count=groups):
    def weight(b):
        return pl.BlockSpec((None, D, group), lambda i, m: (b, 0, first + busy(i, m)))

    heads = at_entry((SEQ, group), lambda i: (0, first + i))
    return slot_call(
        partial(attend_kernel, first, len(before)),
        m,
        count,
        [x, w_in, w_in, w_in, vec, seg_col, seg_row],
        [full(token_block)]
        + [weight(b) for b in range(3)]
        + [vec_spec, at_entry((SEQ, 1)), at_entry((1, SEQ))],
        [tokens_buffer(D, bf16)] * 4 + [far((entries, groups, 8, SEQ), f32)],
        [heads] * 4 + [at_entry((None, 8, SEQ), lambda i: (first + i, 0, 0))],
        before,
        [pltpu.VMEM((SEQ, SEQ), f32)],
        2 * count,
        "attend",
    )


def normalize(hidden):
    centered = hidden - jnp.mean(hidden, axis=1, keepdims=True)
    variance = jnp.mean(centered * centered, axis=1, keepdims=True)
    rstd = lax.rsqrt(variance + norm_eps)
    return centered * rstd, rstd


def gelu_both(x):
    cdf = 0.5 + 0.5 * lax.erf(x * 0.7071067811865476)
    return x * cdf, cdf + x * (jnp.exp(x * x * -0.5) * 0.3989422804014327)


def forward_kernel(last, n_before, m_ref, mixed_ref, x_ref, wo_ref, wi_ref, wf_ref, vec_ref, *refs):
    seg_row_ref, *refs = refs
    refs = refs[n_before:]
    if last:
        pooled_ref, unit_ref, *refs = refs
    else:
        out_ref, *refs = refs
    xhat1_ref, rstd1_ref, gelu_ref, dgelu_ref, state_ref, xhat2_ref, rstd2_ref, *refs = refs
    normed_ref, acc_ref = refs
    i = pl.program_id(0)

    @pl.when(m_ref[0] < MICRO)
    def _():
        @pl.when(i == 0)
        def _():
            attended = mm(mixed_ref[...], wo_ref[...]) + vec_ref[4:5, :]
            xhat, rstd = normalize(x_ref[...].astype(f32) + attended)
            xhat1_ref[...] = xhat.astype(bf16)
            rstd1_ref[...] = rstd
            normed = xhat * vec_ref[0:1, :] + vec_ref[5:6, :]
            normed_ref[...] = normed.astype(bf16)
            acc_ref[...] = normed + vec_ref[6:7, :]

        pre_act = mm(normed_ref[...], wi_ref[...]) + vec_ref[pl.ds(8 + i, 1), :]
        value, slope = gelu_both(pre_act)
        value = value.astype(bf16)
        gelu_ref[...] = value
        dgelu_ref[...] = slope.astype(bf16)
        acc_ref[...] += mm(value, wf_ref[...])

        @pl.when(i == pl.num_programs(0) - 1)
        def _():
            xhat, rstd = normalize(acc_ref[...])
            xhat2_ref[...] = xhat.astype(bf16)
            rstd2_ref[...] = rstd
            out = xhat * vec_ref[1:2, :] + vec_ref[7:8, :]
            state_ref[...] = out.astype(bf16)
            if not last:
                out_ref[...] = out.astype(bf16)
            else:
                member = seg_row_ref[...] == lax.broadcasted_iota(jnp.int32, (8, SEQ), 0)
                count = jnp.sum(member.astype(f32), axis=1, keepdims=True)
                member = member.astype(bf16)
                high = out.astype(bf16)
                rest = out - high.astype(f32)
                middle = rest.astype(bf16)
                low = (rest - middle.astype(f32)).astype(bf16)
                pooled = mm(member, high) + mm(member, middle) + mm(member, low)
                pooled = pooled / jnp.maximum(count, 1.0)
                pooled_ref[...] = pooled
                norm = jnp.sum(pooled * pooled, axis=1, keepdims=True) + unit_eps
                unit_ref[...] = pooled * lax.rsqrt(norm)

    if last:

        @pl.when(m_ref[0] >= MICRO)
        def _():
            pooled_ref[...] = jnp.zeros((8, D), f32)
            unit_ref[...] = jnp.zeros((8, D), f32)


def forward(m, mixed, x, w_wide, w_narrow, vec, seg_row, last, before):
    part = at_entry(token_block, lambda i: (0, i))
    now = [sds((8, D), f32)] * 2 if last else [sds(token_block, bf16)]
    row = sds((entries, SEQ, 1), f32)
    outs = now + [tokens_buffer(D, bf16), row] + [tokens_buffer(FF, bf16)] * 2
    outs += [tokens_buffer(D, bf16), tokens_buffer(D, bf16), row]
    return slot_call(
        partial(forward_kernel, last, len(before)),
        m,
        FF // D,
        [mixed, x, w_wide, w_wide, w_narrow, vec, seg_row],
        [
            at_entry(token_block),
            full(token_block),
            pl.BlockSpec((None, D, D), lambda i, m: (0, 0, 0)),
            pl.BlockSpec((None, D, D), lambda i, m: (1 + busy(i, m), 0, 0)),
            pl.BlockSpec((None, D, D), lambda i, m: (0, busy(i, m), 0)),
            vec_spec,
            at_entry((1, SEQ)),
        ],
        outs,
        [full(out.shape) for out in now]
        + [at_entry(token_block), at_entry((SEQ, 1)), part, part]
        + [at_entry(token_block), at_entry(token_block), at_entry((SEQ, 1))],
        before,
        [pltpu.VMEM(token_block, bf16), pltpu.VMEM(token_block, f32)],
        9,
        "forward",
    )


def contrast_kernel(me_ref, table_ref, pooled_ref, groups_ref, partner_ref, seg_row_ref, *refs, micro, total):
    loss_ref, gseg_ref = refs
    me = me_ref[0]
    dot = partial(lax.dot_general, precision=highest, preferred_element_type=f32)
    rows_nt = (((1,), (1,)), ((), ()))
    table = table_ref[...].reshape(-1, D)
    count = table.shape[0]
    devices = count // 8
    every = groups_ref.shape[1]
    segs = every // devices

    def sentence(shape, axis):
        index = lax.broadcasted_iota(jnp.int32, shape, axis)
        block, place = index >> 3, index & 7
        owner = jnp.zeros_like(block)
        far_one = devices // 2
        bit = 0
        while far_one >= 1:
            owner = owner | ((block >> bit) & 1) * far_one
            bit += 1
            far_one //= 2
        return jnp.where(place < segs, (owner ^ me) * segs + place, -1)

    ids_row, ids_col = sentence((1, count), 1), sentence((count, 1), 0)
    ids = groups_ref[micro : micro + 1, :].astype(f32)
    ids = jnp.broadcast_to(ids, (8, every))
    hot_row = (lax.broadcasted_iota(jnp.int32, (every, 1), 0) == ids_row).astype(f32)
    hot_col = (lax.broadcasted_iota(jnp.int32, (1, every), 1) == ids_col).astype(f32)
    groups_row = dot(ids, hot_row, (((1,), (0,)), ((), ())))[0:1]
    groups_col = dot(hot_col, ids, rows_nt)[:, 0:1]
    logits = contrast_scale * dot(table, table, rows_nt)
    real = (ids_row >= 0) & (ids_col >= 0)
    allowed = real & (groups_col == groups_row) & (ids_col != ids_row)
    masked = jnp.where(allowed, logits, masked_value)
    top = jnp.max(masked, axis=0, keepdims=True)
    lse_row = top + jnp.log(column_sum(jnp.exp(masked - top)))
    mine = masked[:8]
    top = jnp.max(mine, axis=1, keepdims=True)
    raw = jnp.exp(mine - top)
    raw_total = jnp.sum(raw, axis=1, keepdims=True)
    across = jnp.exp(mine - lse_row)
    place = lax.broadcasted_iota(jnp.int32, (8, 1), 0)
    partner = jnp.zeros((8, 1), jnp.int32)
    for s in range(segs):
        partner = jnp.where(place == s, partner_ref[micro, s], partner)
    chosen = ((partner == ids_row) & (place < segs)).astype(f32)
    terms = top + jnp.log(raw_total) - jnp.sum(chosen * logits[:8], axis=1, keepdims=True)
    loss = column_sum(jnp.where(place < segs, terms, 0.0)) / total
    loss_ref[...] = jnp.broadcast_to(loss, (1, D))
    grad = raw / raw_total + across - 2.0 * chosen
    grad = contrast_scale * dot(grad, table, (((1,), (0,)), ((), ())))
    pooled = pooled_ref[...]
    scale = lax.rsqrt(jnp.sum(pooled * pooled, axis=1, keepdims=True) + unit_eps)
    dots = jnp.sum(grad * pooled, axis=1, keepdims=True)
    grad = scale * grad - pooled * (scale * scale * scale * dots)
    member = (seg_row_ref[...] == lax.broadcasted_iota(jnp.int32, (8, SEQ), 0)).astype(f32)
    gseg_ref[...] = grad / jnp.maximum(jnp.sum(member, axis=1, keepdims=True), 1.0)


def contrast(me, table, pooled, group_ids, partner, seg_row, micro, total):
    smem = pl.BlockSpec(memory_space=pltpu.SMEM)
    return pl.pallas_call(
        partial(contrast_kernel, micro=micro, total=total),
        grid=(1,),
        out_shape=[sds((1, D), f32), sds((8, D), f32)],
        in_specs=[
            smem,
            full(table.shape),
            full((8, D)),
            full(group_ids.shape),
            smem,
            pl.BlockSpec((None, 1, SEQ), lambda i: (micro, 0, 0)),
        ],
        out_specs=[full((1, D)), full((8, D))],
        compiler_params=params(slot_vmem),
        name="contrast",
    )(me, table, pooled, group_ids, partner, seg_row)


def norm_back(grad, xhat, rstd, gain):
    scaled = grad * gain
    mean = jnp.mean(scaled, axis=1, keepdims=True)
    along = jnp.mean(scaled * xhat, axis=1, keepdims=True)
    return rstd * (scaled - mean - xhat * along)


def ff_back_kernel(last, n_before, m_ref, cot_ref, *refs):
    if last:
        seg_col_ref, gseg_ref, loss_ref, *refs = refs
    xhat2_ref, rstd2_ref, vec_ref, wf_ref, dgelu_ref, wi_ref, xhat1_ref, rstd1_ref, *refs = refs
    wo_ref, small_in_ref, *refs = refs
    ghid_ref, gmixed_ref, small_ref, gbranch_ref, gpre_ref, gatt_ref, acc_ref = refs[n_before:]
    i = pl.program_id(0)

    @pl.when(i == 0)
    def _():
        small_ref[...] = small_in_ref[...]

    @pl.when(m_ref[0] < MICRO)
    def _():
        @pl.when(i == 0)
        def _():
            grad = cot_ref[...].astype(f32)
            if last:
                for s in range(4):
                    grad = grad + jnp.where(seg_col_ref[...] == s, gseg_ref[s : s + 1, :], 0.0)
            xhat = xhat2_ref[...].astype(f32)
            grad_sum = norm_back(grad, xhat, rstd2_ref[...], vec_ref[1:2, :])
            acc_ref[...] = grad_sum
            low = grad_sum.astype(bf16)
            gbranch_ref[...] = low
            if last:
                small_ref[loss_row : loss_row + 1, :] += loss_ref[...]
            small_ref[1:2, :] += column_sum(grad * xhat)
            small_ref[6:7, :] += column_sum(low.astype(f32))
            small_ref[7:8, :] += column_sum(grad)

        grad_gelu = mm_nt(gbranch_ref[...], wf_ref[...])
        grad_pre = (grad_gelu * dgelu_ref[...].astype(f32)).astype(bf16)
        gpre_ref[...] = grad_pre
        small_ref[pl.ds(8 + i, 1), :] += column_sum(grad_pre.astype(f32))
        acc_ref[...] += mm_nt(grad_pre, wi_ref[...])

        @pl.when(i == pl.num_programs(0) - 1)
        def _():
            grad = acc_ref[...]
            xhat = xhat1_ref[...].astype(f32)
            grad_hidden = norm_back(grad, xhat, rstd1_ref[...], vec_ref[0:1, :])
            ghid_ref[...] = grad_hidden
            low = grad_hidden.astype(bf16)
            gatt_ref[...] = low
            gmixed_ref[...] = mm_nt(low, wo_ref[...]).astype(bf16)
            small_ref[0:1, :] += column_sum(grad * xhat)
            small_ref[4:5, :] += column_sum(low.astype(f32))
            small_ref[5:6, :] += column_sum(grad)


def ff_back(m, cot, segs, xhat2, rstd2, vec, w_narrow, dgelu, w_wide, xhat1, rstd1, small, before):
    last = len(segs) > 0
    part = at_entry(token_block, lambda i: (0, i))
    return slot_call(
        partial(ff_back_kernel, last, len(before)),
        m,
        FF // D,
        [cot, *segs, xhat2, rstd2, vec, w_narrow, dgelu, w_wide, xhat1, rstd1, w_wide, small],
        (
            [at_micro(token_block), at_entry((SEQ, 1)), full((8, D)), full((1, D))]
            if last
            else [full(token_block)]
        )
        + [
            at_entry(token_block),
            at_entry((SEQ, 1)),
            vec_spec,
            pl.BlockSpec((None, D, D), lambda i, m: (0, busy(i, m), 0)),
            part,
            pl.BlockSpec((None, D, D), lambda i, m: (1 + busy(i, m), 0, 0)),
            at_entry(token_block),
            at_entry((SEQ, 1)),
            pl.BlockSpec((None, D, D), lambda i, m: (0, 0, 0)),
            full((16, D)),
        ],
        [sds(token_block, f32), sds(token_block, bf16), sds((16, D), f32)]
        + [tokens_buffer(D, bf16), tokens_buffer(FF, bf16), far((entries, 4, SEQ, D), bf16)],
        [full(token_block), full(token_block), full((16, D))]
        + [at_entry(token_block), part, at_entry((None, SEQ, D), lambda i: (3, 0, 0))],
        before,
        [pltpu.VMEM(token_block, f32)],
        12,
        "ff_back",
    )


def attend_back_kernel(first, n_total, n_before, m_ref, *refs):
    q_ref, k_ref, v_ref, gm_ref, lse_ref, wq_ref, wk_ref, wv_ref, *refs = refs
    totals, refs = refs[:n_total], refs[n_total:]
    seg_col_ref, seg_row_ref, small_in_ref, *refs = refs
    low_ref, small_ref, gx_ref, gqkv_ref, mask_ref = refs[n_before:]
    i = pl.program_id(0)
    active = m_ref[0] < MICRO

    @pl.when(i == 0)
    def _():
        small_ref[...] = small_in_ref[...]

    @pl.when((i == 0) & active)
    def _():
        mask_ref[...] = jnp.where(seg_col_ref[...] == seg_row_ref[...], 0.0, masked_value)
        gx_ref[...] = totals[0][...]

    @pl.when((i == 0) & jnp.logical_not(active))
    def _():
        gx_ref[...] = totals[-1][...]

    @pl.when(active)
    def _():
        q, k, v, gm = q_ref[...], k_ref[...], v_ref[...], gm_ref[...]
        scaled = q * jnp.asarray(HEAD**-0.5, bf16)
        lse = lse_ref[...]
        parts = [[], [], []]
        for h in range(group // HEAD):
            c = slice(h * HEAD, (h + 1) * HEAD)
            probs = jnp.exp(mm_nt(k[:, c], scaled[:, c]) + mask_ref[...] - lse[h : h + 1, :])
            grad_probs = mm_nt(v[:, c], gm[:, c])
            parts[2].append(mm(probs.astype(bf16), gm[:, c]))
            dots = column_sum(grad_probs * probs)
            grad_scores = (probs * (grad_probs - dots)).astype(bf16)
            parts[1].append(mm(grad_scores, scaled[:, c]))
            parts[0].append(mm_tn(grad_scores, k[:, c]) * HEAD**-0.5)
        grads = [jnp.concatenate(part, axis=1).astype(bf16) for part in parts]
        for b, grad in enumerate(grads):
            gqkv_ref[b] = grad
        lanes = pl.ds(pl.multiple_of((first + i) * group, group), group)
        small_ref[2:3, lanes] += column_sum(grads[0].astype(f32))
        small_ref[3:4, lanes] += column_sum(grads[2].astype(f32))
        gx_ref[...] += (
            mm_nt(grads[0], wq_ref[...]) + mm_nt(grads[1], wk_ref[...]) + mm_nt(grads[2], wv_ref[...])
        )

        @pl.when(i == pl.num_programs(0) - 1)
        def _():
            low_ref[...] = gx_ref[...].astype(bf16)


def attend_back(m, q, k, v, gm, lse, w_in, totals, seg_col, seg_row, small, first, count, before):
    def weight(b):
        return pl.BlockSpec((None, D, group), lambda i, m: (b, 0, first + busy(i, m)))

    heads = at_entry((SEQ, group), lambda i: (0, first + i))
    buffer = at_micro(token_block)
    total_specs = [buffer] if first else [full(token_block), buffer][: len(totals)]
    return slot_call(
        partial(attend_back_kernel, first, len(totals), len(before)),
        m,
        count,
        [q, k, v, gm, lse, w_in, w_in, w_in, *totals, seg_col, seg_row, small],
        [heads] * 3
        + [pl.BlockSpec((SEQ, group), lambda i, m: (0, first + busy(i, m)))]
        + [at_entry((None, 8, SEQ), lambda i: (first + i, 0, 0))]
        + [weight(b) for b in range(3)]
        + total_specs
        + [at_entry((SEQ, 1)), at_entry((1, SEQ)), full((16, D))],
        [sds(token_block, bf16), sds((16, D), f32)]
        + [far((MICRO, SEQ, D), f32), far((entries, 4, SEQ, D), bf16)],
        [full(token_block), full((16, D)), buffer]
        + [at_entry((3, SEQ, group), lambda i: (0, 0, first + i))],
        before,
        [pltpu.VMEM((SEQ, SEQ), f32)],
        6 * count,
        "attend_back",
        (7 + len(totals), 2) if first or len(totals) > 1 else None,
    )


def put(slot, keep_ref, send_ref, index, value):
    @pl.when(slot < 8)
    def _():
        keep_ref[(slot,) + index] = value

    @pl.when(slot >= 8)
    def _():
        send_ref[(slot - 8,) + index] = value


def weight_call(kernel, slot, ins, in_specs, scratch, name):
    outs = [sds((8, FF // 16, D), bf16)] * 2
    return pl.pallas_call(
        kernel,
        grid_spec=pltpu.PrefetchScalarGridSpec(
            num_scalar_prefetch=1,
            grid=(4,),
            in_specs=in_specs,
            out_specs=[full(out.shape) for out in outs],
            scratch_shapes=scratch,
        ),
        out_shape=outs,
        compiler_params=params(),
        cost_estimate=cost(8 * product, 3e7, 10),
        name=name,
    )(slot, *[in_place(value) for value in ins])


def weight_out_kernel(slot_ref, gelu_ref, gbranch_ref, keep_ref, send_ref):
    i = pl.program_id(0)
    rows = FF // 16
    total = sum(mm_tn(gelu_ref[m], gbranch_ref[m]) for m in range(MICRO)).astype(bf16)
    for j in range(4):
        put(slot_ref[4 * i + j], keep_ref, send_ref, (), total[j * rows : (j + 1) * rows])


def weight_wide_kernel(slot_ref, xhat_ref, vec_ref, gpre_ref, keep_ref, send_ref, normed_ref):
    i = pl.program_id(0)
    rows = D // 16

    @pl.when(i == 0)
    def _():
        for m in range(MICRO):
            normed = (xhat_ref[m].astype(f32) * vec_ref[0:1, :] + vec_ref[5:6, :]).astype(bf16)
            normed_ref[:, m * SEQ : (m + 1) * SEQ] = jnp.transpose(normed)

    total = mm(normed_ref[...], gpre_ref[...].reshape(MICRO * SEQ, D)).astype(bf16)
    row = pl.multiple_of(rows * i, 16)
    for d in range(16):
        put(slot_ref[d], keep_ref, send_ref, (pl.ds(row, rows),), total[d * rows : (d + 1) * rows])


def weight_attn_kernel(slot_ref, x_ref, mixed_ref, grad_ref, keep_ref, send_ref, left_ref):
    i = pl.program_id(0)
    rows = D // 16

    def turn(ref):
        for m in range(MICRO):
            left_ref[:, m * SEQ : (m + 1) * SEQ] = jnp.transpose(ref[m])

    @pl.when(i == 0)
    def _():
        turn(x_ref)

    @pl.when(i == 3)
    def _():
        turn(mixed_ref)

    total = mm(left_ref[...], grad_ref[...].reshape(MICRO * SEQ, D)).astype(bf16)
    row = pl.multiple_of(rows * i, 16)
    for d in range(16):
        put(slot_ref[d], keep_ref, send_ref, (pl.ds(row, rows),), total[d * rows : (d + 1) * rows])


both_blocks = (MICRO, SEQ, D)
both_parts = pl.BlockSpec(both_blocks, lambda i, _: (0, 0, i))


def weight_out(slot, gelu, gbranch):
    specs = [both_parts, full(both_blocks)]
    return weight_call(weight_out_kernel, slot, [gelu, gbranch], specs, [], "weight_out")


def weight_wide(slot, xhat1, vec, gpre):
    specs = [full(both_blocks), vec_spec, both_parts]
    scratch = [pltpu.VMEM((D, MICRO * SEQ), bf16)]
    return weight_call(weight_wide_kernel, slot, [xhat1, vec, gpre], specs, scratch, "weight_wide")


def weight_attn(slot, x, mixed, grads):
    grad_spec = pl.BlockSpec((MICRO, None, SEQ, D), lambda i, _: (0, i, 0, 0))
    specs = [full(both_blocks), full(both_blocks), grad_spec]
    scratch = [pltpu.VMEM((D, MICRO * SEQ), bf16)]
    return weight_call(weight_attn_kernel, slot, [x, mixed, grads], specs, scratch, "weight_attn")


def blocked(shard):
    rows, columns = shard.shape
    return shard.reshape(rows, columns // D, D).transpose(1, 0, 2)


def unblocked(shard):
    blocks, rows, columns = shard.shape
    return shard.transpose(1, 0, 2).reshape(rows, blocks * columns)


def gather_plain(shard):
    return blocked(lax.all_gather(shard.astype(bf16), "dp", axis=0, tiled=True))


def local(
    tokens,
    out_cotangent,
    lengths,
    partner,
    group_ids,
    attn_in,
    attn_out,
    ff_in,
    ff_out,
    norm_gains,
    biases,
    ff_bias,
):
    section = lax.axis_index("section").astype(jnp.int32)
    me = lax.axis_index("dp").astype(jnp.int32)
    leading = section == 0
    n_dp = lax.axis_size("dp")
    rows_in = D // n_dp
    rows_out = FF // n_dp
    segs = lengths.shape[-1]

    vectors = jnp.concatenate(
        [norm_gains[0].reshape(-1), biases[0].reshape(-1), ff_bias[0].reshape(-1)]
    ).astype(bf16)

    def vector_table(every):
        rows = every[:, : 8 * rows_in].reshape(n_dp, 8, rows_in).transpose(1, 0, 2).reshape(8, D)
        return jnp.concatenate([rows, every[:, 8 * rows_in :].reshape(4, D)]).astype(f32)

    spare = jnp.int32(MICRO)

    def entry(micro, layer):
        return jnp.where(section == layer, jnp.int32(micro), spare)[None]

    def segment_forms(lengths):
        row_ends = jnp.cumsum(lengths[:, 0], axis=-1, dtype=jnp.int32)
        places = jnp.arange(SEQ, dtype=jnp.int32)
        segment = jnp.sum((places[None, :, None] >= row_ends[:, None, :]).astype(jnp.int32), axis=-1)
        segment = jnp.concatenate([segment, segment[:1]])
        return segment[:, :, None], segment[:, None, :]

    order = Order(lengths[0, 0, 0])
    onward = order.onward

    first = Slot(entry(0, 0))
    x = tokens[0, 0]
    if fast_ring():
        in_gather = Gather(blocked(attn_in[0].astype(bf16)))
        table = jnp.pad(vectors[None], ((0, 15), (0, D - vectors.shape[0])))
        vec_gather = Gather(table[None])
        onward([in_gather, vec_gather])
        onward([in_gather, vec_gather])
        late = tie((attn_out, ff_in, ff_out, lengths, me), in_gather.pieces[1])
        wide_shard = [late[0][0].astype(bf16)[None], blocked(late[1][0].astype(bf16))]
        wide_gather = Gather(jnp.concatenate(wide_shard))
        seg_col, seg_row = segment_forms(late[3])
        owner, slot = gather_owners(late[4]), slots(late[4])
        onward([in_gather, vec_gather])
        onward([wide_gather])
        onward([in_gather, vec_gather])
        narrow_gather = Gather(tie(late[2], in_gather.pieces[3])[0].astype(bf16)[None])
        onward([in_gather, vec_gather])
        onward([wide_gather])
        onward([narrow_gather])
        onward([in_gather, vec_gather])
        vec = assemble(vec_gather.all(), owner).reshape(n_dp, 16, D)
        vec = vector_table(vec[:, 0, : vectors.shape[0]])
        w_in = assemble(in_gather.all(), owner)
        heads = attend(first, x, w_in, vec, seg_col, seg_row, [])
        heads = onward([wide_gather, narrow_gather], heads)
        onward([wide_gather, narrow_gather])
        onward([wide_gather])
        onward([narrow_gather])
        onward([wide_gather])
        w_wide = assemble(wide_gather.all(), owner)
        onward([narrow_gather])
        onward([narrow_gather])
        w_narrow = assemble(narrow_gather.all(), owner)
    else:
        w_in = gather_plain(attn_in[0])
        w_wide = jnp.concatenate([gather_plain(attn_out[0]), gather_plain(ff_in[0])])
        w_narrow = gather_plain(ff_out[0])
        vec = vector_table(lax.all_gather(vectors, "dp"))
        seg_col, seg_row = segment_forms(lengths)
        slot = slots(me)
        heads = attend(first, x, w_in, vec, seg_col, seg_row, [])
    out, *stored = forward(first, heads[3], x, w_wide, w_narrow, vec, seg_row, False, [])
    pairs = [(0, 1)]
    sent0 = Sent(out, pairs)

    second = Slot(entry(1, 0), True)
    x = tokens[1, 0]
    heads = attend(second, x, w_in, vec, seg_col, seg_row, heads)
    out, *stored = forward(second, heads[3], x, w_wide, w_narrow, vec, seg_row, False, stored)
    heads, stored, out = onward([sent0], (heads, stored, out))
    sent1 = Sent(out, pairs)

    third = Slot(entry(0, 1), True)
    x = received0 = sent0.value()
    heads = attend(third, x, w_in, vec, seg_col, seg_row, heads)
    pooled0, unit0, *stored = forward(
        third, heads[3], x, w_wide, w_narrow, vec, seg_row, True, stored
    )
    near0 = Near(unit0)
    heads, stored = onward([sent1], (heads, stored))

    fourth = Slot(entry(1, 1))
    x = received1 = sent1.value()
    heads = attend(fourth, x, w_in, vec, seg_col, seg_row, heads)
    heads = onward([near0], heads)
    pooled1, unit1, *stored = forward(
        fourth, heads[3], x, w_wide, w_narrow, vec, seg_row, True, stored
    )
    q, k, v, mixed, lse = heads
    xhat1, rstd1, gelu, dgelu, states, xhat2, rstd2 = stored

    total = MICRO * n_dp * segs

    def contrasted(near, pooled, micro):
        while near.moving:
            onward([near])
        table = near.value.reshape(-1, D)
        loss, grad_segs = contrast(
            me[None], table, pooled, group_ids, partner, seg_row, micro, total
        )
        return seg_col, grad_segs, loss

    near1 = Near(unit1)
    segs0 = contrasted(near0, pooled0, 0)

    cots = out_cotangent[:, 0]
    grads = []
    hidden_grads = []
    small = jnp.zeros((16, D), f32)

    def ff_slot(m, cot, segs_in, small):
        grad_hidden, grad_mixed, small, *buffers = ff_back(
            m, cot, segs_in, xhat2, rstd2, vec, w_narrow, dgelu, w_wide, xhat1, rstd1, small, grads
        )
        return grad_hidden, grad_mixed, small, buffers

    def heads_slot(m, grad_hidden, grad_mixed, small, buffers, items, calls):
        total, all_grads = grad_hidden, buffers[2]
        for first, count in calls:
            low, small, total, all_grads = attend_back(
                m,
                *(q, k, v, grad_mixed, lse, w_in),
                [total] if first else [total] + hidden_grads,
                *(seg_col, seg_row, small, first, count, [all_grads]),
            )
            total, all_grads, low, small = onward(items(), (total, all_grads, low, small))
        return low, small, [total], [buffers[0], buffers[1], all_grads]

    all_heads = ((0, groups),)
    pairs = [(1, 0)]
    m = Slot(entry(0, 1))
    state = ff_slot(m, cots, segs0, small)
    state = onward([near1], state)
    low, small, hidden_grads, grads = heads_slot(m, *state, lambda: [near1], all_heads)
    sent0 = Sent(low, pairs)

    m = Slot(entry(1, 1), True)
    state = ff_slot(m, cots, contrasted(near1, pooled1, 1), small)
    low, small, hidden_grads, grads = heads_slot(m, *state, lambda: [sent0], all_heads)
    sent1 = Sent(low, pairs)

    m = Slot(entry(0, 0), True)
    state = ff_slot(m, sent0.value(), (), small)
    states_out, state = onward([], (states[None, :MICRO, None], state))
    low, small, hidden_grads, grads = heads_slot(m, *state, lambda: [sent1], all_heads)

    m = Slot(entry(1, 0))
    core = (me % 2)[None]
    running = []

    def reduction(chunk):
        running.append(Reduction(core, *chunk))
        return running[-1]

    *state, buffers = ff_slot(m, sent1.value(), (), small)
    chunk_out = weight_out(slot, gelu, buffers[0])
    reduced_out = reduction(chunk_out)
    chunk_wide = weight_wide(slot, xhat1, vec, buffers[1])
    state, buffers = onward(running, (state, buffers))
    reduced_wide = reduction(chunk_wide)
    one_by_one = [(first, 1) for first in range(groups)]
    low, small, hidden_grads, grads = heads_slot(m, *state, buffers, lambda: running, one_by_one)
    inputs = jnp.where(leading, tokens[:, 0], jnp.stack([received0, received1]))
    chunk_attn = weight_attn(slot, inputs, mixed, grads[2])
    reduced_attn = reduction(chunk_attn)
    small = Sum(small)
    running += [small]
    loss = None
    while True:
        if loss is None and not small.moving:
            loss = Swapped(small.value[loss_row : loss_row + 1, :128])
            running.append(loss)
        if not any(item.moving for item in running):
            break
        onward([reduced_attn])
        onward([item for item in running if item is not reduced_attn])

    if fast_ring():
        own_ff_out = reduced_out.value()
        own_ff_in = unblocked(reduced_wide.value().reshape(4, rows_in, D))
        own_attn = reduced_attn.value()
        own_attn_in = unblocked(own_attn[: 3 * rows_in].reshape(3, rows_in, D))
        own_attn_out = own_attn[3 * rows_in :]
    else:

        def natural(chunk, blocks):
            both = jnp.concatenate(chunk).reshape(16, blocks, -1, D)
            return both.transpose(1, 0, 2, 3).reshape(blocks, -1, D)

        attn = natural(chunk_attn, 4)
        whole = [unblocked(attn[:3]), attn[3], unblocked(natural(chunk_wide, 4))]
        whole.append(natural(chunk_out, 1)[0])
        own_attn_in, own_attn_out, own_ff_in, own_ff_out = (
            lax.psum_scatter(grad.astype(f32), "dp", scatter_dimension=0, tiled=True)
            for grad in whole
        )

    contrast_loss = jnp.where(order.token < 0, 0.0, loss.both[0, 0])
    small = small.value
    own_rows = lax.dynamic_slice(small, (0, me * rows_in), (8, rows_in))
    spot = me * rows_out
    own_bias = lax.dynamic_slice(small, (8 + spot // D, spot % D), (1, rows_out))
    return (
        contrast_loss,
        states_out,
        hidden_grads[0][None, :, None],
        own_attn_in[None],
        own_attn_out[None],
        own_ff_in[None],
        own_ff_out[None],
        own_rows[None, :2],
        own_rows[None, 2:],
        own_bias,
    )


def solution(mesh):
    return jax.shard_map(
        local,
        mesh=mesh,
        in_specs=(
            P(None, "dp", None, None),
            P(None, "dp", None, None),
            P(None, "dp", None),
            P(None, "dp"),
            P(),
            P("section", "dp", None),
            P("section", "dp", None),
            P("section", "dp", None),
            P("section", "dp", None),
            P("section", None, "dp"),
            P("section", None, "dp"),
            P("section", "dp"),
        ),
        out_specs=(
            P(),
            P("section", None, "dp", None, None),
            P("section", None, "dp", None, None),
            P("section", "dp", None),
            P("section", "dp", None),
            P("section", "dp", None),
            P("section", "dp", None),
            P("section", None, "dp"),
            P("section", None, "dp"),
            P("section", "dp"),
        ),
        check_vma=False,
    )
```

```python
from functools import partial

import jax
import jax.numpy as jnp
from jax import lax
from jax.experimental import pallas as pl
from jax.experimental.pallas import tpu as pltpu
from jax.sharding import PartitionSpec as P

D = 768
HEADS = 12
HEAD = 64
SEQ = 512
MICRO = 2
FF = 3072

bf16 = jnp.bfloat16
f32 = jnp.float32
highest = lax.Precision.HIGHEST
norm_eps = 1e-05
unit_eps = 1e-06
masked_value = -1000000000.0
contrast_scale = 10.0
vmem_limit = 16 * 2**20
slot_vmem = 36 * 2**20


def params(size=vmem_limit):
    return pltpu.CompilerParams(vmem_limit_bytes=size)


def cost(flops, size, factor=2):
    return pl.CostEstimate(
        flops=int(factor * flops), bytes_accessed=int(factor * size), transcendentals=0
    )


def swapped(value, axis, mask):
    count = lax.axis_size(axis)
    return lax.ppermute(value, axis, [(i, i ^ mask) for i in range(count)])


def ring_order(chips):
    return list(range(0, chips, 2)) + list(range(chips - 1, 0, -2))


def ring_hop(value, backward=False):
    chips = lax.axis_size("dp") // 2
    order = ring_order(chips)
    pairs = []
    for place in range(chips):
        for core in range(2):
            step = 1 if core == 0 else -1
            pairs.append((order[place] * 2 + core, order[(place + step) % chips] * 2 + core))
    return lax.ppermute(value, "dp", pairs)


def ring_place(me):
    chips = lax.axis_size("dp") // 2
    order = ring_order(chips)
    places = [order.index(chip) for chip in range(chips)]
    place = jnp.asarray(places, jnp.int32)[me // 2]
    core = me % 2
    return place, 1 - 2 * core, core


def owners(me, steps, cores):
    chips = lax.axis_size("dp") // 2
    place, way, core = ring_place(me)
    order = jnp.asarray(ring_order(chips), jnp.int32)
    found = order[(place + way * jnp.asarray(steps, jnp.int32)) % chips] * 2
    return found + (core + jnp.asarray(cores, jnp.int32)) % 2


def fast_ring():
    return lax.axis_size("dp") == 16


def gather_owners(me):
    steps = [0, 0, -1, -1, -2, -2, -3, -3, -4, 1, 1, 2, 2, 3, 3, 4]
    cores = [0, 1, 0, 1, 0, 1, 0, 1, 0, 1, 0, 1, 0, 1, 0, 1]
    return owners(me, steps, cores)


def assemble_kernel(counts, owner_ref, *refs):
    pieces, out_ref, sems = refs[: len(counts)], refs[-2], refs[-1]
    rows = pieces[0].shape[2]
    copies = []
    for piece, count in zip(pieces, counts):
        for k in range(count):
            start = pl.multiple_of(owner_ref[len(copies)] * rows, 16)
            copies.append(
                pltpu.make_async_copy(
                    piece.at[k], out_ref.at[:, pl.ds(start, rows), :], sems.at[len(copies)]
                )
            )
    for copy in copies:
        copy.start()
    for copy in copies:
        copy.wait()


def assemble(pieces, owner):
    counts = [piece.shape[0] for piece in pieces]
    total = sum(counts)
    blocks, rows = pieces[0].shape[1:3]
    return pl.pallas_call(
        partial(assemble_kernel, counts),
        out_shape=jax.ShapeDtypeStruct((blocks, total * rows, D), bf16),
        in_specs=[pl.BlockSpec(memory_space=pltpu.SMEM)]
        + [pl.BlockSpec(memory_space=pl.ANY)] * len(pieces),
        out_specs=pl.BlockSpec(memory_space=pltpu.VMEM),
        scratch_shapes=[pltpu.SemaphoreType.DMA((total,))],
        compiler_params=params(),
        cost_estimate=cost(0, 1e7),
        name="assemble",
    )(owner, *[pltpu.with_memory_space_constraint(piece, pltpu.HBM) for piece in pieces])


unit_steps = [1, 1, 2, 2, 3, 3, 4, 0]


def slots(me):
    if not fast_ring():
        return jnp.arange(16, dtype=jnp.int32)
    both = jnp.arange(6, dtype=jnp.int32) % 2
    keep = owners(me, unit_steps, [0] * 8)
    send = owners(me, [-step for step in unit_steps], [1] * 8)
    table = [keep[:6] // 2 * 2 + both, keep[6:], send[:6] // 2 * 2 + both, send[6:]]
    table = jnp.concatenate(table)
    index = jnp.arange(16, dtype=jnp.int32)
    return jnp.sum(jnp.where(table[None, :] == index[:, None], index[None, :], 0), axis=1)


def fold_first_kernel(keep_ref, mate_ref, out_ref, own_ref):
    total = keep_ref[...].astype(f32) + mate_ref[...].astype(f32)
    out_ref[...] = total[:1].astype(bf16)
    own_ref[...] = total[1]


def fold_first(keep, mate):
    rows, width = keep.shape[1:]
    tile = rows // 2
    units = pl.BlockSpec((2, tile, width), lambda i: (3, i, 0))
    return pl.pallas_call(
        fold_first_kernel,
        grid=(2,),
        in_specs=[units, units],
        out_specs=[
            pl.BlockSpec((1, tile, width), lambda i: (0, i, 0)),
            pl.BlockSpec((tile, width), lambda i: (i, 0)),
        ],
        out_shape=[
            jax.ShapeDtypeStruct((1, rows, width), bf16),
            jax.ShapeDtypeStruct((rows, width), f32),
        ],
        compiler_params=params(),
        cost_estimate=cost(0, 0),
        name="fold_first",
    )(keep, mate)


def fold_kernel(one, core_ref, keep_ref, mate_ref, there_ref, out_ref):
    there = there_ref[...].astype(f32)
    if one:
        there = jnp.where(pl.program_id(0) == core_ref[0], there, 0.0)
    total = keep_ref[...].astype(f32) + mate_ref[...].astype(f32) + there
    out_ref[...] = total.astype(bf16)


def fold(core, keep, mate, first, there):
    rows, width = keep.shape[1:]
    one = there.shape[0] == 1
    unit = pl.BlockSpec((1, rows, width), lambda i, _: (first + i, 0, 0))
    out = pl.BlockSpec((1, rows, width), lambda i, _: (i, 0, 0))
    arrived = pl.BlockSpec((1, rows, width), lambda i, _: (0, 0, 0)) if one else out
    return pl.pallas_call(
        partial(fold_kernel, one),
        grid_spec=pltpu.PrefetchScalarGridSpec(
            num_scalar_prefetch=1, grid=(2,), in_specs=[unit, unit, arrived], out_specs=out
        ),
        out_shape=jax.ShapeDtypeStruct((2, rows, width), bf16),
        compiler_params=params(),
        cost_estimate=cost(0, 0),
        name="fold",
    )(core, keep, mate, there)


class Reduction:
    def __init__(self, core, keep, send):
        self.core, self.keep, self.send = core, keep, send
        self.moving = [swapped(send, "dp", 1)] if fast_ring() else []
        self.stage = 0

    def step(self):
        arrived = self.moving[0]
        if self.stage == 0:
            self.mate = arrived
            first, self.own = fold_first(self.keep, self.mate)
            self.moving = [ring_hop(first)]
        elif self.stage < 4:
            first = 6 - 2 * self.stage
            self.moving = [ring_hop(fold(self.core, self.keep, self.mate, first, arrived))]
        elif self.stage == 4:
            self.near = arrived
            self.moving = [swapped(self.near, "dp", 1)]
        else:
            self.last = arrived
            self.moving = []
        self.stage += 1

    def value(self):
        def mine(pair):
            return lax.dynamic_index_in_dim(pair, self.core[0], 0, keepdims=False).astype(f32)

        return self.own + mine(self.near) + mine(self.last)


class Sent:
    def __init__(self, value, pairs):
        self.moving = [lax.ppermute(value, "section", pairs)]

    def step(self):
        self.arrived = self.moving[0]
        self.moving = []

    def value(self):
        return self.arrived


class Near:
    def __init__(self, value):
        self.value, self.mask = value, lax.axis_size("dp") // 2
        self.send()

    def send(self):
        self.moving = [swapped(self.value, "dp", self.mask)] if self.mask else []

    def step(self):
        self.value = jnp.concatenate([self.value, self.moving[0]])
        self.mask //= 2
        self.send()


class Sum:
    def __init__(self, value):
        self.value, self.mask = value, lax.axis_size("dp") // 2
        self.send()

    def send(self):
        self.moving = [swapped(self.value, "dp", self.mask)] if self.mask else []

    def step(self):
        self.value = self.value + self.moving[0]
        self.mask //= 2
        self.send()


class Swapped:
    def __init__(self, value):
        self.own, self.moving = value, [swapped(value, "section", 1)]

    def step(self):
        self.both = self.own + self.moving[0]
        self.moving = []


class Gather:
    def __init__(self, shard):
        self.pieces, self.mates = [shard], []
        self.moving = [swapped(shard, "dp", 1)]
        self.stage = 0

    def step(self):
        if self.stage == 0:
            self.pieces = [jnp.stack([self.pieces[0], self.moving[0]])]
            self.moving = [ring_hop(self.pieces[0])]
        elif self.stage < 5:
            self.pieces.append(self.moving[0])
            self.mates += self.moving[1:]
            self.moving = [swapped(self.pieces[-1], "dp", 1)]
            if self.stage < 4:
                last = self.pieces[-1] if self.stage < 3 else self.pieces[-1][:1]
                self.moving = [ring_hop(last)] + self.moving
        else:
            self.mates += self.moving
            self.moving = []
        self.stage += 1

    def all(self):
        return self.pieces + self.mates


class Order:
    def __init__(self, start):
        self.token = start

    def onward(self, items, values=()):
        for item in items:
            if item.moving:
                item.moving, self.token = lax.optimization_barrier((item.moving, self.token))
                item.step()
        values, self.token = lax.optimization_barrier((values, self.token))
        return values


def tie(values, *others):
    return lax.optimization_barrier((values, others))[0]


def add_up(value, axis):
    mask = 1
    while mask < lax.axis_size(axis):
        value = value + swapped(value, axis, mask)
        mask *= 2
    return value


def mm(a, b):
    return lax.dot_general(a, b, (((1,), (0,)), ((), ())), preferred_element_type=f32)


def mm_nt(a, b):
    return lax.dot_general(a, b, (((1,), (1,)), ((), ())), preferred_element_type=f32)


def mm_tn(a, b):
    return lax.dot_general(a, b, (((0,), (0,)), ((), ())), preferred_element_type=f32)


def full(shape):
    return pl.BlockSpec(shape, lambda i, *_: (0,) * len(shape))


def sds(shape, dtype):
    return jax.ShapeDtypeStruct(shape, dtype)


def far(shape, dtype):
    return pltpu.HBM(shape, dtype)


group = 256
groups = D // group
product = 2 * SEQ * D * D
token_block = (SEQ, D)
table_rows = 12
loss_row = 12
entries = MICRO + 1
everything = pl.BlockSpec(memory_space=pl.ANY)


def far(shape, dtype):
    return pltpu.HBM(shape, dtype)


def tokens_buffer(width, dtype):
    return far((entries, SEQ, width), dtype)


def busy(i, m):
    return jnp.where(m[0] < MICRO, i, 0)


def at_entry(block, *where):
    place = where[0] if where else (lambda i: (0,) * len(block))
    return pl.BlockSpec((None, *block), lambda i, m: (m[0], *place(busy(i, m))))


def at_micro(block):
    return pl.BlockSpec((None, *block), lambda i, m: (jnp.minimum(m[0], MICRO - 1),) + (0,) * len(block))


def column_sum(value):
    return jnp.sum(value, axis=0, keepdims=True)


class Slot:
    def __init__(self, entry, ahead=False):
        self.entry, self.ahead = entry, ahead


def in_place(value):
    if value.ndim > 2 and value.shape[0] in (MICRO, entries):
        return pltpu.with_memory_space_constraint(value, pltpu.HBM)
    return value


def slot_call(kernel, m, grid, ins, in_specs, outs, out_specs, before, scratch, size, name, kept=None):
    first = len(outs) - len(before)
    aliases = {1 + len(ins) + n: first + n for n in range(len(before))}
    if kept is not None:
        aliases[1 + kept[0]] = kept[1]
    return pl.pallas_call(
        kernel,
        grid_spec=pltpu.PrefetchScalarGridSpec(
            num_scalar_prefetch=1,
            grid=(grid,),
            in_specs=in_specs + [everything] * len(before),
            out_specs=out_specs,
            scratch_shapes=scratch,
        ),
        out_shape=outs,
        input_output_aliases=aliases,
        compiler_params=params(slot_vmem),
        cost_estimate=cost(0, 0) if m.ahead else cost(size * product, 3e7, 10 if "back" in name else 2),
        name=name,
    )(m.entry, *[in_place(value) for value in ins], *[in_place(value) for value in before])


def attend_kernel(first, n_before, m_ref, *refs):
    x_ref, wq_ref, wk_ref, wv_ref, vec_ref, seg_col_ref, seg_row_ref, *refs = refs
    q_ref, k_ref, v_ref, mixed_ref, lse_ref, mask_ref = refs[n_before:]
    i = pl.program_id(0)

    @pl.when(m_ref[0] < MICRO)
    def _():
        @pl.when(i == 0)
        def _():
            mask_ref[...] = jnp.where(seg_col_ref[...] == seg_row_ref[...], 0.0, masked_value)

        lanes = pl.ds(pl.multiple_of((first + i) * group, group), group)
        x = x_ref[...]
        q = (mm(x, wq_ref[...]) + vec_ref[2:3, lanes]).astype(bf16)
        k = mm(x, wk_ref[...]).astype(bf16)
        v = (mm(x, wv_ref[...]) + vec_ref[3:4, lanes]).astype(bf16)
        q_ref[...] = q
        k_ref[...] = k
        v_ref[...] = v
        scaled = q * jnp.asarray(HEAD**-0.5, bf16)
        outs, lses = [], []
        for h in range(group // HEAD):
            c = slice(h * HEAD, (h + 1) * HEAD)
            scores = mm_nt(scaled[:, c], k[:, c]) + mask_ref[...]
            top = jnp.max(scores, axis=1, keepdims=True)
            raw = jnp.exp(scores - top)
            total = jnp.sum(raw, axis=1, keepdims=True)
            outs.append(mm(raw.astype(bf16), v[:, c]) / total)
            lses.append(top + jnp.log(total))
        mixed_ref[...] = jnp.concatenate(outs, axis=1).astype(bf16)
        lses = jnp.concatenate(lses + [jnp.zeros((SEQ, 128 - len(lses)), f32)], axis=1)
        lse_ref[...] = jnp.transpose(lses)[:8]


vec_spec = full((table_rows, D))


def attend(m, x, w_in, vec, seg_col, seg_row, before, first=0, count=groups):
    def weight(b):
        return pl.BlockSpec((None, D, group), lambda i, m: (b, 0, first + busy(i, m)))

    heads = at_entry((SEQ, group), lambda i: (0, first + i))
    return slot_call(
        partial(attend_kernel, first, len(before)),
        m,
        count,
        [x, w_in, w_in, w_in, vec, seg_col, seg_row],
        [full(token_block)]
        + [weight(b) for b in range(3)]
        + [vec_spec, at_entry((SEQ, 1)), at_entry((1, SEQ))],
        [tokens_buffer(D, bf16)] * 4 + [far((entries, groups, 8, SEQ), f32)],
        [heads] * 4 + [at_entry((None, 8, SEQ), lambda i: (first + i, 0, 0))],
        before,
        [pltpu.VMEM((SEQ, SEQ), f32)],
        2 * count,
        "attend",
    )


def normalize(hidden):
    centered = hidden - jnp.mean(hidden, axis=1, keepdims=True)
    variance = jnp.mean(centered * centered, axis=1, keepdims=True)
    rstd = lax.rsqrt(variance + norm_eps)
    return centered * rstd, rstd


def gelu_both(x):
    cdf = 0.5 + 0.5 * lax.erf(x * 0.7071067811865476)
    return x * cdf, cdf + x * (jnp.exp(x * x * -0.5) * 0.3989422804014327)


def forward_kernel(last, n_before, m_ref, mixed_ref, x_ref, wo_ref, wi_ref, wf_ref, vec_ref, *refs):
    seg_row_ref, *refs = refs
    refs = refs[n_before:]
    if last:
        pooled_ref, unit_ref, *refs = refs
    else:
        out_ref, *refs = refs
    xhat1_ref, rstd1_ref, gelu_ref, dgelu_ref, state_ref, xhat2_ref, rstd2_ref, *refs = refs
    normed_ref, acc_ref = refs
    i = pl.program_id(0)

    @pl.when(m_ref[0] < MICRO)
    def _():
        @pl.when(i == 0)
        def _():
            attended = mm(mixed_ref[...], wo_ref[...]) + vec_ref[4:5, :]
            xhat, rstd = normalize(x_ref[...].astype(f32) + attended)
            xhat1_ref[...] = xhat.astype(bf16)
            rstd1_ref[...] = rstd
            normed = xhat * vec_ref[0:1, :] + vec_ref[5:6, :]
            normed_ref[...] = normed.astype(bf16)
            acc_ref[...] = normed + vec_ref[6:7, :]

        pre_act = mm(normed_ref[...], wi_ref[...]) + vec_ref[pl.ds(8 + i, 1), :]
        value, slope = gelu_both(pre_act)
        value = value.astype(bf16)
        gelu_ref[...] = value
        dgelu_ref[...] = slope.astype(bf16)
        acc_ref[...] += mm(value, wf_ref[...])

        @pl.when(i == pl.num_programs(0) - 1)
        def _():
            xhat, rstd = normalize(acc_ref[...])
            xhat2_ref[...] = xhat.astype(bf16)
            rstd2_ref[...] = rstd
            out = xhat * vec_ref[1:2, :] + vec_ref[7:8, :]
            state_ref[...] = out.astype(bf16)
            if not last:
                out_ref[...] = out.astype(bf16)
            else:
                member = seg_row_ref[...] == lax.broadcasted_iota(jnp.int32, (8, SEQ), 0)
                count = jnp.sum(member.astype(f32), axis=1, keepdims=True)
                member = member.astype(bf16)
                high = out.astype(bf16)
                rest = out - high.astype(f32)
                middle = rest.astype(bf16)
                low = (rest - middle.astype(f32)).astype(bf16)
                pooled = mm(member, high) + mm(member, middle) + mm(member, low)
                pooled = pooled / jnp.maximum(count, 1.0)
                pooled_ref[...] = pooled
                norm = jnp.sum(pooled * pooled, axis=1, keepdims=True) + unit_eps
                unit_ref[...] = pooled * lax.rsqrt(norm)

    if last:

        @pl.when(m_ref[0] >= MICRO)
        def _():
            pooled_ref[...] = jnp.zeros((8, D), f32)
            unit_ref[...] = jnp.zeros((8, D), f32)


def forward(m, mixed, x, w_wide, w_narrow, vec, seg_row, last, before):
    part = at_entry(token_block, lambda i: (0, i))
    now = [sds((8, D), f32)] * 2 if last else [sds(token_block, bf16)]
    row = sds((entries, SEQ, 1), f32)
    outs = now + [tokens_buffer(D, bf16), row] + [tokens_buffer(FF, bf16)] * 2
    outs += [tokens_buffer(D, bf16), tokens_buffer(D, bf16), row]
    return slot_call(
        partial(forward_kernel, last, len(before)),
        m,
        FF // D,
        [mixed, x, w_wide, w_wide, w_narrow, vec, seg_row],
        [
            at_entry(token_block),
            full(token_block),
            pl.BlockSpec((None, D, D), lambda i, m: (0, 0, 0)),
            pl.BlockSpec((None, D, D), lambda i, m: (1 + busy(i, m), 0, 0)),
            pl.BlockSpec((None, D, D), lambda i, m: (0, busy(i, m), 0)),
            vec_spec,
            at_entry((1, SEQ)),
        ],
        outs,
        [full(out.shape) for out in now]
        + [at_entry(token_block), at_entry((SEQ, 1)), part, part]
        + [at_entry(token_block), at_entry(token_block), at_entry((SEQ, 1))],
        before,
        [pltpu.VMEM(token_block, bf16), pltpu.VMEM(token_block, f32)],
        9,
        "forward",
    )


def contrast_kernel(me_ref, table_ref, pooled_ref, groups_ref, partner_ref, seg_row_ref, *refs, micro, total):
    loss_ref, gseg_ref = refs
    me = me_ref[0]
    dot = partial(lax.dot_general, precision=highest, preferred_element_type=f32)
    rows_nt = (((1,), (1,)), ((), ()))
    table = table_ref[...].reshape(-1, D)
    count = table.shape[0]
    devices = count // 8
    every = groups_ref.shape[1]
    segs = every // devices

    def sentence(shape, axis):
        index = lax.broadcasted_iota(jnp.int32, shape, axis)
        block, place = index >> 3, index & 7
        owner = jnp.zeros_like(block)
        far_one = devices // 2
        bit = 0
        while far_one >= 1:
            owner = owner | ((block >> bit) & 1) * far_one
            bit += 1
            far_one //= 2
        return jnp.where(place < segs, (owner ^ me) * segs + place, -1)

    ids_row, ids_col = sentence((1, count), 1), sentence((count, 1), 0)
    ids = groups_ref[micro : micro + 1, :].astype(f32)
    ids = jnp.broadcast_to(ids, (8, every))
    hot_row = (lax.broadcasted_iota(jnp.int32, (every, 1), 0) == ids_row).astype(f32)
    hot_col = (lax.broadcasted_iota(jnp.int32, (1, every), 1) == ids_col).astype(f32)
    groups_row = dot(ids, hot_row, (((1,), (0,)), ((), ())))[0:1]
    groups_col = dot(hot_col, ids, rows_nt)[:, 0:1]
    logits = contrast_scale * dot(table, table, rows_nt)
    real = (ids_row >= 0) & (ids_col >= 0)
    allowed = real & (groups_col == groups_row) & (ids_col != ids_row)
    masked = jnp.where(allowed, logits, masked_value)
    top = jnp.max(masked, axis=0, keepdims=True)
    lse_row = top + jnp.log(column_sum(jnp.exp(masked - top)))
    mine = masked[:8]
    top = jnp.max(mine, axis=1, keepdims=True)
    raw = jnp.exp(mine - top)
    raw_total = jnp.sum(raw, axis=1, keepdims=True)
    across = jnp.exp(mine - lse_row)
    place = lax.broadcasted_iota(jnp.int32, (8, 1), 0)
    partner = jnp.zeros((8, 1), jnp.int32)
    for s in range(segs):
        partner = jnp.where(place == s, partner_ref[micro, s], partner)
    chosen = ((partner == ids_row) & (place < segs)).astype(f32)
    terms = top + jnp.log(raw_total) - jnp.sum(chosen * logits[:8], axis=1, keepdims=True)
    loss = column_sum(jnp.where(place < segs, terms, 0.0)) / total
    loss_ref[...] = jnp.broadcast_to(loss, (1, D))
    grad = raw / raw_total + across - 2.0 * chosen
    grad = contrast_scale * dot(grad, table, (((1,), (0,)), ((), ())))
    pooled = pooled_ref[...]
    scale = lax.rsqrt(jnp.sum(pooled * pooled, axis=1, keepdims=True) + unit_eps)
    dots = jnp.sum(grad * pooled, axis=1, keepdims=True)
    grad = scale * grad - pooled * (scale * scale * scale * dots)
    member = (seg_row_ref[...] == lax.broadcasted_iota(jnp.int32, (8, SEQ), 0)).astype(f32)
    gseg_ref[...] = grad / jnp.maximum(jnp.sum(member, axis=1, keepdims=True), 1.0)


def contrast(me, table, pooled, group_ids, partner, seg_row, micro, total):
    smem = pl.BlockSpec(memory_space=pltpu.SMEM)
    return pl.pallas_call(
        partial(contrast_kernel, micro=micro, total=total),
        grid=(1,),
        out_shape=[sds((1, D), f32), sds((8, D), f32)],
        in_specs=[
            smem,
            full(table.shape),
            full((8, D)),
            full(group_ids.shape),
            smem,
            pl.BlockSpec((None, 1, SEQ), lambda i: (micro, 0, 0)),
        ],
        out_specs=[full((1, D)), full((8, D))],
        compiler_params=params(slot_vmem),
        name="contrast",
    )(me, table, pooled, group_ids, partner, seg_row)


def norm_back(grad, xhat, rstd, gain):
    scaled = grad * gain
    mean = jnp.mean(scaled, axis=1, keepdims=True)
    along = jnp.mean(scaled * xhat, axis=1, keepdims=True)
    return rstd * (scaled - mean - xhat * along)


def ff_back_kernel(last, n_before, m_ref, cot_ref, *refs):
    if last:
        seg_col_ref, gseg_ref, loss_ref, *refs = refs
    xhat2_ref, rstd2_ref, vec_ref, wf_ref, dgelu_ref, wi_ref, xhat1_ref, rstd1_ref, *refs = refs
    wo_ref, small_in_ref, *refs = refs
    ghid_ref, gmixed_ref, small_ref, gbranch_ref, gpre_ref, gatt_ref, acc_ref = refs[n_before:]
    i = pl.program_id(0)

    @pl.when(i == 0)
    def _():
        small_ref[...] = small_in_ref[...]

    @pl.when(m_ref[0] < MICRO)
    def _():
        @pl.when(i == 0)
        def _():
            grad = cot_ref[...].astype(f32)
            if last:
                for s in range(4):
                    grad = grad + jnp.where(seg_col_ref[...] == s, gseg_ref[s : s + 1, :], 0.0)
            xhat = xhat2_ref[...].astype(f32)
            grad_sum = norm_back(grad, xhat, rstd2_ref[...], vec_ref[1:2, :])
            acc_ref[...] = grad_sum
            low = grad_sum.astype(bf16)
            gbranch_ref[...] = low
            if last:
                small_ref[loss_row : loss_row + 1, :] += loss_ref[...]
            small_ref[1:2, :] += column_sum(grad * xhat)
            small_ref[6:7, :] += column_sum(low.astype(f32))
            small_ref[7:8, :] += column_sum(grad)

        grad_gelu = mm_nt(gbranch_ref[...], wf_ref[...])
        grad_pre = (grad_gelu * dgelu_ref[...].astype(f32)).astype(bf16)
        gpre_ref[...] = grad_pre
        small_ref[pl.ds(8 + i, 1), :] += column_sum(grad_pre.astype(f32))
        acc_ref[...] += mm_nt(grad_pre, wi_ref[...])

        @pl.when(i == pl.num_programs(0) - 1)
        def _():
            grad = acc_ref[...]
            xhat = xhat1_ref[...].astype(f32)
            grad_hidden = norm_back(grad, xhat, rstd1_ref[...], vec_ref[0:1, :])
            ghid_ref[...] = grad_hidden
            low = grad_hidden.astype(bf16)
            gatt_ref[...] = low
            gmixed_ref[...] = mm_nt(low, wo_ref[...]).astype(bf16)
            small_ref[0:1, :] += column_sum(grad * xhat)
            small_ref[4:5, :] += column_sum(low.astype(f32))
            small_ref[5:6, :] += column_sum(grad)


def ff_back(m, cot, segs, xhat2, rstd2, vec, w_narrow, dgelu, w_wide, xhat1, rstd1, small, before):
    last = len(segs) > 0
    part = at_entry(token_block, lambda i: (0, i))
    return slot_call(
        partial(ff_back_kernel, last, len(before)),
        m,
        FF // D,
        [cot, *segs, xhat2, rstd2, vec, w_narrow, dgelu, w_wide, xhat1, rstd1, w_wide, small],
        (
            [at_micro(token_block), at_entry((SEQ, 1)), full((8, D)), full((1, D))]
            if last
            else [full(token_block)]
        )
        + [
            at_entry(token_block),
            at_entry((SEQ, 1)),
            vec_spec,
            pl.BlockSpec((None, D, D), lambda i, m: (0, busy(i, m), 0)),
            part,
            pl.BlockSpec((None, D, D), lambda i, m: (1 + busy(i, m), 0, 0)),
            at_entry(token_block),
            at_entry((SEQ, 1)),
            pl.BlockSpec((None, D, D), lambda i, m: (0, 0, 0)),
            full((16, D)),
        ],
        [sds(token_block, f32), sds(token_block, bf16), sds((16, D), f32)]
        + [tokens_buffer(D, bf16), tokens_buffer(FF, bf16), far((entries, 4, SEQ, D), bf16)],
        [full(token_block), full(token_block), full((16, D))]
        + [at_entry(token_block), part, at_entry((None, SEQ, D), lambda i: (3, 0, 0))],
        before,
        [pltpu.VMEM(token_block, f32)],
        12,
        "ff_back",
    )


def attend_back_kernel(first, n_total, n_before, m_ref, *refs):
    q_ref, k_ref, v_ref, gm_ref, lse_ref, wq_ref, wk_ref, wv_ref, *refs = refs
    totals, refs = refs[:n_total], refs[n_total:]
    seg_col_ref, seg_row_ref, small_in_ref, *refs = refs
    low_ref, small_ref, gx_ref, gqkv_ref, mask_ref = refs[n_before:]
    i = pl.program_id(0)
    active = m_ref[0] < MICRO

    @pl.when(i == 0)
    def _():
        small_ref[...] = small_in_ref[...]

    @pl.when((i == 0) & active)
    def _():
        mask_ref[...] = jnp.where(seg_col_ref[...] == seg_row_ref[...], 0.0, masked_value)
        gx_ref[...] = totals[0][...]

    @pl.when((i == 0) & jnp.logical_not(active))
    def _():
        gx_ref[...] = totals[-1][...]

    @pl.when(active)
    def _():
        q, k, v, gm = q_ref[...], k_ref[...], v_ref[...], gm_ref[...]
        scaled = q * jnp.asarray(HEAD**-0.5, bf16)
        lse = lse_ref[...]
        parts = [[], [], []]
        for h in range(group // HEAD):
            c = slice(h * HEAD, (h + 1) * HEAD)
            probs = jnp.exp(mm_nt(k[:, c], scaled[:, c]) + mask_ref[...] - lse[h : h + 1, :])
            grad_probs = mm_nt(v[:, c], gm[:, c])
            parts[2].append(mm(probs.astype(bf16), gm[:, c]))
            dots = column_sum(grad_probs * probs)
            grad_scores = (probs * (grad_probs - dots)).astype(bf16)
            parts[1].append(mm(grad_scores, scaled[:, c]))
            parts[0].append(mm_tn(grad_scores, k[:, c]) * HEAD**-0.5)
        grads = [jnp.concatenate(part, axis=1).astype(bf16) for part in parts]
        for b, grad in enumerate(grads):
            gqkv_ref[b] = grad
        lanes = pl.ds(pl.multiple_of((first + i) * group, group), group)
        small_ref[2:3, lanes] += column_sum(grads[0].astype(f32))
        small_ref[3:4, lanes] += column_sum(grads[2].astype(f32))
        gx_ref[...] += (
            mm_nt(grads[0], wq_ref[...]) + mm_nt(grads[1], wk_ref[...]) + mm_nt(grads[2], wv_ref[...])
        )

        @pl.when(i == pl.num_programs(0) - 1)
        def _():
            low_ref[...] = gx_ref[...].astype(bf16)


def attend_back(m, q, k, v, gm, lse, w_in, totals, seg_col, seg_row, small, first, count, before):
    def weight(b):
        return pl.BlockSpec((None, D, group), lambda i, m: (b, 0, first + busy(i, m)))

    heads = at_entry((SEQ, group), lambda i: (0, first + i))
    buffer = at_micro(token_block)
    total_specs = [buffer] if first else [full(token_block), buffer][: len(totals)]
    return slot_call(
        partial(attend_back_kernel, first, len(totals), len(before)),
        m,
        count,
        [q, k, v, gm, lse, w_in, w_in, w_in, *totals, seg_col, seg_row, small],
        [heads] * 3
        + [pl.BlockSpec((SEQ, group), lambda i, m: (0, first + busy(i, m)))]
        + [at_entry((None, 8, SEQ), lambda i: (first + i, 0, 0))]
        + [weight(b) for b in range(3)]
        + total_specs
        + [at_entry((SEQ, 1)), at_entry((1, SEQ)), full((16, D))],
        [sds(token_block, bf16), sds((16, D), f32)]
        + [far((MICRO, SEQ, D), f32), far((entries, 4, SEQ, D), bf16)],
        [full(token_block), full((16, D)), buffer]
        + [at_entry((3, SEQ, group), lambda i: (0, 0, first + i))],
        before,
        [pltpu.VMEM((SEQ, SEQ), f32)],
        6 * count,
        "attend_back",
        (7 + len(totals), 2) if first or len(totals) > 1 else None,
    )


def put(slot, keep_ref, send_ref, index, value):
    @pl.when(slot < 8)
    def _():
        keep_ref[(slot,) + index] = value

    @pl.when(slot >= 8)
    def _():
        send_ref[(slot - 8,) + index] = value


def weight_call(kernel, slot, ins, in_specs, scratch, name):
    outs = [sds((8, FF // 16, D), bf16)] * 2
    return pl.pallas_call(
        kernel,
        grid_spec=pltpu.PrefetchScalarGridSpec(
            num_scalar_prefetch=1,
            grid=(4,),
            in_specs=in_specs,
            out_specs=[full(out.shape) for out in outs],
            scratch_shapes=scratch,
        ),
        out_shape=outs,
        compiler_params=params(),
        cost_estimate=cost(8 * product, 3e7, 10),
        name=name,
    )(slot, *[in_place(value) for value in ins])


def weight_out_kernel(slot_ref, gelu_ref, gbranch_ref, keep_ref, send_ref):
    i = pl.program_id(0)
    rows = FF // 16
    total = sum(mm_tn(gelu_ref[m], gbranch_ref[m]) for m in range(MICRO)).astype(bf16)
    for j in range(4):
        put(slot_ref[4 * i + j], keep_ref, send_ref, (), total[j * rows : (j + 1) * rows])


def weight_wide_kernel(slot_ref, xhat_ref, vec_ref, gpre_ref, keep_ref, send_ref, normed_ref):
    i = pl.program_id(0)
    rows = D // 16

    @pl.when(i == 0)
    def _():
        for m in range(MICRO):
            normed = (xhat_ref[m].astype(f32) * vec_ref[0:1, :] + vec_ref[5:6, :]).astype(bf16)
            normed_ref[:, m * SEQ : (m + 1) * SEQ] = jnp.transpose(normed)

    total = mm(normed_ref[...], gpre_ref[...].reshape(MICRO * SEQ, D)).astype(bf16)
    row = pl.multiple_of(rows * i, 16)
    for d in range(16):
        put(slot_ref[d], keep_ref, send_ref, (pl.ds(row, rows),), total[d * rows : (d + 1) * rows])


def weight_attn_kernel(slot_ref, x_ref, mixed_ref, grad_ref, keep_ref, send_ref, left_ref):
    i = pl.program_id(0)
    rows = D // 16

    def turn(ref):
        for m in range(MICRO):
            left_ref[:, m * SEQ : (m + 1) * SEQ] = jnp.transpose(ref[m])

    @pl.when(i == 0)
    def _():
        turn(x_ref)

    @pl.when(i == 3)
    def _():
        turn(mixed_ref)

    total = mm(left_ref[...], grad_ref[...].reshape(MICRO * SEQ, D)).astype(bf16)
    row = pl.multiple_of(rows * i, 16)
    for d in range(16):
        put(slot_ref[d], keep_ref, send_ref, (pl.ds(row, rows),), total[d * rows : (d + 1) * rows])


both_blocks = (MICRO, SEQ, D)
both_parts = pl.BlockSpec(both_blocks, lambda i, _: (0, 0, i))


def weight_out(slot, gelu, gbranch):
    specs = [both_parts, full(both_blocks)]
    return weight_call(weight_out_kernel, slot, [gelu, gbranch], specs, [], "weight_out")


def weight_wide(slot, xhat1, vec, gpre):
    specs = [full(both_blocks), vec_spec, both_parts]
    scratch = [pltpu.VMEM((D, MICRO * SEQ), bf16)]
    return weight_call(weight_wide_kernel, slot, [xhat1, vec, gpre], specs, scratch, "weight_wide")


def weight_attn(slot, x, mixed, grads):
    grad_spec = pl.BlockSpec((MICRO, None, SEQ, D), lambda i, _: (0, i, 0, 0))
    specs = [full(both_blocks), full(both_blocks), grad_spec]
    scratch = [pltpu.VMEM((D, MICRO * SEQ), bf16)]
    return weight_call(weight_attn_kernel, slot, [x, mixed, grads], specs, scratch, "weight_attn")


def blocked(shard):
    rows, columns = shard.shape
    return shard.reshape(rows, columns // D, D).transpose(1, 0, 2)


def unblocked(shard):
    blocks, rows, columns = shard.shape
    return shard.transpose(1, 0, 2).reshape(rows, blocks * columns)


def gather_plain(shard):
    return blocked(lax.all_gather(shard.astype(bf16), "dp", axis=0, tiled=True))


def local(
    tokens,
    out_cotangent,
    lengths,
    partner,
    group_ids,
    attn_in,
    attn_out,
    ff_in,
    ff_out,
    norm_gains,
    biases,
    ff_bias,
):
    section = lax.axis_index("section").astype(jnp.int32)
    me = lax.axis_index("dp").astype(jnp.int32)
    leading = section == 0
    n_dp = lax.axis_size("dp")
    rows_in = D // n_dp
    rows_out = FF // n_dp
    segs = lengths.shape[-1]

    vectors = jnp.concatenate(
        [norm_gains[0].reshape(-1), biases[0].reshape(-1), ff_bias[0].reshape(-1)]
    ).astype(bf16)

    def vector_table(every):
        rows = every[:, : 8 * rows_in].reshape(n_dp, 8, rows_in).transpose(1, 0, 2).reshape(8, D)
        return jnp.concatenate([rows, every[:, 8 * rows_in :].reshape(4, D)]).astype(f32)

    spare = jnp.int32(MICRO)

    def entry(micro, layer):
        return jnp.where(section == layer, jnp.int32(micro), spare)[None]

    def segment_forms(lengths):
        row_ends = jnp.cumsum(lengths[:, 0], axis=-1, dtype=jnp.int32)
        places = jnp.arange(SEQ, dtype=jnp.int32)
        segment = jnp.sum((places[None, :, None] >= row_ends[:, None, :]).astype(jnp.int32), axis=-1)
        segment = jnp.concatenate([segment, segment[:1]])
        return segment[:, :, None], segment[:, None, :]

    order = Order(lengths[0, 0, 0])
    onward = order.onward

    first = Slot(entry(0, 0))
    x = tokens[0, 0]
    if fast_ring():
        in_gather = Gather(blocked(attn_in[0].astype(bf16)))
        table = jnp.pad(vectors[None], ((0, 15), (0, D - vectors.shape[0])))
        vec_gather = Gather(table[None])
        onward([in_gather, vec_gather])
        onward([in_gather, vec_gather])
        late = tie((attn_out, ff_in, ff_out, lengths, me), in_gather.pieces[1])
        wide_shard = [late[0][0].astype(bf16)[None], blocked(late[1][0].astype(bf16))]
        wide_gather = Gather(jnp.concatenate(wide_shard))
        seg_col, seg_row = segment_forms(late[3])
        owner, slot = gather_owners(late[4]), slots(late[4])
        onward([in_gather, vec_gather])
        onward([wide_gather])
        onward([in_gather, vec_gather])
        narrow_gather = Gather(tie(late[2], in_gather.pieces[3])[0].astype(bf16)[None])
        onward([in_gather, vec_gather])
        onward([wide_gather])
        onward([narrow_gather])
        onward([in_gather, vec_gather])
        vec = assemble(vec_gather.all(), owner).reshape(n_dp, 16, D)
        vec = vector_table(vec[:, 0, : vectors.shape[0]])
        w_in = assemble(in_gather.all(), owner)
        heads = attend(first, x, w_in, vec, seg_col, seg_row, [])
        heads = onward([wide_gather, narrow_gather], heads)
        onward([wide_gather, narrow_gather])
        onward([wide_gather])
        onward([narrow_gather])
        onward([wide_gather])
        w_wide = assemble(wide_gather.all(), owner)
        onward([narrow_gather])
        onward([narrow_gather])
        w_narrow = assemble(narrow_gather.all(), owner)
    else:
        w_in = gather_plain(attn_in[0])
        w_wide = jnp.concatenate([gather_plain(attn_out[0]), gather_plain(ff_in[0])])
        w_narrow = gather_plain(ff_out[0])
        vec = vector_table(lax.all_gather(vectors, "dp"))
        seg_col, seg_row = segment_forms(lengths)
        slot = slots(me)
        heads = attend(first, x, w_in, vec, seg_col, seg_row, [])
    out, *stored = forward(first, heads[3], x, w_wide, w_narrow, vec, seg_row, False, [])
    pairs = [(0, 1)]
    sent0 = Sent(out, pairs)

    second = Slot(entry(1, 0), True)
    x = tokens[1, 0]
    heads = attend(second, x, w_in, vec, seg_col, seg_row, heads)
    out, *stored = forward(second, heads[3], x, w_wide, w_narrow, vec, seg_row, False, stored)
    heads, stored, out = onward([sent0], (heads, stored, out))
    sent1 = Sent(out, pairs)

    third = Slot(entry(0, 1), True)
    x = received0 = sent0.value()
    heads = attend(third, x, w_in, vec, seg_col, seg_row, heads)
    pooled0, unit0, *stored = forward(
        third, heads[3], x, w_wide, w_narrow, vec, seg_row, True, stored
    )
    near0 = Near(unit0)
    heads, stored = onward([sent1], (heads, stored))

    fourth = Slot(entry(1, 1))
    x = received1 = sent1.value()
    heads = attend(fourth, x, w_in, vec, seg_col, seg_row, heads)
    heads = onward([near0], heads)
    pooled1, unit1, *stored = forward(
        fourth, heads[3], x, w_wide, w_narrow, vec, seg_row, True, stored
    )
    q, k, v, mixed, lse = heads
    xhat1, rstd1, gelu, dgelu, states, xhat2, rstd2 = stored

    total = MICRO * n_dp * segs

    def contrasted(near, pooled, micro):
        while near.moving:
            onward([near])
        table = near.value.reshape(-1, D)
        loss, grad_segs = contrast(
            me[None], table, pooled, group_ids, partner, seg_row, micro, total
        )
        return seg_col, grad_segs, loss

    near1 = Near(unit1)
    segs0 = contrasted(near0, pooled0, 0)

    cots = out_cotangent[:, 0]
    grads = []
    hidden_grads = []
    small = jnp.zeros((16, D), f32)

    def ff_slot(m, cot, segs_in, small):
        grad_hidden, grad_mixed, small, *buffers = ff_back(
            m, cot, segs_in, xhat2, rstd2, vec, w_narrow, dgelu, w_wide, xhat1, rstd1, small, grads
        )
        return grad_hidden, grad_mixed, small, buffers

    def heads_slot(m, grad_hidden, grad_mixed, small, buffers, items, calls):
        total, all_grads = grad_hidden, buffers[2]
        for first, count in calls:
            low, small, total, all_grads = attend_back(
                m,
                *(q, k, v, grad_mixed, lse, w_in),
                [total] if first else [total] + hidden_grads,
                *(seg_col, seg_row, small, first, count, [all_grads]),
            )
            total, all_grads, low, small = onward(items(), (total, all_grads, low, small))
        return low, small, [total], [buffers[0], buffers[1], all_grads]

    all_heads = ((0, groups),)
    pairs = [(1, 0)]
    m = Slot(entry(0, 1))
    state = ff_slot(m, cots, segs0, small)
    state = onward([near1], state)
    low, small, hidden_grads, grads = heads_slot(m, *state, lambda: [near1], all_heads)
    sent0 = Sent(low, pairs)

    m = Slot(entry(1, 1), True)
    state = ff_slot(m, cots, contrasted(near1, pooled1, 1), small)
    low, small, hidden_grads, grads = heads_slot(m, *state, lambda: [sent0], all_heads)
    sent1 = Sent(low, pairs)

    m = Slot(entry(0, 0), True)
    state = ff_slot(m, sent0.value(), (), small)
    states_out, state = onward([], (states[None, :MICRO, None], state))
    low, small, hidden_grads, grads = heads_slot(m, *state, lambda: [sent1], all_heads)

    m = Slot(entry(1, 0))
    core = (me % 2)[None]
    running = []

    def reduction(chunk):
        running.append(Reduction(core, *chunk))
        return running[-1]

    *state, buffers = ff_slot(m, sent1.value(), (), small)
    chunk_out = weight_out(slot, gelu, buffers[0])
    reduced_out = reduction(chunk_out)
    chunk_wide = weight_wide(slot, xhat1, vec, buffers[1])
    state, buffers = onward(running, (state, buffers))
    reduced_wide = reduction(chunk_wide)
    one_by_one = [(first, 1) for first in range(groups)]
    low, small, hidden_grads, grads = heads_slot(m, *state, buffers, lambda: running, one_by_one)
    inputs = jnp.where(leading, tokens[:, 0], jnp.stack([received0, received1]))
    chunk_attn = weight_attn(slot, inputs, mixed, grads[2])
    reduced_attn = reduction(chunk_attn)
    small = Sum(small)
    running += [small]
    loss = None
    while True:
        if loss is None and not small.moving:
            loss = Swapped(small.value[loss_row : loss_row + 1, :128])
            running.insert(0, loss)
        if not any(item.moving for item in running):
            break
        onward([reduced_attn])
        onward([item for item in running if item is not reduced_attn])

    if fast_ring():
        own_ff_out = reduced_out.value()
        own_ff_in = unblocked(reduced_wide.value().reshape(4, rows_in, D))
        own_attn = reduced_attn.value()
        own_attn_in = unblocked(own_attn[: 3 * rows_in].reshape(3, rows_in, D))
        own_attn_out = own_attn[3 * rows_in :]
    else:

        def natural(chunk, blocks):
            both = jnp.concatenate(chunk).reshape(16, blocks, -1, D)
            return both.transpose(1, 0, 2, 3).reshape(blocks, -1, D)

        attn = natural(chunk_attn, 4)
        whole = [unblocked(attn[:3]), attn[3], unblocked(natural(chunk_wide, 4))]
        whole.append(natural(chunk_out, 1)[0])
        own_attn_in, own_attn_out, own_ff_in, own_ff_out = (
            lax.psum_scatter(grad.astype(f32), "dp", scatter_dimension=0, tiled=True)
            for grad in whole
        )

    contrast_loss = jnp.where(order.token < 0, 0.0, loss.both[0, 0])
    small = small.value
    own_rows = lax.dynamic_slice(small, (0, me * rows_in), (8, rows_in))
    spot = me * rows_out
    own_bias = lax.dynamic_slice(small, (8 + spot // D, spot % D), (1, rows_out))
    return (
        contrast_loss,
        states_out,
        hidden_grads[0][None, :, None],
        own_attn_in[None],
        own_attn_out[None],
        own_ff_in[None],
        own_ff_out[None],
        own_rows[None, :2],
        own_rows[None, 2:],
        own_bias,
    )


def solution(mesh):
    return jax.shard_map(
        local,
        mesh=mesh,
        in_specs=(
            P(None, "dp", None, None),
            P(None, "dp", None, None),
            P(None, "dp", None),
            P(None, "dp"),
            P(),
            P("section", "dp", None),
            P("section", "dp", None),
            P("section", "dp", None),
            P("section", "dp", None),
            P("section", None, "dp"),
            P("section", None, "dp"),
            P("section", "dp"),
        ),
        out_specs=(
            P(),
            P("section", None, "dp", None, None),
            P("section", None, "dp", None, None),
            P("section", "dp", None),
            P("section", "dp", None),
            P("section", "dp", None),
            P("section", "dp", None),
            P("section", None, "dp"),
            P("section", None, "dp"),
            P("section", "dp"),
        ),
        check_vma=False,
    )
```
